32 devices in a mesh: dp: 8 (over z, x), fsdp: 4 (over y, core).
Axes of the slice: x: 2, y: 2, z: 4, core: 2. Of those that a mesh axis runs over, the one named last changes fastest.
Arguments:
- inputs: float32 [32768, 768], P(('dp', 'fsdp')), may hold values from -6 to 6
- img_lens: int32 [32, 12], P(('dp', 'fsdp')), may hold values from 1 to 128, 1024 in all within a row
- valid_rows: int32 [32], P(('dp', 'fsdp')), may hold values from 896 to 1024
- w_qkv: float32 [1769472], P(('dp', 'fsdp')), may hold values from -0.21875 to 0.21875
- w_proj: float32 [589824], P(('dp', 'fsdp')), may hold values from -0.625 to 0.625
- w_fc1: float32 [2359296], P(('dp', 'fsdp')), may hold values from -0.21875 to 0.21875
- b_fc1: float32 [3072], P(('dp', 'fsdp')), may hold values from -1.2 to 1.2
- w_fc2: float32 [2359296], P(('dp', 'fsdp')), may hold values from -0.109375 to 0.109375
- vectors: float32 [7680], P(('dp', 'fsdp')), may hold values from -1.2 to 1.6, as said below
- cotangent: float32 [32768, 768], P(('dp', 'fsdp')), may hold values from -6 to 6
Outputs:
- output: float32 [32768, 768], P(('dp', 'fsdp'))
- d_input: float32 [32768, 768], P(('dp', 'fsdp'))
- g_qkv: float32 [1769472], P(('dp', 'fsdp'))
- g_proj: float32 [589824], P(('dp', 'fsdp'))
- g_fc1: float32 [2359296], P(('dp', 'fsdp'))
- g_bfc1: float32 [3072], P(('dp', 'fsdp'))
- g_fc2: float32 [2359296], P(('dp', 'fsdp'))
- g_vectors: float32 [7680], P(('dp', 'fsdp'))
The draws below stay inside these ranges and needn't reach their ends.
Inputs may be any that keep to these rules, and one draw needn't show every extreme that they name: `img_lens`: each set's 12 lengths sum to 1024, and the largest is exactly 128. `vectors`: norm gains lie near 1, layer scales between 0.5 and 1.5, biases near 0.
All inputs are finite; a program needn't handle non-finite values.
Results may differ from the reference program's by a relative error of at most 0.012.
Values may be sent and summed in bfloat16 or wider, within the bound.
No kernel may reach another device: no remote copies, remote signals or barrier semaphores. Data moves between devices by JAX's collectives and lax.ppermute only.
A program may use at most 320 MiB of HBM per device.

```python
import math
import jax
import jax.numpy as jnp
import numpy as np
from jax import lax

D = 768
HEADS = 12
HD = 64
FF = 3072
ROWS = 1024
IMGS = 12
MOST = 128
SETS = 32
TOKENS = 32768


def draw_vectors(key, part):
    key = jax.random.fold_in(key, 7)
    first_key, second_key = jax.random.split(key)
    jitter = jnp.clip(jax.random.normal(first_key, (10, D), jnp.float32), -4.0, 4.0)
    layer_scale = jax.random.uniform(second_key, (10, D), jnp.float32, 0.5, 1.5)
    row_kind = jnp.arange(10)[:, None]
    gain_rows = (row_kind == 0) | (row_kind == 6)
    scale_rows = (row_kind == 5) | (row_kind == 9)
    result = jnp.where(gain_rows, 1.0 + 0.15 * jitter, 0.3 * jitter)
    result = jnp.where(scale_rows, layer_scale, result)
    return result.reshape(10 * D)


def set_ends(values, own_key, low, largest):
    index_at = [jax.random.randint(jax.random.fold_in(own_key, axis), (), 0, length) for axis, length in enumerate(values.shape)]
    main_axis = values.shape.index(max(values.shape))
    neighbour = index_at[:main_axis] + [(index_at[main_axis] + 1) % values.shape[main_axis]] + index_at[main_axis + 1:]
    return values.at[tuple(index_at)].set(low).at[tuple(neighbour)].set(largest)


def level_of(stream_key, shape, shards, smallest, high):
    factor_of, own = 1.0, jax.random.fold_in(stream_key, 6)
    for dim, blocks in shards:
        draws = jnp.exp(jax.random.uniform(jax.random.fold_in(own, dim), (blocks,), jnp.float32, smallest / len(shards), high / len(shards)))
        factor_of = factor_of * jnp.repeat(draws, shape[dim] // blocks).reshape([-1 if axis == dim else 1 for axis in range(len(shape))])
    return factor_of


def length_profile(number_of, total, most, skew):
    portions = [(1 << 20) // math.isqrt(standing ** skew) + 1 for standing in range(2, number_of + 1)]
    surplus, given = total - most - (number_of - 1), [1] * (number_of - 1)
    while surplus > 0:
        free = [i for i in range(number_of - 1) if given[i] < most]
        pool, budget = sum([portions[i] for i in free]), surplus
        for i in free:
            more = min(most - given[i], max(1, budget * portions[i] // pool), surplus)
            given[i] = given[i] + more
            surplus = surplus - more
    return np.array([most] + given)


def ragged(key, number_of, total, limit, skew):
    if number_of == 2:
        one = jax.random.randint(key, (), max(1, total - limit), min(limit, total - 1) + 1)
        return jnp.stack([one, total - one])
    sizes = jnp.asarray(length_profile(number_of, total, limit, skew), jnp.int32)
    twos = (number_of - 1) // 2
    giver, receiver = sizes[1:1 + 2 * twos:2], sizes[2:2 + 2 * twos:2]
    slack = jnp.minimum(giver - 1, limit - receiver)
    passed = jax.random.randint(jax.random.fold_in(key, 1), (twos,), 0, 1 << 20) % (slack + 1)
    sizes = sizes.at[1:1 + 2 * twos:2].set(giver - passed).at[2:2 + 2 * twos:2].set(receiver + passed)
    return sizes[jax.random.permutation(jax.random.fold_in(key, 2), number_of)]


def scatter_about(rng, extent, width, bound, pieces=(), kind=jnp.bfloat16):
    values = width * jax.random.normal(rng, extent, jnp.float32)
    if pieces:
        values = values * level_of(rng, extent, pieces, -0.22, 0.18)
    return jnp.clip(values, -bound, bound).astype(kind)


def setup_inputs(seed: int = 0) -> dict:
    key_of = jax.random.split(jax.random.key(seed), 11)
    inputs = scatter_about(key_of[0], (TOKENS, D), 1.0, 6.0, ((0, 32),), jnp.float32)
    img_lens = jax.vmap(lambda own: ragged(own, IMGS, ROWS, MOST, 1))(jax.random.split(key_of[1], SETS)).reshape((SETS, IMGS)).astype(jnp.int32)
    valid_rows = set_ends(jax.random.randint(key_of[2], (SETS,), ROWS - ROWS // 8, ROWS + 1), jax.random.fold_in(key_of[2], 1), ROWS - ROWS // 8, ROWS).astype(jnp.int32)
    w_qkv = scatter_about(key_of[3], (3 * D * D,), D ** -0.5, 0.21875, ((0, 32),), jnp.float32)
    w_proj = scatter_about(key_of[4], (D * D,), (D // 8) ** -0.5, 0.625, ((0, 32),), jnp.float32)
    w_fc1 = scatter_about(key_of[5], (D * FF,), D ** -0.5, 0.21875, ((0, 32),), jnp.float32)
    b_fc1 = scatter_about(key_of[6], (FF,), 0.3, 1.2, ((0, 32),), jnp.float32)
    w_fc2 = scatter_about(key_of[7], (FF * D,), FF ** -0.5, 0.109375, ((0, 32),), jnp.float32)
    vectors = draw_vectors(jax.random.fold_in(key_of[10], 71), 0)
    cotangent = scatter_about(key_of[9], (TOKENS, D), 1.0, 6.0, ((0, 32),), jnp.float32)
    return dict(inputs=inputs, img_lens=img_lens, valid_rows=valid_rows, w_qkv=w_qkv, w_proj=w_proj, w_fc1=w_fc1, b_fc1=b_fc1, w_fc2=w_fc2, vectors=vectors, cotangent=cotangent)


@jax.custom_vjp
def low(v):
    return lax.optimization_barrier(v.astype(jnp.bfloat16)).astype(jnp.float32)

@jax.custom_vjp
def low_back(v):
    return v

def low_keep(v):
    return (low(v), None)

def low_pass(kept, grad):
    return (grad,)

def back_keep(v):
    return (v, None)

def back_low(kept, grad):
    return (low(grad),)
low.defvjp(low_keep, low_pass)
low_back.defvjp(back_keep, back_low)
highest = lax.Precision.HIGHEST
eps = 1e-06

def layer_norm(values, gain, shift):
    center = values - lax.optimization_barrier(jnp.mean(values, axis=-1, keepdims=True))
    spread = lax.optimization_barrier(jnp.mean(center * center, axis=-1, keepdims=True))
    return center * lax.rsqrt(spread + eps) * gain + shift

def gelu_exact(values):
    return 0.5 * values * (1.0 + lax.erf(values * 0.7071067811865476))

def segment_ids(lengths, valid_len):
    ends = jnp.cumsum(lengths)
    position = jnp.arange(ROWS, dtype=jnp.int32)
    segment = lax.optimization_barrier(jnp.sum((position[:, None] >= ends[None, :]).astype(jnp.int32), axis=1))
    return jnp.where(position < valid_len, segment, -1)

def set_attention(operands):
    queries, keys, values, segment = operands
    qheads = queries.reshape(ROWS, HEADS, HD)
    kheads = keys.reshape(ROWS, HEADS, HD)
    vheads = values.reshape(ROWS, HEADS, HD)
    scores = low_back(jnp.einsum('qhd,khd->hqk', qheads, kheads, precision=highest) * 0.125)
    allowed = segment[:, None] == segment[None, :]
    scores = jnp.where(allowed[None], scores, -1000000000.0)
    peak = lax.optimization_barrier(jnp.max(scores, axis=2, keepdims=True))
    expo = jnp.exp(scores - peak)
    probs = low(expo / lax.optimization_barrier(jnp.sum(expo, axis=2, keepdims=True)))
    mixed = jnp.einsum('hqk,khd->qhd', probs, vheads, precision=highest)
    return mixed.reshape(ROWS, HEADS * HD)

def forward(inputs, w_qkv, w_proj, w_fc1, b_fc1, w_fc2, vectors, segment):
    vec_rows = low(vectors).reshape(10, D)
    normed1 = low(layer_norm(inputs, vec_rows[0], vec_rows[1]))
    qkv_sum = jnp.dot(normed1, low(w_qkv).reshape(D, 3 * D), precision=highest)
    queries = low(low_back(qkv_sum[:, :D] + vec_rows[2]))
    keys = low(low_back(qkv_sum[:, D:2 * D]))
    values = low(low_back(qkv_sum[:, 2 * D:] + vec_rows[3]))
    mixed = lax.map(jax.checkpoint(set_attention), (queries.reshape(SETS, ROWS, D), keys.reshape(SETS, ROWS, D), values.reshape(SETS, ROWS, D), segment))
    mixed = low(low_back(mixed.reshape(TOKENS, D)))
    branch1 = low_back(jnp.dot(mixed, low(w_proj).reshape(D, D), precision=highest) + vec_rows[4])
    inner = inputs + vec_rows[5] * branch1
    normed2 = low(layer_norm(inner, vec_rows[6], vec_rows[7]))
    pre_act = low_back(jnp.dot(normed2, low(w_fc1).reshape(D, FF), precision=highest) + low(b_fc1))
    activated = low(gelu_exact(pre_act))
    branch2 = low_back(jnp.dot(activated, low(w_fc2).reshape(FF, D), precision=highest) + vec_rows[8])
    return inner + vec_rows[9] * branch2

def reference(inputs, img_lens, valid_rows, w_qkv, w_proj, w_fc1, b_fc1, w_fc2, vectors, cotangent):
    segment = jax.vmap(segment_ids)(img_lens, valid_rows)

    def wrapped(inputs, w_qkv, w_proj, w_fc1, b_fc1, w_fc2, vectors):
        return forward(inputs, w_qkv, w_proj, w_fc1, b_fc1, w_fc2, vectors, segment)
    result, puller = jax.vjp(wrapped, inputs, w_qkv, w_proj, w_fc1, b_fc1, w_fc2, vectors)
    grads = puller(cotangent)
    return (result, grads[0], grads[1], grads[2], grads[3], grads[4], grads[5], grads[6])
```

```python
import functools

import jax
import jax.numpy as jnp
from jax import lax
from jax.experimental import pallas as pl
from jax.experimental.pallas import tpu as pltpu
from jax.sharding import Mesh
from jax.sharding import PartitionSpec as P

HEADS = 12
HD = 64
ROWS = 1024
D = HEADS * HD
FF = 4 * D
PAIRS = HEADS // 2
BLK = 128
WIN = 3 * BLK
NBLK = ROWS // BLK
TILE = 256
EPS = 1e-06
ALL = ("a", "b", "f", "c")
bf16 = jnp.bfloat16
f32 = jnp.float32
VMEM_LIMIT = 60 * 1024 * 1024


def dot_nn(left, right):
    return lax.dot_general(left, right, (((1,), (0,)), ((), ())), preferred_element_type=f32)


def dot_nt(left, right):
    return lax.dot_general(left, right, (((1,), (1,)), ((), ())), preferred_element_type=f32)


def dot_tn(left, right):
    return lax.dot_general(left, right, (((0,), (0,)), ((), ())), preferred_element_type=f32)


def eye():
    rows = lax.broadcasted_iota(jnp.int32, (BLK, BLK), 0)
    cols = lax.broadcasted_iota(jnp.int32, (BLK, BLK), 1)
    return (rows == cols).astype(f32).astype(bf16)


def flip(one, block):
    return dot_nt(one, block).astype(bf16)


def norm_parts(values):
    center = values - jnp.mean(values, axis=-1, keepdims=True)
    scale = lax.rsqrt(jnp.mean(center * center, axis=-1, keepdims=True) + EPS)
    return center * scale, scale


def norm_back(grad, normed, scale, gain):
    inner = grad * gain
    first = jnp.mean(inner, axis=-1, keepdims=True)
    second = jnp.mean(inner * normed, axis=-1, keepdims=True)
    return scale * (inner - first - normed * second)


def col_sum(values):
    return jnp.sum(values, axis=0, keepdims=True)


def gelu_parts(u):
    mag = jnp.abs(u) * 0.7071067811865476
    t = 1.0 / (1.0 + 0.3275911 * mag)
    e = jnp.exp(-(mag * mag))
    poly = t * (0.254829592 + t * (-0.284496736 + t * (1.421413741 + t * (-1.453152027 + t * 1.061405429))))
    tail = poly * e
    half = 0.5 * jnp.where(u >= 0, 2.0 - tail, tail)
    return u * half, half + 0.3989422804014327 * u * e


def params(**kw):
    return pltpu.CompilerParams(vmem_limit_bytes=VMEM_LIMIT, **kw)


def whole(shape):
    return pl.BlockSpec(shape, lambda *_: (0,) * len(shape))


def qkv_kernel(x_ref, w_ref, vec_ref, q_ref, k_ref, v_ref, kt_ref, vt_ref, ht_ref):
    normed, _ = norm_parts(x_ref[...])
    low = (normed * vec_ref[0:1] + vec_ref[1:2]).astype(bf16)
    one = eye()
    q_ref[...] = ((dot_nn(low, w_ref[:, :D]) + vec_ref[2:3]).astype(bf16).astype(f32) * 0.125).astype(bf16)
    k = dot_nn(low, w_ref[:, D : 2 * D]).astype(bf16)
    v = (dot_nn(low, w_ref[:, 2 * D :]) + vec_ref[3:4]).astype(bf16)
    k_ref[...] = k
    v_ref[...] = v
    for p in range(PAIRS):
        s = slice(p * BLK, (p + 1) * BLK)
        kt_ref[s] = flip(one, k[:, s])
        vt_ref[s] = flip(one, v[:, s])
        ht_ref[s] = flip(one, low[:, s])


def qkv_call(x, w, vec):
    tok = pl.BlockSpec((TILE, D), lambda i: (i, 0))
    feat = pl.BlockSpec((D, TILE), lambda i: (0, i))
    return pl.pallas_call(
        qkv_kernel,
        grid=(ROWS // TILE,),
        in_specs=[tok, whole((D, 3 * D)), whole((16, D))],
        out_specs=[tok, tok, tok, feat, feat, feat],
        out_shape=[jax.ShapeDtypeStruct((ROWS, D), bf16)] * 3 + [jax.ShapeDtypeStruct((D, ROWS), bf16)] * 3,
        compiler_params=params(),
        cost_estimate=pl.CostEstimate(flops=6 * ROWS * D * D, bytes_accessed=16 << 20, transcendentals=0),
        name="norm_qkv",
    )(x, w, vec)


def fill_segments(lens_ref, valid_ref, segc, segr):
    row_c = lax.broadcasted_iota(jnp.int32, (ROWS, BLK), 0)
    row_r = lax.broadcasted_iota(jnp.int32, (8, ROWS), 1)
    sum_c = jnp.zeros((ROWS, BLK), jnp.int32)
    sum_r = jnp.zeros((8, ROWS), jnp.int32)
    end = jnp.int32(0)
    for j in range(lens_ref.shape[1]):
        end = end + lens_ref[0, j]
        sum_c = sum_c + (row_c >= end).astype(jnp.int32)
        sum_r = sum_r + (row_r >= end).astype(jnp.int32)
    valid = valid_ref[0]
    segc[...] = jnp.where(row_c < valid, sum_c, -1)
    segr[...] = jnp.where(row_r < valid, sum_r, -1)


def block_start(i):
    return pl.multiple_of(jnp.clip(i - 1, 0, NBLK - 3) * BLK, BLK)


def block_bias(segc, segr, i, start):
    keys = segc[pl.ds(start, WIN), :]
    rows = segr[0:1, pl.ds(pl.multiple_of(i * BLK, BLK), BLK)]
    bias = jnp.where(keys == rows, 0.0, -1000000000.0).astype(f32)
    return jnp.concatenate([bias, bias], axis=1)


def lane_masks():
    low = lax.broadcasted_iota(jnp.int32, (1, BLK), 1) < HD
    return low.astype(f32).astype(bf16), (1.0 - low.astype(f32)).astype(bf16)


def stack_pair(block, masks):
    return jnp.concatenate([block * masks[0], block * masks[1]], axis=0)


def attn_kernel(lens_ref, valid_ref, q_ref, k_ref, vt_ref, o_ref, ot_ref, lse_ref, segc, segr):
    i = pl.program_id(0)

    @pl.when(i == 0)
    def _():
        fill_segments(lens_ref, valid_ref, segc, segr)

    start = block_start(i)
    bias = block_bias(segc, segr, i, start)
    masks = lane_masks()
    one = eye()
    for p in range(PAIRS):
        s = slice(p * BLK, (p + 1) * BLK)
        queries = stack_pair(q_ref[:, s], masks)
        scores = dot_nt(k_ref[pl.ds(start, WIN), s], queries) + bias
        peak = jnp.max(scores, axis=0, keepdims=True)
        expo = jnp.exp(scores - peak)
        total = col_sum(expo)
        mixed = dot_nn(vt_ref[s, pl.ds(start, WIN)], expo.astype(bf16)) / total
        flat = jnp.concatenate([mixed[:HD, :BLK], mixed[HD:, BLK:]], axis=0).astype(bf16)
        ot_ref[s] = flat
        o_ref[:, s] = flip(one, flat)
        lse_ref[0, p : p + 1] = peak + jnp.log(total)


def attn_call(lens, valid, q, k, vt):
    return pl.pallas_call(
        attn_kernel,
        grid=(NBLK,),
        in_specs=[
            pl.BlockSpec(memory_space=pltpu.SMEM),
            pl.BlockSpec(memory_space=pltpu.SMEM),
            pl.BlockSpec((BLK, D), lambda i: (i, 0)),
            whole((ROWS, D)),
            whole((D, ROWS)),
        ],
        out_specs=[
            pl.BlockSpec((BLK, D), lambda i: (i, 0)),
            pl.BlockSpec((D, BLK), lambda i: (0, i)),
            pl.BlockSpec((1, 8, 2 * BLK), lambda i: (i, 0, 0)),
        ],
        out_shape=[
            jax.ShapeDtypeStruct((ROWS, D), bf16),
            jax.ShapeDtypeStruct((D, ROWS), bf16),
            jax.ShapeDtypeStruct((NBLK, 8, 2 * BLK), f32),
        ],
        scratch_shapes=[pltpu.VMEM((ROWS, BLK), jnp.int32), pltpu.VMEM((8, ROWS), jnp.int32)],
        compiler_params=params(),
        cost_estimate=pl.CostEstimate(flops=4 << 30, bytes_accessed=8 << 20, transcendentals=5 << 20),
        name="attend",
    )(lens, valid, q, k, vt)


def proj_kernel(o_ref, w_ref, x_ref, ct_ref, vec_ref, x1_ref, a_ref, h_ref, ht_ref, dz_ref):
    branch = dot_nn(o_ref[...], w_ref[...]) + vec_ref[4:5]
    inner = x_ref[...] + vec_ref[5:6] * branch
    x1_ref[...] = inner
    a_ref[...] = branch.astype(bf16)
    normed, _ = norm_parts(inner)
    low = (normed * vec_ref[6:7] + vec_ref[7:8]).astype(bf16)
    h_ref[...] = low
    one = eye()
    for p in range(PAIRS):
        s = slice(p * BLK, (p + 1) * BLK)
        ht_ref[s] = flip(one, low[:, s])
    dz_ref[...] = (vec_ref[9:10] * ct_ref[...]).astype(bf16)


def proj_call(o, w, x, ct, vec):
    tok = pl.BlockSpec((TILE, D), lambda i: (i, 0))
    feat = pl.BlockSpec((D, TILE), lambda i: (0, i))
    return pl.pallas_call(
        proj_kernel,
        grid=(ROWS // TILE,),
        in_specs=[tok, whole((D, D)), tok, tok, whole((16, D))],
        out_specs=[tok, tok, tok, feat, tok],
        out_shape=[
            jax.ShapeDtypeStruct((ROWS, D), f32),
            jax.ShapeDtypeStruct((ROWS, D), bf16),
            jax.ShapeDtypeStruct((ROWS, D), bf16),
            jax.ShapeDtypeStruct((D, ROWS), bf16),
            jax.ShapeDtypeStruct((ROWS, D), bf16),
        ],
        compiler_params=params(),
        cost_estimate=pl.CostEstimate(flops=2 * ROWS * D * D, bytes_accessed=18 << 20, transcendentals=0),
        name="proj_norm",
    )(o, w, x, ct, vec)


CHUNK = 512


def up_kernel(h_ref, dz_ref, w_ref, b_ref, m_ref, gp_ref, dw_ref):
    for t in range(ROWS // TILE):
        r = slice(t * TILE, (t + 1) * TILE)
        m, gp = gelu_parts(dot_nn(h_ref[r], w_ref[...]) + b_ref[...])
        m_ref[r] = m.astype(bf16)
        gp_ref[r] = gp.astype(bf16)
    dw_ref[...] = dot_tn(m_ref[...], dz_ref[...]).astype(bf16)


def up_call(h, dz, w, b):
    part = pl.BlockSpec((ROWS, CHUNK), lambda j: (0, j))
    return pl.pallas_call(
        up_kernel,
        grid=(FF // CHUNK,),
        in_specs=[
            whole((ROWS, D)),
            whole((ROWS, D)),
            pl.BlockSpec((D, CHUNK), lambda j: (0, j)),
            pl.BlockSpec((1, CHUNK), lambda j: (0, j)),
        ],
        out_specs=[part, part, pl.BlockSpec((CHUNK, D), lambda j: (j, 0))],
        out_shape=[
            jax.ShapeDtypeStruct((ROWS, FF), bf16),
            jax.ShapeDtypeStruct((ROWS, FF), bf16),
            jax.ShapeDtypeStruct((FF, D), bf16),
        ],
        compiler_params=params(),
        cost_estimate=pl.CostEstimate(flops=4 * ROWS * D * FF, bytes_accessed=25 << 20, transcendentals=6 << 20),
        name="mlp_up",
    )(h, dz, w, b)


def down_kernel(
    m_ref, gp_ref, dz_ref, ht_ref, w1_ref, w2_ref, x1_ref, ct_ref, a_ref, ot_ref, wp_ref, vec_ref,
    out_ref, dx_ref, do_ref, dw1_ref, dwp_ref, db1_ref, sums_ref, z_acc, dh_acc,
):
    j = pl.program_id(0)
    z = dot_nn(m_ref[...], w2_ref[...])
    du = (dot_nt(dz_ref[...], w2_ref[...]) * gp_ref[...].astype(f32)).astype(bf16)
    db1_ref[...] = col_sum(du.astype(f32))
    dw1_ref[...] = dot_nn(ht_ref[...], du).astype(bf16)
    dh = dot_nt(du, w1_ref[...])

    @pl.when(j == 0)
    def _():
        z_acc[...] = z
        dh_acc[...] = dh

    @pl.when(j > 0)
    def _():
        z_acc[...] += z
        dh_acc[...] += dh

    @pl.when(j == FF // CHUNK - 1)
    def _():
        sums = [jnp.zeros((1, D), f32) for _ in range(6)]
        dwp = jnp.zeros((D, D), f32)
        for t in range(ROWS // TILE):
            r = slice(t * TILE, (t + 1) * TILE)
            inner, ct, branch = x1_ref[r], ct_ref[r], z_acc[r] + vec_ref[8:9]
            out_ref[r] = inner + vec_ref[9:10] * branch
            normed, scale = norm_parts(inner)
            dh_t = dh_acc[r]
            dx = ct + norm_back(dh_t, normed, scale, vec_ref[6:7])
            dx_ref[r] = dx
            da = (vec_ref[5:6] * dx).astype(bf16)
            do_ref[r] = dot_nt(da, wp_ref[...]).astype(bf16)
            dwp = dwp + dot_nn(ot_ref[:, r], da)
            adds = (da.astype(f32), dx * a_ref[r].astype(f32), dh_t * normed, dh_t, dz_ref[r].astype(f32), ct * branch)
            sums = [s + col_sum(v) for s, v in zip(sums, adds)]
        dwp_ref[...] = dwp.astype(bf16)
        sums_ref[...] = jnp.concatenate(sums + [jnp.zeros((2, D), f32)], axis=0)


def down_call(m, gp, dz, ht, w1, w2, x1, ct, a, ot, wp, vec):
    part = pl.BlockSpec((ROWS, CHUNK), lambda j: (0, j))
    return pl.pallas_call(
        down_kernel,
        grid=(FF // CHUNK,),
        in_specs=[
            part,
            part,
            whole((ROWS, D)),
            whole((D, ROWS)),
            pl.BlockSpec((D, CHUNK), lambda j: (0, j)),
            pl.BlockSpec((CHUNK, D), lambda j: (j, 0)),
            whole((ROWS, D)),
            whole((ROWS, D)),
            whole((ROWS, D)),
            whole((D, ROWS)),
            whole((D, D)),
            whole((16, D)),
        ],
        out_specs=[
            whole((ROWS, D)),
            whole((ROWS, D)),
            whole((ROWS, D)),
            pl.BlockSpec((D, CHUNK), lambda j: (0, j)),
            whole((D, D)),
            pl.BlockSpec((1, CHUNK), lambda j: (0, j)),
            whole((8, D)),
        ],
        out_shape=[
            jax.ShapeDtypeStruct((ROWS, D), f32),
            jax.ShapeDtypeStruct((ROWS, D), f32),
            jax.ShapeDtypeStruct((ROWS, D), bf16),
            jax.ShapeDtypeStruct((D, FF), bf16),
            jax.ShapeDtypeStruct((D, D), bf16),
            jax.ShapeDtypeStruct((1, FF), f32),
            jax.ShapeDtypeStruct((8, D), f32),
        ],
        scratch_shapes=[pltpu.VMEM((ROWS, D), f32), pltpu.VMEM((ROWS, D), f32)],
        compiler_params=params(),
        cost_estimate=pl.CostEstimate(flops=8 * ROWS * D * FF + 4 * ROWS * D * D, bytes_accessed=50 << 20, transcendentals=0),
        name="mlp_down",
    )(m, gp, dz, ht, w1, w2, x1, ct, a, ot, wp, vec)


def back_kernel(
    lens_ref, valid_ref, q_ref, k_ref, v_ref, do_ref, kt_ref, lse_ref, ht_ref,
    dqkv_ref, dw_ref, sums_ref, segc, segr, dk_acc, dv_acc,
):
    i = pl.program_id(0)

    @pl.when(i == 0)
    def _():
        fill_segments(lens_ref, valid_ref, segc, segr)
        dk_acc[...] = jnp.zeros_like(dk_acc)
        dv_acc[...] = jnp.zeros_like(dv_acc)

    start = block_start(i)
    here = pl.multiple_of(i * BLK, BLK)
    bias = block_bias(segc, segr, i, start)
    masks = lane_masks()
    one = eye()
    window = pl.ds(start, WIN)
    for p in range(PAIRS):
        s = slice(p * BLK, (p + 1) * BLK)
        queries = stack_pair(q_ref[:, s], masks)
        grads = stack_pair(do_ref[:, s], masks)
        probs = jnp.exp(dot_nt(k_ref[window, s], queries) + bias - lse_ref[0, p : p + 1])
        dprobs = dot_nt(v_ref[window, s], grads)
        dv_acc[window, s] += dot_nn(probs.astype(bf16), grads)
        center = col_sum(probs * dprobs)
        dscores = (probs * (dprobs - center)).astype(bf16)
        dk_acc[window, s] += dot_nn(dscores, queries)
        dq = dot_nn(kt_ref[s, window], dscores)
        dq = (jnp.concatenate([dq[:HD, :BLK], dq[HD:, BLK:]], axis=0) * 0.125).astype(bf16)
        dqkv_ref[pl.ds(here, BLK), s] = flip(one, dq)

    @pl.when(i == NBLK - 1)
    def _():
        dqkv_ref[:, D : 2 * D] = dk_acc[...].astype(bf16)
        dqkv_ref[:, 2 * D :] = dv_acc[...].astype(bf16)
        for c in range(3):
            s = slice(c * D, (c + 1) * D)
            dw_ref[:, s] = dot_nn(ht_ref[...], dqkv_ref[:, s]).astype(bf16)
        dbq = col_sum(dqkv_ref[:, :D].astype(f32))
        dbv = col_sum(dqkv_ref[:, 2 * D :].astype(f32))
        sums_ref[...] = jnp.concatenate([dbq, dbv, jnp.zeros((6, D), f32)], axis=0)


def back_call(lens, valid, q, k, v, do, kt, lse, ht):
    tok = pl.BlockSpec((BLK, D), lambda i: (i, 0))
    return pl.pallas_call(
        back_kernel,
        grid=(NBLK,),
        in_specs=[
            pl.BlockSpec(memory_space=pltpu.SMEM),
            pl.BlockSpec(memory_space=pltpu.SMEM),
            tok,
            whole((ROWS, D)),
            whole((ROWS, D)),
            tok,
            whole((D, ROWS)),
            pl.BlockSpec((1, 8, 2 * BLK), lambda i: (i, 0, 0)),
            whole((D, ROWS)),
        ],
        out_specs=[whole((ROWS, 3 * D)), whole((D, 3 * D)), whole((8, D))],
        out_shape=[
            jax.ShapeDtypeStruct((ROWS, 3 * D), bf16),
            jax.ShapeDtypeStruct((D, 3 * D), bf16),
            jax.ShapeDtypeStruct((8, D), f32),
        ],
        scratch_shapes=[
            pltpu.VMEM((ROWS, BLK), jnp.int32),
            pltpu.VMEM((8, ROWS), jnp.int32),
            pltpu.VMEM((ROWS, D), f32),
            pltpu.VMEM((ROWS, D), f32),
        ],
        compiler_params=params(),
        cost_estimate=pl.CostEstimate(flops=20 << 30, bytes_accessed=20 << 20, transcendentals=5 << 20),
        name="attend_back",
    )(lens, valid, q, k, v, do, kt, lse, ht)


def input_kernel(dqkv_ref, w_ref, x_ref, dx1_ref, vec_ref, dx_ref, sums_ref):
    i = pl.program_id(0)
    dh = dot_nt(dqkv_ref[...], w_ref[...])
    normed, scale = norm_parts(x_ref[...])
    dx_ref[...] = dx1_ref[...] + norm_back(dh, normed, scale, vec_ref[0:1])
    sums = jnp.concatenate([col_sum(dh * normed), col_sum(dh), jnp.zeros((6, D), f32)], axis=0)

    @pl.when(i == 0)
    def _():
        sums_ref[...] = sums

    @pl.when(i > 0)
    def _():
        sums_ref[...] += sums


def input_call(dqkv, w, x, dx1, vec):
    tok = pl.BlockSpec((TILE, D), lambda i: (i, 0))
    return pl.pallas_call(
        input_kernel,
        grid=(ROWS // TILE,),
        in_specs=[pl.BlockSpec((TILE, 3 * D), lambda i: (i, 0)), whole((D, 3 * D)), tok, tok, whole((16, D))],
        out_specs=[tok, whole((8, D))],
        out_shape=[jax.ShapeDtypeStruct((ROWS, D), f32), jax.ShapeDtypeStruct((8, D), f32)],
        compiler_params=params(),
        cost_estimate=pl.CostEstimate(flops=6 * ROWS * D * D, bytes_accessed=18 << 20, transcendentals=0),
        name="input_back",
    )(dqkv, w, x, dx1, vec)


def swap_cores(x):
    return lax.ppermute(x, "c", [(0, 1), (1, 0)])


def spread(x, axes):
    count = lax.axis_size(axes)
    return lax.all_to_all(jnp.broadcast_to(x[None], (count,) + x.shape), axes, 0, 0)


def gather_start(shard):
    mine = spread(spread(shard, "a"), ("b", "f"))
    return mine, swap_cores(mine)


def gather_rows(mine, other, cols):
    core = lax.axis_index("c")
    mine, other = mine[..., cols], other[..., cols]
    both = jnp.stack([jnp.where(core == 0, mine, other), jnp.where(core == 0, other, mine)], axis=2)
    return jnp.transpose(both, (1, 0, 2, 3, 4))


def scatter_sum(grad, rows):
    na, nbf = lax.axis_size("a"), lax.axis_size(("b", "f"))
    core = lax.axis_index("c")
    grad = grad.reshape(na, nbf, 2, rows, grad.shape[-1])
    away = lax.dynamic_index_in_dim(grad, 1 - core, 2, keepdims=False)
    keep = lax.dynamic_index_in_dim(grad, core, 2, keepdims=False)
    half = (keep.astype(f32) + swap_cores(away).astype(f32)).astype(bf16)
    part = lax.all_to_all(jnp.swapaxes(half, 0, 1), ("b", "f"), 0, 0)
    part = jnp.sum(part.astype(f32), axis=0).astype(bf16)
    part = lax.all_to_all(part, "a", 0, 0)
    return jnp.sum(part.astype(f32), axis=0)


def shards(inputs, img_lens, valid_rows, w_qkv, w_proj, w_fc1, b_fc1, w_fc2, vectors, cotangent):
    devices = lax.axis_size(ALL)
    rows = D // devices
    slots = rows * BLK
    small = jnp.concatenate([vectors, b_fc1])
    small = jnp.pad(small, (0, slots - small.shape[0])).reshape(rows, BLK)
    head = jnp.concatenate([w_qkv.reshape(rows, 3 * D), small], axis=1).astype(bf16)
    fc2_shard = jnp.swapaxes(w_fc2.reshape(4, rows, D), 0, 1).reshape(rows, 4 * D)
    rest = jnp.concatenate([w_proj.reshape(rows, D), w_fc1.reshape(rows, FF), fc2_shard], axis=1).astype(bf16)

    head_parts = gather_start(head)
    rest_parts = gather_start(rest)
    small = gather_rows(*head_parts, slice(3 * D, 3 * D + BLK)).reshape(devices, slots)
    nvec = vectors.shape[0]
    vec = small[:, :nvec].astype(f32).reshape(10, D)
    vec = jnp.concatenate([vec, jnp.zeros((6, D), f32)], axis=0)
    b1 = small[:, nvec : nvec + b_fc1.shape[0]].astype(f32).reshape(1, FF)
    wqkv = gather_rows(*head_parts, slice(0, 3 * D)).reshape(D, 3 * D)

    q, k, v, kt, vt, h1t = qkv_call(inputs, wqkv, vec)
    o, ot, lse = attn_call(img_lens, valid_rows, q, k, vt)

    wp = gather_rows(*rest_parts, slice(0, D)).reshape(D, D)
    w1 = gather_rows(*rest_parts, slice(D, D + FF)).reshape(D, FF)
    w2 = jnp.stack([gather_rows(*rest_parts, slice(D + FF + g * D, D + FF + (g + 1) * D)) for g in range(4)], axis=3)
    w2 = w2.reshape(FF, D)

    x1, a, h2, h2t, dz = proj_call(o, wp, inputs, cotangent, vec)
    m, gp, dw2 = up_call(h2, dz, w1, b1)
    g_fc2 = scatter_sum(dw2, 4 * rows)
    result, dx1, do, dw1, dwp, db1, sums2 = down_call(m, gp, dz, h2t, w1, w2, x1, cotangent, a, ot, wp, vec)
    g_fc1 = scatter_sum(dw1, rows)
    g_proj = scatter_sum(dwp, rows)
    dqkv, dwqkv, sums1 = back_call(img_lens, valid_rows, q, k, v, do, kt, lse, h1t)
    g_qkv = scatter_sum(dwqkv, rows)
    d_input, sums0 = input_call(dqkv, wqkv, inputs, dx1, vec)

    gvec = jnp.concatenate([sums0[:2], sums1[:2], sums2[:6]], axis=0).reshape(devices, nvec)
    gsmall = jnp.concatenate([gvec, db1.reshape(devices, b_fc1.shape[0])], axis=1)
    gsmall = jnp.pad(gsmall, ((0, 0), (0, -gsmall.shape[1] % BLK))).astype(bf16)
    gsmall = scatter_sum(gsmall, 1).reshape(-1)
    return (
        result,
        d_input,
        g_qkv.reshape(-1),
        g_proj.reshape(-1),
        g_fc1.reshape(-1),
        gsmall[nvec : nvec + b_fc1.shape[0]],
        g_fc2.reshape(-1),
        gsmall[:nvec],
    )


def solution(mesh):
    dp, fsdp = mesh.shape["dp"], mesh.shape["fsdp"]
    fine = Mesh(mesh.devices.reshape(dp // 2, 2, fsdp // 2, 2), ALL)
    rows, flat = P(ALL, None), P(ALL)
    return jax.shard_map(
        shards,
        mesh=fine,
        in_specs=(rows, rows, flat, flat, flat, flat, flat, flat, flat, rows),
        out_specs=(rows, rows, flat, flat, flat, flat, flat, flat),
        check_vma=False,
    )
```

```python
import functools

import jax
import jax.numpy as jnp
from jax import lax
from jax.experimental import pallas as pl
from jax.experimental.pallas import tpu as pltpu
from jax.sharding import Mesh
from jax.sharding import PartitionSpec as P

HEADS = 12
HD = 64
ROWS = 1024
D = HEADS * HD
FF = 4 * D
PAIRS = HEADS // 2
BLK = 128
WIN = 3 * BLK
NBLK = ROWS // BLK
TILE = 256
EPS = 1e-06
ALL = ("a", "b", "f", "c")
bf16 = jnp.bfloat16
f32 = jnp.float32
VMEM_LIMIT = 60 * 1024 * 1024
ANY = pl.BlockSpec(memory_space=pl.ANY)


def cost(us):
    return pl.CostEstimate(flops=us * 1_100_000_000, bytes_accessed=us * 3_000_000, transcendentals=0)


def dot_nn(left, right):
    return lax.dot_general(left, right, (((1,), (0,)), ((), ())), preferred_element_type=f32)


def dot_nt(left, right):
    return lax.dot_general(left, right, (((1,), (1,)), ((), ())), preferred_element_type=f32)


def dot_tn(left, right):
    return lax.dot_general(left, right, (((0,), (0,)), ((), ())), preferred_element_type=f32)


def eye():
    rows = lax.broadcasted_iota(jnp.int32, (BLK, BLK), 0)
    cols = lax.broadcasted_iota(jnp.int32, (BLK, BLK), 1)
    return (rows == cols).astype(f32).astype(bf16)


def flip(one, block):
    return dot_nt(one, block).astype(bf16)


def norm_parts(values):
    center = values - jnp.mean(values, axis=-1, keepdims=True)
    scale = lax.rsqrt(jnp.mean(center * center, axis=-1, keepdims=True) + EPS)
    return center * scale, scale


def norm_back(grad, normed, scale, gain):
    inner = grad * gain
    first = jnp.mean(inner, axis=-1, keepdims=True)
    second = jnp.mean(inner * normed, axis=-1, keepdims=True)
    return scale * (inner - first - normed * second)


def col_sum(values):
    return jnp.sum(values, axis=0, keepdims=True)


def gelu_parts(u):
    mag = jnp.abs(u) * 0.7071067811865476
    t = 1.0 / (1.0 + 0.3275911 * mag)
    e = jnp.exp(-(mag * mag))
    poly = t * (0.254829592 + t * (-0.284496736 + t * (1.421413741 + t * (-1.453152027 + t * 1.061405429))))
    tail = poly * e
    half = 0.5 * jnp.where(u >= 0, 2.0 - tail, tail)
    return u * half, half + 0.3989422804014327 * u * e


def params(**kw):
    return pltpu.CompilerParams(vmem_limit_bytes=VMEM_LIMIT, **kw)


def whole(shape):
    return pl.BlockSpec(shape, lambda *_: (0,) * len(shape))


def qkv_kernel(*refs):
    parts, refs = refs[:-15], refs[-15:]
    x_ref, turn_ref, vec_ref, _, q_ref, k_ref, v_ref, kt_ref, vt_ref, ht_ref, w_out, w_ref, sems, out_sem, _ = refs
    size = D // len(parts)

    def copies():
        return [
            pltpu.make_async_copy(p.at[:, : 3 * D], w_ref.at[pl.ds(n * size, size)], sems.at[n]) for n, p in enumerate(parts)
        ]

    def keep():
        return pltpu.make_async_copy(w_ref, w_out, out_sem)

    @pl.when(pl.program_id(0) == 0)
    def _():
        for copy in copies():
            copy.start()
        for copy in copies():
            copy.wait()
        keep().start()

    normed, _ = norm_parts(x_ref[...])
    low = dot_nn((normed * vec_ref[0:1] + vec_ref[1:2]).astype(bf16), turn_ref[...]).astype(bf16)
    one = eye()
    q_ref[...] = ((dot_nn(low, w_ref[:, :D]) + vec_ref[2:3]).astype(bf16).astype(f32) * 0.125).astype(bf16)
    k = dot_nn(low, w_ref[:, D : 2 * D]).astype(bf16)
    v = (dot_nn(low, w_ref[:, 2 * D :]) + vec_ref[3:4]).astype(bf16)
    k_ref[...] = k
    v_ref[...] = v
    for p in range(PAIRS):
        s = slice(p * BLK, (p + 1) * BLK)
        kt_ref[s] = flip(one, k[:, s])
        vt_ref[s] = flip(one, v[:, s])
        ht_ref[s] = flip(one, low[:, s])

    @pl.when(pl.program_id(0) == ROWS // TILE - 1)
    def _():
        keep().wait()


def qkv_call(parts, x, turn, vec, token):
    tok = pl.BlockSpec((TILE, D), lambda i: (i, 0))
    feat = pl.BlockSpec((D, TILE), lambda i: (0, i))
    return pl.pallas_call(
        qkv_kernel,
        grid=(ROWS // TILE,),
        in_specs=[ANY] * len(parts) + [tok, whole((D, D)), whole((16, D)), ANY],
        out_specs=[tok, tok, tok, feat, feat, feat, ANY],
        out_shape=[jax.ShapeDtypeStruct((ROWS, D), bf16)] * 3
        + [jax.ShapeDtypeStruct((D, ROWS), bf16)] * 3
        + [jax.ShapeDtypeStruct((D, 3 * D), bf16)],
        scratch_shapes=[
            pltpu.VMEM((D, 3 * D), bf16),
            pltpu.SemaphoreType.DMA((len(parts),)),
            pltpu.SemaphoreType.DMA,
            pltpu.VMEM((8, BLK), f32),
        ],
        compiler_params=params(),
        cost_estimate=cost(14),
        name="norm_qkv",
    )(*parts, x, turn, vec, token)


def fill_segments(lens_ref, valid_ref, segc, segr):
    row_c = lax.broadcasted_iota(jnp.int32, (ROWS, BLK), 0)
    row_r = lax.broadcasted_iota(jnp.int32, (8, ROWS), 1)
    sum_c = jnp.zeros((ROWS, BLK), jnp.int32)
    sum_r = jnp.zeros((8, ROWS), jnp.int32)
    end = jnp.int32(0)
    for j in range(lens_ref.shape[1]):
        end = end + lens_ref[0, j]
        sum_c = sum_c + (row_c >= end).astype(jnp.int32)
        sum_r = sum_r + (row_r >= end).astype(jnp.int32)
    valid = valid_ref[0]
    segc[...] = jnp.where(row_c < valid, sum_c, -1)
    segr[...] = jnp.where(row_r < valid, sum_r, -1)


def block_start(i):
    return pl.multiple_of(jnp.clip(i - 1, 0, NBLK - 3) * BLK, BLK)


def block_bias(segc, segr, i, start):
    keys = segc[pl.ds(start, WIN), :]
    rows = segr[0:1, pl.ds(pl.multiple_of(i * BLK, BLK), BLK)]
    bias = jnp.where(keys == rows, 0.0, -1000000000.0).astype(f32)
    return jnp.concatenate([bias, bias], axis=1)


def lane_masks():
    low = lax.broadcasted_iota(jnp.int32, (1, BLK), 1) < HD
    return low.astype(f32).astype(bf16), (1.0 - low.astype(f32)).astype(bf16)


def stack_pair(block, masks):
    return jnp.concatenate([block * masks[0], block * masks[1]], axis=0)


def attn_kernel(lens_ref, valid_ref, q_ref, k_ref, vt_ref, o_ref, lse_ref, segc, segr):
    i = pl.program_id(0)

    @pl.when(i == 0)
    def _():
        fill_segments(lens_ref, valid_ref, segc, segr)

    start = block_start(i)
    bias = block_bias(segc, segr, i, start)
    masks = lane_masks()
    one = eye()
    for p in range(PAIRS):
        s = slice(p * BLK, (p + 1) * BLK)
        queries = stack_pair(q_ref[:, s], masks)
        scores = dot_nt(k_ref[pl.ds(start, WIN), s], queries) + bias
        peak = jnp.max(scores, axis=0, keepdims=True)
        expo = jnp.exp(scores - peak)
        total = col_sum(expo)
        mixed = dot_nn(vt_ref[s, pl.ds(start, WIN)], expo.astype(bf16)) / total
        flat = jnp.concatenate([mixed[:HD, :BLK], mixed[HD:, BLK:]], axis=0).astype(bf16)
        o_ref[:, s] = flip(one, flat)
        lse_ref[0, p : p + 1] = peak + jnp.log(total)


def attn_call(lens, valid, q, k, vt):
    return pl.pallas_call(
        attn_kernel,
        grid=(NBLK,),
        in_specs=[
            pl.BlockSpec(memory_space=pltpu.SMEM),
            pl.BlockSpec(memory_space=pltpu.SMEM),
            pl.BlockSpec((BLK, D), lambda i: (i, 0)),
            whole((ROWS, D)),
            whole((D, ROWS)),
        ],
        out_specs=[
            pl.BlockSpec((BLK, D), lambda i: (i, 0)),
            pl.BlockSpec((1, 8, 2 * BLK), lambda i: (i, 0, 0)),
        ],
        out_shape=[
            jax.ShapeDtypeStruct((ROWS, D), bf16),
            jax.ShapeDtypeStruct((NBLK, 8, 2 * BLK), f32),
        ],
        scratch_shapes=[pltpu.VMEM((ROWS, BLK), jnp.int32), pltpu.VMEM((8, ROWS), jnp.int32)],
        compiler_params=params(),
        cost_estimate=cost(20),
        name="attend",
    )(lens, valid, q, k, vt)


def proj_kernel(o_ref, w_ref, x_ref, ct_ref, turn_ref, vec_ref, x1_ref, a_ref, h_ref, ht_ref, ot_ref, dz_ref):
    weight = w_ref[...].astype(f32).reshape(D, D).astype(bf16)
    branch = dot_nn(o_ref[...], weight) + vec_ref[4:5]
    inner = x_ref[...] + vec_ref[5:6] * branch
    x1_ref[...] = inner
    a_ref[...] = branch.astype(bf16)
    normed, _ = norm_parts(inner)
    low = (normed * vec_ref[6:7] + vec_ref[7:8]).astype(bf16)
    h_ref[...] = low
    one = eye()
    turned = dot_nn(low, turn_ref[...]).astype(bf16)
    turned_o = dot_nn(o_ref[...], turn_ref[...]).astype(bf16)
    for p in range(PAIRS):
        s = slice(p * BLK, (p + 1) * BLK)
        ht_ref[s] = flip(one, turned[:, s])
        ot_ref[s] = flip(one, turned_o[:, s])
    dz_ref[...] = (vec_ref[9:10] * ct_ref[...]).astype(bf16)


def proj_call(o, mlp, x, ct, turn, vec):
    n, _, _ = mlp.shape
    r = D // n
    tok = pl.BlockSpec((TILE, D), lambda i: (i, 0))
    feat = pl.BlockSpec((D, TILE), lambda i: (0, i))
    return pl.pallas_call(
        proj_kernel,
        grid=(ROWS // TILE,),
        in_specs=[tok, pl.BlockSpec((n, r, D), lambda i: (0, 8, 0)), tok, tok, whole((D, D)), whole((16, D))],
        out_specs=[tok, tok, tok, feat, feat, tok],
        out_shape=[
            jax.ShapeDtypeStruct((ROWS, D), f32),
            jax.ShapeDtypeStruct((ROWS, D), bf16),
            jax.ShapeDtypeStruct((ROWS, D), bf16),
            jax.ShapeDtypeStruct((D, ROWS), bf16),
            jax.ShapeDtypeStruct((D, ROWS), bf16),
            jax.ShapeDtypeStruct((ROWS, D), bf16),
        ],
        compiler_params=params(),
        cost_estimate=cost(11),
        name="proj_norm",
    )(o, mlp, x, ct, turn, vec)


STEPS = FF // D


def up_kernel(me_ref, h_ref, dz_ref, w_ref, b_ref, m_ref, gp_ref, *refs):
    weight = w_ref[...].astype(f32).reshape(D, D).astype(bf16)
    for t in range(ROWS // TILE):
        r = slice(t * TILE, (t + 1) * TILE)
        m, gp = gelu_parts(dot_nn(h_ref[r], weight) + b_ref[...])
        m_ref[r] = m.astype(bf16)
        gp_ref[r] = gp.astype(bf16)
    if len(refs) == 1:
        refs[0][...] = dot_tn(m_ref[...], dz_ref[...]).astype(bf16)
        return
    keep_ref, away_ref, dw_ref = refs
    dw_ref[...] = dot_tn(m_ref[...], dz_ref[...])
    count, _, size, _ = keep_ref.shape
    for k in range(count):
        for c, ref in enumerate((keep_ref, away_ref)):
            row = ((k ^ me_ref[1]) * 2 + (c ^ me_ref[2])) * size
            ref[k, 0] = dw_ref[pl.ds(pl.multiple_of(row, 8), size), :].astype(bf16)


def up_call(me, h, dz, mlp, b, direct):
    n = mlp.shape[0]
    r = D // n
    part = pl.BlockSpec((ROWS, D), lambda j, me: (0, j ^ me[0]))
    if direct:
        grads = (n // (2 * STEPS), STEPS, 4 * r, D)
        spec = pl.BlockSpec((grads[0], 1, 4 * r, D), lambda j, me: (0, j, 0, 0))
        grad_specs, grad_shapes = [spec] * 2, [jax.ShapeDtypeStruct(grads, bf16)] * 2
    else:
        grad_specs = [pl.BlockSpec((D, D), lambda j, me: (j ^ me[0], 0))]
        grad_shapes = [jax.ShapeDtypeStruct((FF, D), bf16)]
    return pl.pallas_call(
        up_kernel,
        grid_spec=pltpu.PrefetchScalarGridSpec(
            num_scalar_prefetch=1,
            grid=(STEPS,),
            in_specs=[
                whole((ROWS, D)),
                whole((ROWS, D)),
                pl.BlockSpec((n, r, D), lambda j, me: (0, 4 + (j ^ me[0]), 0)),
                pl.BlockSpec((1, D), lambda j, me: (0, j ^ me[0])),
            ],
            out_specs=[part, part] + grad_specs,
            scratch_shapes=[pltpu.VMEM((D, D), f32)] if direct else [],
        ),
        out_shape=[jax.ShapeDtypeStruct((ROWS, FF), bf16)] * 2 + grad_shapes,
        compiler_params=params(),
        cost_estimate=cost(25),
        name="mlp_up",
    )(me, h, dz, mlp, b)


def down_kernel(m_ref, gp_ref, dz_ref, ht_ref, w1_ref, w2_ref, x1_ref, ct_ref, a_ref, ot_ref, wp_ref, vec_ref, *refs):
    out_ref, dx_ref, do_ref, keep_ref, away_ref, db1_ref, sums_ref, _, z_acc, dh_acc = refs[-10:]
    j = pl.program_id(0)

    @pl.when(j < STEPS)
    def _():
        w1 = w1_ref[...].astype(f32).reshape(D, D).astype(bf16)
        w2 = w2_ref[...].reshape(D, D)
        z = dot_nn(m_ref[...], w2)
        du = (dot_nt(dz_ref[...], w2) * gp_ref[...].astype(f32)).astype(bf16)
        db1_ref[...] = col_sum(du.astype(f32))
        keep_ref[...] = dot_nn(ht_ref[: D // 2], du).astype(bf16)
        away_ref[...] = dot_nn(ht_ref[D // 2 :], du).astype(bf16)
        dh = dot_nt(du, w1)

        @pl.when(j == 0)
        def _():
            z_acc[...] = z
            dh_acc[...] = dh

        @pl.when(j > 0)
        def _():
            z_acc[...] += z
            dh_acc[...] += dh

    @pl.when(j == STEPS)
    def _():
        wp = wp_ref[...].astype(f32).reshape(D, D).astype(bf16)
        sums = [jnp.zeros((1, D), f32) for _ in range(6)]
        dwp = jnp.zeros((D, D), f32)
        for t in range(ROWS // TILE):
            r = slice(t * TILE, (t + 1) * TILE)
            inner, ct, branch = x1_ref[r], ct_ref[r], z_acc[r] + vec_ref[8:9]
            out_ref[r] = inner + vec_ref[9:10] * branch
            normed, scale = norm_parts(inner)
            dh_t = dh_acc[r]
            dx = ct + norm_back(dh_t, normed, scale, vec_ref[6:7])
            dx_ref[r] = dx
            da = (vec_ref[5:6] * dx).astype(bf16)
            do_ref[r] = dot_nt(da, wp).astype(bf16)
            dwp = dwp + dot_nn(ot_ref[:, r], da)
            adds = (da.astype(f32), dx * a_ref[r].astype(f32), dh_t * normed, dh_t, dz_ref[r].astype(f32), ct * branch)
            sums = [s + col_sum(v) for s, v in zip(sums, adds)]
        keep_ref[...] = dwp[: D // 2].astype(bf16)
        away_ref[...] = dwp[D // 2 :].astype(bf16)
        sums_ref[...] = jnp.concatenate(sums + [jnp.zeros((2, D), f32)], axis=0)


def down_call(m, gp, dz, ht, mlp, x1, ct, a, ot, vec, passed, tokens):
    n = mlp.shape[0]
    r = D // n

    def last(j):
        return jnp.minimum(j, STEPS - 1)

    part = pl.BlockSpec((ROWS, D), lambda j: (0, last(j)))
    grad = pl.BlockSpec((D // 2, D), lambda j: (0, j))
    return pl.pallas_call(
        down_kernel,
        grid=(STEPS + 1,),
        in_specs=[
            part,
            part,
            whole((ROWS, D)),
            whole((D, ROWS)),
            pl.BlockSpec((n, r, D), lambda j: (0, 4 + last(j), 0)),
            pl.BlockSpec((n // 4, 4 * r, D), lambda j: (last(j), 0, 0)),
            whole((ROWS, D)),
            whole((ROWS, D)),
            whole((ROWS, D)),
            whole((D, ROWS)),
            pl.BlockSpec((n, r, D), lambda j: (0, 8, 0)),
            whole((16, D)),
            ANY,
        ]
        + [ANY] * len(tokens),
        out_specs=[
            whole((ROWS, D)),
            whole((ROWS, D)),
            whole((ROWS, D)),
            grad,
            grad,
            pl.BlockSpec((1, D), lambda j: (0, last(j))),
            whole((8, D)),
            ANY,
        ],
        out_shape=[
            jax.ShapeDtypeStruct((ROWS, D), f32),
            jax.ShapeDtypeStruct((ROWS, D), f32),
            jax.ShapeDtypeStruct((ROWS, D), bf16),
            jax.ShapeDtypeStruct((D // 2, FF + D), bf16),
            jax.ShapeDtypeStruct((D // 2, FF + D), bf16),
            jax.ShapeDtypeStruct((1, FF), f32),
            jax.ShapeDtypeStruct((8, D), f32),
            jax.ShapeDtypeStruct(passed.shape, passed.dtype),
        ],
        scratch_shapes=[pltpu.VMEM((ROWS, D), f32), pltpu.VMEM((ROWS, D), f32)],
        input_output_aliases={12: 7},
        compiler_params=params(),
        cost_estimate=cost(40),
        name="mlp_down",
    )(m, gp, dz, ht, mlp, mlp, x1, ct, a, ot, mlp, vec, passed, *tokens)


GROUPS = 1
WIDE = D // GROUPS


def back_kernel(group, passed, lens_ref, valid_ref, q_ref, k_ref, v_ref, do_ref, kt_ref, lse_ref, ht_ref, *refs):
    dq_ref, dk_ref, dv_ref, keep_ref, away_ref, sums_ref = refs[-10 - passed :][:6]
    segc, segr, dk_acc, dv_acc = refs[-4:]
    i = pl.program_id(0)

    @pl.when(i == 0)
    def _():
        fill_segments(lens_ref, valid_ref, segc, segr)
        dk_acc[...] = jnp.zeros_like(dk_acc)
        dv_acc[...] = jnp.zeros_like(dv_acc)

    start = block_start(i)
    here = pl.multiple_of(i * BLK, BLK)
    bias = block_bias(segc, segr, i, start)
    masks = lane_masks()
    one = eye()
    window = pl.ds(start, WIN)
    for p in range(PAIRS // GROUPS):
        s = slice(p * BLK, (p + 1) * BLK)
        n = group * (PAIRS // GROUPS) + p
        queries = stack_pair(q_ref[:, s], masks)
        grads = stack_pair(do_ref[:, s], masks)
        probs = jnp.exp(dot_nt(k_ref[window, s], queries) + bias - lse_ref[0, n : n + 1])
        dprobs = dot_nt(v_ref[window, s], grads)
        dv_acc[window, s] += dot_nn(probs.astype(bf16), grads)
        center = col_sum(probs * dprobs)
        dscores = (probs * (dprobs - center)).astype(bf16)
        dk_acc[window, s] += dot_nn(dscores, queries)
        dq = dot_nn(kt_ref[s, window], dscores)
        dq = (jnp.concatenate([dq[:HD, :BLK], dq[HD:, BLK:]], axis=0) * 0.125).astype(bf16)
        dq_ref[pl.ds(here, BLK), s] = flip(one, dq)

    @pl.when(i == NBLK - 1)
    def _():
        dk_ref[...] = dk_acc[...].astype(bf16)
        dv_ref[...] = dv_acc[...].astype(bf16)
        for c, ref in enumerate((dq_ref, dk_ref, dv_ref)):
            s = slice(c * WIDE, (c + 1) * WIDE)
            away_ref[:, s] = dot_nn(ht_ref[D // 2 :], ref[...]).astype(bf16)
            keep_ref[:, s] = dot_nn(ht_ref[: D // 2], ref[...]).astype(bf16)
        dbq = col_sum(dq_ref[...].astype(f32))
        dbv = col_sum(dv_ref[...].astype(f32))
        sums_ref[...] = jnp.concatenate([dbq, dbv, jnp.zeros((6, WIDE), f32)], axis=0)


def back_call(group, lens, valid, q, k, v, do, kt, lse, ht, before=(), passed=(), tokens=()):
    tok = pl.BlockSpec((BLK, WIDE), lambda i: (i, group))
    full = pl.BlockSpec((ROWS, WIDE), lambda i: (0, group))
    extra = list(before) + list(passed) + list(tokens)
    aliases = {9 + n: n for n in range(len(before))}
    aliases.update({9 + len(before) + n: 6 + n for n in range(len(passed))})
    out = pl.pallas_call(
        functools.partial(back_kernel, group, len(passed)),
        grid=(NBLK,),
        in_specs=[
            pl.BlockSpec(memory_space=pltpu.SMEM),
            pl.BlockSpec(memory_space=pltpu.SMEM),
            tok,
            full,
            full,
            tok,
            pl.BlockSpec((WIDE, ROWS), lambda i: (group, 0)),
            pl.BlockSpec((1, 8, 2 * BLK), lambda i: (i, 0, 0)),
            whole((D, ROWS)),
        ]
        + [ANY] * len(extra),
        out_specs=[full] * 3 + [whole((D // 2, 3 * WIDE))] * 2 + [whole((8, WIDE))] + [ANY] * len(passed),
        out_shape=[jax.ShapeDtypeStruct((ROWS, D), bf16)] * 3
        + [jax.ShapeDtypeStruct((D // 2, 3 * WIDE), bf16)] * 2
        + [jax.ShapeDtypeStruct((8, WIDE), f32)]
        + [jax.ShapeDtypeStruct(p.shape, p.dtype) for p in passed],
        scratch_shapes=[
            pltpu.VMEM((ROWS, BLK), jnp.int32),
            pltpu.VMEM((8, ROWS), jnp.int32),
            pltpu.VMEM((ROWS, WIDE), f32),
            pltpu.VMEM((ROWS, WIDE), f32),
        ],
        input_output_aliases=aliases,
        compiler_params=params(),
        cost_estimate=cost(22),
        name="attend_back",
    )(lens, valid, q, k, v, do, kt, lse, ht, *extra)
    return out[:6], out[6:]


def input_kernel(passed, dq_ref, dk_ref, dv_ref, w_ref, turn_ref, x_ref, dx1_ref, vec_ref, *refs):
    dx_ref, sums_ref = refs[len(refs) - 2 - passed :][:2]
    i = pl.program_id(0)
    dh = dot_nt(dq_ref[...], w_ref[:, :D]) + dot_nt(dk_ref[...], w_ref[:, D : 2 * D]) + dot_nt(dv_ref[...], w_ref[:, 2 * D :])
    dh = dot_nt(dh.astype(bf16), turn_ref[...])
    normed, scale = norm_parts(x_ref[...])
    dx_ref[...] = dx1_ref[...] + norm_back(dh, normed, scale, vec_ref[0:1])
    sums = jnp.concatenate([col_sum(dh * normed), col_sum(dh), jnp.zeros((6, D), f32)], axis=0)

    @pl.when(i == 0)
    def _():
        sums_ref[...] = sums

    @pl.when(i > 0)
    def _():
        sums_ref[...] += sums


def input_call(dq, dk, dv, w, turn, x, dx1, vec, passed=(), tokens=()):
    tok = pl.BlockSpec((TILE, D), lambda i: (i, 0))
    extra = list(passed) + list(tokens)
    out = pl.pallas_call(
        functools.partial(input_kernel, len(passed)),
        grid=(ROWS // TILE,),
        in_specs=[tok, tok, tok, whole((D, 3 * D)), whole((D, D)), tok, tok, whole((16, D))] + [ANY] * len(extra),
        out_specs=[tok, whole((8, D))] + [ANY] * len(passed),
        out_shape=[jax.ShapeDtypeStruct((ROWS, D), f32), jax.ShapeDtypeStruct((8, D), f32)]
        + [jax.ShapeDtypeStruct(p.shape, p.dtype) for p in passed],
        input_output_aliases={8 + n: 2 + n for n in range(len(passed))},
        compiler_params=params(),
        cost_estimate=cost(13),
        name="input_back",
    )(dq, dk, dv, w, turn, x, dx1, vec, *extra)
    return out[:2], out[2:]


def swap_cores(x):
    return lax.ppermute(x, "c", [(0, 1), (1, 0)])


def from_peer(x, axes, k):
    return lax.ppermute(x, axes, [(i, i ^ k) for i in range(lax.axis_size(axes))])


def gate_kernel(*refs):
    del refs


def gate(array, tokens):
    return pl.pallas_call(
        gate_kernel,
        in_specs=[ANY] * (1 + len(tokens)),
        out_specs=ANY,
        out_shape=jax.ShapeDtypeStruct(array.shape, array.dtype),
        input_output_aliases={0: 0},
        name="gate",
    )(array, *tokens)


def own_order(rows):
    place = jnp.arange(D, dtype=jnp.int32)
    k, rest = place % rows, place // rows
    na, nb, nf = lax.axis_size("a"), lax.axis_size("b"), lax.axis_size("f")
    a, rest = rest % na ^ lax.axis_index("a"), rest // na
    f, rest = rest % nf ^ lax.axis_index("f"), rest // nf
    b, c = rest % nb ^ lax.axis_index("b"), rest // nb ^ lax.axis_index("c")
    return (((a * nb + b) * nf + f) * 2 + c) * rows + k


def gather_own(shard):
    stack = jnp.concatenate([shard] + [from_peer(shard, "a", k) for k in range(1, lax.axis_size("a"))], axis=0)
    parts = [stack] + [from_peer(stack, ("b", "f"), k) for k in range(1, lax.axis_size(("b", "f")))]
    if stack.shape[0] % 16:
        parts = [jnp.concatenate(parts, axis=0)]
    return parts + [swap_cores(p) for p in parts]


def add(terms):
    total = 0.0
    for array, low, high in terms:
        total = total + array[low:high].astype(f32)
    return total


def plain(arrays):
    return [(g, 0, g.shape[0]) for g in arrays]


def exchange(terms, axes):
    count = lax.axis_size(axes)
    size = (terms[0][2] - terms[0][1]) // count

    def block(k):
        return [(t, low + k * size, low + (k + 1) * size) for t, low, _ in terms]

    return block(0), [from_peer(add(block(k)).astype(bf16), axes, k) for k in range(1, count)]


def hold(terms, array):
    return [(array,) + terms[0][1:]] + terms[1:]


def scatter_own(keep, away):
    terms = plain([keep, swap_cores(away)])
    for axes in (("b", "f"), "a"):
        terms, got = exchange(terms, axes)
        terms = terms + plain(got)
    return add(terms)


def join_owners(mlp, rows):
    group = 1 if rows % 8 == 0 else 8
    if group == 1:
        return mlp
    count = mlp.shape[0] // group
    tall = mlp[:, : 4 * rows].reshape(count, group * 4 * rows, D)
    wide = mlp[:, 4 * rows : 8 * rows].reshape(count, group, 4, rows, D)
    wide = jnp.swapaxes(wide, 1, 2).reshape(count, group * 4 * rows, D)
    proj = mlp[:, 8 * rows :].reshape(count, group * rows, D)
    return jnp.concatenate([tall, wide, proj], axis=1)


def shards(inputs, img_lens, valid_rows, w_qkv, w_proj, w_fc1, b_fc1, w_fc2, vectors, cotangent):
    devices = lax.axis_size(ALL)
    rows = D // devices
    slots = rows * BLK
    small = jnp.concatenate([vectors, b_fc1])
    small = jnp.pad(small, (0, slots - small.shape[0])).reshape(rows, BLK)
    head = jnp.concatenate([w_qkv.reshape(rows, 3 * D), small], axis=1).astype(bf16)
    fc1_shard = jnp.swapaxes(w_fc1.reshape(rows, 4, D), 0, 1).reshape(4 * rows, D)
    mlp = jnp.concatenate([w_fc2.reshape(4 * rows, D), fc1_shard, w_proj.reshape(rows, D)], axis=0).astype(bf16)
    mlp = join_owners(lax.all_gather(mlp, ALL, axis=0), rows)

    order = own_order(rows)
    turn = (jnp.arange(D, dtype=jnp.int32)[:, None] == order[None, :]).astype(bf16)
    parts = gather_own(head)
    small = jnp.concatenate([p[:, 3 * D :] for p in parts], axis=0)
    small = jnp.dot(turn, small, preferred_element_type=f32).reshape(devices, slots)
    nvec = vectors.shape[0]
    vec = jnp.pad(small[:, :nvec].reshape(10, D), ((0, 6), (0, 0)))
    b1 = small[:, nvec : nvec + b_fc1.shape[0]].reshape(1, FF)

    q, k, v, kt, vt, h1t, wqkv = qkv_call(parts, inputs, turn, vec, order)
    o, lse = attn_call(img_lens, valid_rows, q, k, vt)
    x1, a, h2, h2t, ot, dz = proj_call(o, mlp, inputs, cotangent, turn, vec)
    na, nb, nf = lax.axis_size("a"), lax.axis_size("b"), lax.axis_size("f")
    direct = na == STEPS and rows % 8 == 0
    zero = jnp.zeros((), jnp.int32)
    me = jnp.stack(
        [lax.axis_index("a") if direct else zero, lax.axis_index(("b", "f")), lax.axis_index("c")]
    ).astype(jnp.int32)
    m, gp, *dw2 = up_call(me, h2, dz, mlp, b1, direct)
    if direct:
        keep2, away2 = [g.reshape(FF // 2, D) for g in dw2]
    else:
        dw2 = jnp.take(dw2[0].reshape(devices, 4 * rows, D), order[::rows] // rows, axis=0).reshape(FF, D)
        keep2, away2 = dw2[: FF // 2], dw2[FF // 2 :]

    bf = ("b", "f")
    core2 = swap_cores(away2)
    up2, up2_got = exchange(plain([keep2, core2]), bf)
    result, dx1, do, keep, away, db1, sums2, keep2 = down_call(
        m, gp, dz, h2t, mlp, x1, cotangent, a, ot, vec, passed=keep2, tokens=[core2]
    )
    core = swap_cores(gate(away, up2_got))
    up2, up2_last = exchange(hold(up2, keep2) + plain(up2_got), "a")
    mid, mid_got = exchange(plain([keep, core]), bf)

    (dq, dk, dv, keep1, away1, sums_a), (keep, keep2) = back_call(
        0, img_lens, valid_rows, q, k, v, do, kt, lse, h1t, passed=[keep, keep2], tokens=[core]
    )
    core1 = swap_cores(gate(away1, mid_got + up2_last))
    g_fc2 = add(hold(up2, keep2) + plain(up2_last))
    mid, mid_last = exchange(hold(mid, keep) + plain(mid_got), "a")
    second, second_got = exchange(plain([keep1, core1]), bf)

    (d_input, sums0), (keep, keep1) = input_call(
        dq, dk, dv, wqkv, turn, inputs, dx1, vec, passed=[keep, keep1], tokens=[core1]
    )
    sums0 = gate(sums0, second_got + mid_last)
    second, second_last = exchange(hold(second, keep1) + plain(second_got), "a")
    gvec = jnp.concatenate([sums0[:2], sums_a[:2], sums2[:6]], axis=0).reshape(devices, nvec)
    gsmall = jnp.concatenate([gvec, db1.reshape(devices, b_fc1.shape[0])], axis=1)
    gsmall = jnp.pad(gsmall, ((0, 0), (0, -gsmall.shape[1] % BLK))).astype(bf16)
    pick = (order[::rows] // rows)[:, None] == jnp.arange(devices, dtype=jnp.int32)[None, :]
    gsmall = jnp.dot(pick.astype(bf16), gsmall, preferred_element_type=f32).astype(bf16)
    gsmall = scatter_own(gsmall[: devices // 2], gsmall[devices // 2 :]).reshape(-1)

    g_mid = add(hold(mid, keep) + plain(mid_last))
    g_fc1, g_proj = g_mid[:, :FF], g_mid[:, FF:]
    g_qkv = add(second + plain(second_last))
    return (
        result,
        d_input,
        g_qkv.reshape(-1),
        g_proj.reshape(-1),
        g_fc1.reshape(-1),
        gsmall[nvec : nvec + b_fc1.shape[0]],
        g_fc2.reshape(-1),
        gsmall[:nvec],
    )


def solution(mesh):
    dp, fsdp = mesh.shape["dp"], mesh.shape["fsdp"]
    fine = Mesh(mesh.devices.reshape(dp // 2, 2, fsdp // 2, 2), ALL)
    rows, flat = P(ALL, None), P(ALL)
    return jax.shard_map(
        shards,
        mesh=fine,
        in_specs=(rows, rows, flat, flat, flat, flat, flat, flat, flat, rows),
        out_specs=(rows, rows, flat, flat, flat, flat, flat, flat),
        check_vma=False,
    )
```

```python
import functools

import jax
import jax.numpy as jnp
from jax import lax
from jax.experimental import pallas as pl
from jax.experimental.pallas import tpu as pltpu
from jax.sharding import Mesh
from jax.sharding import PartitionSpec as P

HEADS = 12
HD = 64
ROWS = 1024
D = HEADS * HD
FF = 4 * D
PAIRS = HEADS // 2
BLK = 128
QB = 2 * BLK
WIN = QB + 2 * BLK
TILE = 256
EPS = 1e-06
ALL = ("a", "b", "f", "c")
bf16 = jnp.bfloat16
f32 = jnp.float32
VMEM_LIMIT = 60 * 1024 * 1024
ANY = pl.BlockSpec(memory_space=pl.ANY)


def cost(us):
    return pl.CostEstimate(flops=us * 1_100_000_000, bytes_accessed=us * 3_000_000, transcendentals=0)


def dot_nn(left, right):
    return lax.dot_general(left, right, (((1,), (0,)), ((), ())), preferred_element_type=f32)


def dot_nt(left, right):
    return lax.dot_general(left, right, (((1,), (1,)), ((), ())), preferred_element_type=f32)


def dot_tn(left, right):
    return lax.dot_general(left, right, (((0,), (0,)), ((), ())), preferred_element_type=f32)


def eye():
    rows = lax.broadcasted_iota(jnp.int32, (BLK, BLK), 0)
    cols = lax.broadcasted_iota(jnp.int32, (BLK, BLK), 1)
    return (rows == cols).astype(f32).astype(bf16)


def flip(one, block):
    return dot_nt(one, block).astype(bf16)


def norm_parts(values):
    center = values - jnp.mean(values, axis=-1, keepdims=True)
    scale = lax.rsqrt(jnp.mean(center * center, axis=-1, keepdims=True) + EPS)
    return center * scale, scale


def norm_back(grad, normed, scale, gain):
    inner = grad * gain
    first = jnp.mean(inner, axis=-1, keepdims=True)
    second = jnp.mean(inner * normed, axis=-1, keepdims=True)
    return scale * (inner - first - normed * second)


def col_sum(values):
    return jnp.sum(values, axis=0, keepdims=True)


def gelu_parts(u):
    half = 0.5 + 0.5 * lax.erf(u * 0.7071067811865476)
    e = jnp.exp2((u * u) * -0.7213475204444817)
    return u * half, half + (0.3989422804014327 * u) * e


def params(**kw):
    return pltpu.CompilerParams(vmem_limit_bytes=VMEM_LIMIT, **kw)


def whole(shape):
    return pl.BlockSpec(shape, lambda *_: (0,) * len(shape))


def gather_copies(parts, line_me, me_ref, source, target, sems):
    if len(parts) == 1:
        return [pltpu.make_async_copy(source(parts[0], None), target(None), sems.at[0])]
    half, copies = len(parts) // 2, []
    for n, part in enumerate(parts):
        for k in range(part.shape[0]):
            device = ((k ^ line_me) * half + (n % half ^ me_ref[1])) * 2 + (n // half ^ me_ref[2])
            copies.append(pltpu.make_async_copy(source(part, k), target(device), sems.at[n * part.shape[0] + k]))
    return copies


def copy_count(parts):
    return 1 if len(parts) == 1 else len(parts) * parts[0].shape[0]


def fill_segments(lens_ref, valid_ref, segc, segr):
    row_c = lax.broadcasted_iota(jnp.int32, (ROWS, BLK), 0)
    row_r = lax.broadcasted_iota(jnp.int32, (8, ROWS), 1)
    sum_c = jnp.zeros((ROWS, BLK), jnp.int32)
    sum_r = jnp.zeros((8, ROWS), jnp.int32)
    end = jnp.int32(0)
    for j in range(lens_ref.shape[1]):
        end = end + lens_ref[0, j]
        sum_c = sum_c + (row_c >= end).astype(jnp.int32)
        sum_r = sum_r + (row_r >= end).astype(jnp.int32)
    valid = valid_ref[0]
    segc[...] = jnp.where(row_c < valid, sum_c, -1)
    segr[...] = jnp.where(row_r < valid, sum_r, -1)


def block_place(segc, segr, i):
    start = pl.multiple_of(jnp.clip(i * (QB // BLK) - 1, 0, (ROWS - WIN) // BLK) * BLK, BLK)
    here = pl.ds(pl.multiple_of(i * QB, BLK), QB)
    window = pl.ds(start, WIN)
    rows = jnp.concatenate([segc[here, :]] * (WIN // BLK), axis=1)
    bias = jnp.where(rows == segr[0:1, window], 0.0, -1000000000.0).astype(f32)
    return here, window, jnp.concatenate([bias, bias], axis=0)


def lane_masks():
    low = (lax.broadcasted_iota(jnp.int32, (1, BLK), 1) < HD).astype(f32)
    return low.astype(bf16), (1.0 - low).astype(bf16)


def stack_pair(block, masks):
    return jnp.concatenate([block * masks[0], block * masks[1]], axis=0)


def pick_pair(values):
    low = lax.broadcasted_iota(jnp.int32, (1, BLK), 1) < HD
    return jnp.where(low, values[:QB], values[QB:])


def attend_kernel(count, passed, lens_ref, valid_ref, me_ref, *refs):
    parts, (x_ref, turn_ref, vec_ref) = refs[:count], refs[count : count + 3]
    q_ref, k_ref, v_ref, ht_ref, w_out, o_ref, lse_ref = refs[-16 - passed :][:7]
    stage, w_ref, qs, ks, vs, segc, segr, sems, out_sem = refs[-9:]
    i = pl.program_id(0)
    tiles = ROWS // TILE

    def fetch():
        def source(part, k):
            return part if k is None else part.at[k]

        return gather_copies(parts, me_ref[0], me_ref, source, lambda n: stage if n is None else stage.at[n], sems)

    def store():
        return pltpu.make_async_copy(w_ref, w_out, out_sem)

    @pl.when(i == 0)
    def _():
        for copy in fetch():
            copy.start()
        fill_segments(lens_ref, valid_ref, segc, segr)
        for copy in fetch():
            copy.wait()
        w_ref[...] = stage[...].astype(f32).reshape(D, 3 * D).astype(bf16)
        store().start()

    @pl.when(i < tiles)
    def _():
        rows = pl.ds(pl.multiple_of(i * TILE, TILE), TILE)
        normed, _ = norm_parts(x_ref[...])
        low = (normed * vec_ref[0:1] + vec_ref[1:2]).astype(bf16)
        q = ((dot_nn(low, w_ref[:, :D]) + vec_ref[2:3]).astype(bf16).astype(f32) * 0.125).astype(bf16)
        k = dot_nn(low, w_ref[:, D : 2 * D]).astype(bf16)
        v = (dot_nn(low, w_ref[:, 2 * D :]) + vec_ref[3:4]).astype(bf16)
        for value, ref, scratch in ((q, q_ref, qs), (k, k_ref, ks), (v, v_ref, vs)):
            ref[...] = value
            scratch[rows] = value
        turned = dot_nn(low, turn_ref[...]).astype(bf16)
        one = eye()
        for p in range(PAIRS):
            s = slice(p * BLK, (p + 1) * BLK)
            ht_ref[s] = flip(one, turned[:, s])

    @pl.when(i >= tiles)
    def _():
        here, window, bias = block_place(segc, segr, i - tiles)
        masks = lane_masks()
        for p in range(PAIRS):
            s = slice(p * BLK, (p + 1) * BLK)
            scores = dot_nt(stack_pair(qs[here, s], masks), ks[window, s]) + bias
            peak = jnp.max(scores, axis=1, keepdims=True)
            expo = jnp.exp(scores - peak)
            total = jnp.sum(expo, axis=1, keepdims=True)
            o_ref[:, s] = pick_pair(dot_nn(expo.astype(bf16), vs[window, s]) * (1.0 / total)).astype(bf16)
            lse_ref[0, :, p : p + 1] = peak + jnp.log(total)

    @pl.when(i == tiles + ROWS // QB - 1)
    def _():
        store().wait()


def attend_call(lens, valid, me, parts, x, turn, vec, passed=(), tokens=()):
    tiles = ROWS // TILE

    def first(i):
        return jnp.minimum(i, tiles - 1)

    def second(i):
        return jnp.maximum(i - tiles, 0)

    tok = pl.BlockSpec((TILE, D), lambda i: (first(i), 0))
    smem = pl.BlockSpec(memory_space=pltpu.SMEM)
    count, rows = len(parts), parts[0].shape[1]
    extra = list(passed) + list(tokens)
    out = pl.pallas_call(
        functools.partial(attend_kernel, count, len(passed)),
        grid=(tiles + ROWS // QB,),
        in_specs=[smem] * 3 + [ANY] * count + [tok, whole((D, D)), whole((16, D))] + [ANY] * len(extra),
        out_specs=[
            tok,
            tok,
            tok,
            pl.BlockSpec((D, TILE), lambda i: (0, first(i))),
            ANY,
            pl.BlockSpec((QB, D), lambda i: (second(i), 0)),
            pl.BlockSpec((1, 2 * QB, BLK), lambda i: (second(i), 0, 0)),
        ]
        + [ANY] * len(passed),
        out_shape=[jax.ShapeDtypeStruct((ROWS, D), bf16)] * 3
        + [
            jax.ShapeDtypeStruct((D, ROWS), bf16),
            jax.ShapeDtypeStruct((D, 3 * D), bf16),
            jax.ShapeDtypeStruct((ROWS, D), bf16),
            jax.ShapeDtypeStruct((ROWS // QB, 2 * QB, BLK), f32),
        ]
        + [jax.ShapeDtypeStruct(p.shape, p.dtype) for p in passed],
        scratch_shapes=[
            pltpu.VMEM((D // rows, rows, 3 * D), bf16),
            pltpu.VMEM((D, 3 * D), bf16),
            pltpu.VMEM((ROWS, D), bf16),
            pltpu.VMEM((ROWS, D), bf16),
            pltpu.VMEM((ROWS, D), bf16),
            pltpu.VMEM((ROWS, BLK), jnp.int32),
            pltpu.VMEM((8, ROWS), jnp.int32),
            pltpu.SemaphoreType.DMA((copy_count(parts),)),
            pltpu.SemaphoreType.DMA,
        ],
        input_output_aliases={6 + count + n: 7 + n for n in range(len(passed))},
        compiler_params=params(),
        cost_estimate=cost(25),
        name="attend",
    )(lens, valid, me, *parts, x, turn, vec, *extra)
    return out[:7], out[7:]


STEPS = FF // D


def up_kernel(count, me_ref, o_ref, x_ref, ct_ref, turn_ref, vec_ref, b_ref, *refs):
    parts = refs[:count]
    h, dzs, stage, wp, dw_ref, p_sems, w_sems, out_sem = refs[-8:]
    grads = 2 if count > 1 else 1
    outs = refs[-17 - grads : -8]
    x1_ref, a_ref, ht_ref, ot_ref, dz_ref, wp_out, w_ref, m_ref, gp_ref, *grad_refs = outs
    i = pl.program_id(0)
    tiles = ROWS // TILE

    def fetch(first):
        block = pl.ds(4, 1) if first else pl.ds(0, 4)

        def source(part, k):
            return part.at[block] if k is None else part.at[k, block]

        def target(n):
            return stage.at[block] if n is None else stage.at[block, n]

        return gather_copies(parts, 0, me_ref, source, target, p_sems if first else w_sems)

    def store():
        return pltpu.make_async_copy(wp, wp_out, out_sem)

    @pl.when(i == 0)
    def _():
        for copy in fetch(True):
            copy.start()
        for copy in fetch(False):
            copy.start()
        for copy in fetch(True):
            copy.wait()
        wp[...] = stage[4].astype(f32).reshape(D, D).astype(bf16)
        store().start()

    @pl.when(i < tiles)
    def _():
        rows = pl.ds(pl.multiple_of(i * TILE, TILE), TILE)
        branch = dot_nn(o_ref[...], wp[...]) + vec_ref[4:5]
        inner = x_ref[...] + vec_ref[5:6] * branch
        x1_ref[...] = inner
        a_ref[...] = branch.astype(bf16)
        normed, _ = norm_parts(inner)
        low = (normed * vec_ref[6:7] + vec_ref[7:8]).astype(bf16)
        h[rows] = low
        dz = (vec_ref[9:10] * ct_ref[...]).astype(bf16)
        dz_ref[...] = dz
        dzs[rows] = dz
        one = eye()
        turned = dot_nn(low, turn_ref[...]).astype(bf16)
        turned_o = dot_nn(o_ref[...], turn_ref[...]).astype(bf16)
        for p in range(PAIRS):
            s = slice(p * BLK, (p + 1) * BLK)
            ht_ref[s] = flip(one, turned[:, s])
            ot_ref[s] = flip(one, turned_o[:, s])

    @pl.when(i == tiles)
    def _():
        for copy in fetch(False):
            copy.wait()
        store().wait()

    @pl.when(i >= tiles)
    def _():
        chunk = (i - tiles) ^ (me_ref[0] if count > 1 else 0)
        w_ref[0] = stage[chunk].astype(f32).reshape(D, D).astype(bf16)
        for n in range(D // TILE):
            c = slice(n * TILE, (n + 1) * TILE)
            for t in range(tiles):
                r = slice(t * TILE, (t + 1) * TILE)
                m, gp = gelu_parts(dot_nn(h[r], w_ref[0, :, c]) + b_ref[:, c])
                m_ref[r, c] = m.astype(bf16)
                gp_ref[r, c] = gp.astype(bf16)
        for n in range(D // TILE):
            c = slice(n * TILE, (n + 1) * TILE)
            dw_ref[c] = dot_tn(m_ref[:, c], dzs[...])
        if grads == 1:
            grad_refs[0][...] = dw_ref[...].astype(bf16)
        else:
            blocks, _, size, _ = grad_refs[0].shape
            for k in range(blocks):
                for c, ref in enumerate(grad_refs):
                    row = ((k ^ me_ref[1]) * 2 + (c ^ me_ref[2])) * size
                    ref[k, 0] = dw_ref[pl.ds(pl.multiple_of(row, 8), size), :].astype(bf16)


def up_call(me, o, x, ct, turn, vec, b, parts, tokens=()):
    count = len(parts)
    tiles = ROWS // TILE
    _, n, r, _ = (1,) + parts[0].shape[1:] if count == 1 else (1, D // parts[0].shape[2], parts[0].shape[2], D)

    def first(i):
        return jnp.minimum(i, tiles - 1)

    def chunk(i, me):
        return jnp.maximum(i - tiles, 0) ^ (me[0] if count > 1 else 0)

    tok = pl.BlockSpec((TILE, D), lambda i, me: (first(i), 0))
    feat = pl.BlockSpec((D, TILE), lambda i, me: (0, first(i)))
    part = pl.BlockSpec((ROWS, D), lambda i, me: (0, chunk(i, me)))
    if count > 1:
        blocks = count // 2
        spec = pl.BlockSpec((blocks, 1, 4 * r, D), lambda i, me: (0, jnp.maximum(i - tiles, 0), 0, 0))
        grad_specs, grad_shapes = [spec] * 2, [jax.ShapeDtypeStruct((blocks, STEPS, 4 * r, D), bf16)] * 2
    else:
        grad_specs = [pl.BlockSpec((D, D), lambda i, me: (chunk(i, me), 0))]
        grad_shapes = [jax.ShapeDtypeStruct((FF, D), bf16)]
    return pl.pallas_call(
        functools.partial(up_kernel, count),
        grid_spec=pltpu.PrefetchScalarGridSpec(
            num_scalar_prefetch=1,
            grid=(tiles + STEPS,),
            in_specs=[tok, tok, tok, whole((D, D)), whole((16, D)), pl.BlockSpec((1, D), lambda i, me: (0, chunk(i, me)))]
            + [ANY] * (count + len(tokens)),
            out_specs=[
                tok,
                tok,
                feat,
                feat,
                tok,
                ANY,
                pl.BlockSpec((1, D, D), lambda i, me: (chunk(i, me), 0, 0)),
                part,
                part,
            ]
            + grad_specs,
            scratch_shapes=[
                pltpu.VMEM((ROWS, D), bf16),
                pltpu.VMEM((ROWS, D), bf16),
                pltpu.VMEM((5, n, r, D), bf16),
                pltpu.VMEM((D, D), bf16),
                pltpu.VMEM((D, D), f32),
                pltpu.SemaphoreType.DMA((copy_count(parts),)),
                pltpu.SemaphoreType.DMA((copy_count(parts),)),
                pltpu.SemaphoreType.DMA,
            ],
        ),
        out_shape=[
            jax.ShapeDtypeStruct((ROWS, D), f32),
            jax.ShapeDtypeStruct((ROWS, D), bf16),
            jax.ShapeDtypeStruct((D, ROWS), bf16),
            jax.ShapeDtypeStruct((D, ROWS), bf16),
            jax.ShapeDtypeStruct((ROWS, D), bf16),
            jax.ShapeDtypeStruct((D, D), bf16),
            jax.ShapeDtypeStruct((STEPS, D, D), bf16),
            jax.ShapeDtypeStruct((ROWS, FF), bf16),
            jax.ShapeDtypeStruct((ROWS, FF), bf16),
        ]
        + grad_shapes,
        compiler_params=params(),
        cost_estimate=cost(26),
        name="mlp_up",
    )(me, o, x, ct, turn, vec, b, *parts, *tokens)


def down_kernel(
    count, me_ref, m_ref, gp_ref, dz_ref, ht_ref, w1_ref, x1_ref, ct_ref, a_ref, ot_ref, wp_ref, dzt_ref, vec_ref, *refs
):
    parts = refs[:count]
    out_ref, dx_ref, do_ref, keep_ref, away_ref, db1_ref, sums_ref, _, z_acc, dh_acc, dwp_acc, w2_ref, sems = refs[-13:]
    j = pl.program_id(0)

    def fetch(step):
        if count == 1:
            return [pltpu.make_async_copy(parts[0].at[step], w2_ref.at[step], sems.at[step, 0])]
        half, copies = count // 2, []
        for n, part in enumerate(parts):
            place = (n % half ^ me_ref[1]) * 2 + (n // half ^ me_ref[2])
            copies.append(pltpu.make_async_copy(part.at[step], w2_ref.at[step, place], sems.at[step, n]))
        return copies

    @pl.when(j == 0)
    def _():
        for step in range(STEPS):
            for copy in fetch(step):
                copy.start()
        z_acc[...] = jnp.zeros_like(z_acc)
        dh_acc[...] = jnp.zeros_like(dh_acc)
        dwp_acc[...] = jnp.zeros_like(dwp_acc)
        sums_ref[...] = jnp.zeros_like(sums_ref)

    @pl.when(j < STEPS)
    def _():
        for copy in fetch(j):
            copy.wait()
        w1 = w1_ref[0]
        w2 = w2_ref[j].reshape(D, D)
        du = (dot_nt(dz_ref[...], w2) * gp_ref[...].astype(f32)).astype(bf16)
        db1_ref[...] = col_sum(du.astype(f32))
        keep_ref[...] = dot_nn(ht_ref[: D // 2], du).astype(bf16)
        away_ref[...] = dot_nn(ht_ref[D // 2 :], du).astype(bf16)
        z_acc[...] += dot_nn(m_ref[...], w2)
        dh_acc[...] += dot_nt(du, w1)

    @pl.when(j >= STEPS)
    def _():
        r = pl.ds(pl.multiple_of((j - STEPS) * TILE, TILE), TILE)
        inner, ct, branch = x1_ref[...], ct_ref[...], z_acc[r] + vec_ref[8:9]
        out_ref[...] = inner + vec_ref[9:10] * branch
        normed, scale = norm_parts(inner)
        dh = dh_acc[r]
        dx = ct + norm_back(dh, normed, scale, vec_ref[6:7])
        dx_ref[...] = dx
        da = (vec_ref[5:6] * dx).astype(bf16)
        do_ref[...] = dot_nt(da, wp_ref[...]).astype(bf16)
        dwp_acc[...] += dot_nn(ot_ref[...], da)
        adds = (da.astype(f32), dx * a_ref[...].astype(f32), dh * normed, dh, dzt_ref[...].astype(f32), ct * branch)
        sums_ref[...] += jnp.concatenate([col_sum(v) for v in adds] + [jnp.zeros((2, D), f32)], axis=0)

    @pl.when(j == STEPS + ROWS // TILE - 1)
    def _():
        keep_ref[...] = dwp_acc[: D // 2].astype(bf16)
        away_ref[...] = dwp_acc[D // 2 :].astype(bf16)


def down_call(me, m, gp, dz, ht, w1, parts, x1, ct, a, ot, wp, vec, passed, tokens):
    count = len(parts)
    size = parts[0].shape[-2]

    def last(j):
        return jnp.minimum(j, STEPS - 1)

    def row(j):
        return jnp.maximum(j - STEPS, 0)

    part = pl.BlockSpec((ROWS, D), lambda j: (0, last(j)))
    grad = pl.BlockSpec((D // 2, D), lambda j: (0, jnp.minimum(j, STEPS)))
    tile = pl.BlockSpec((TILE, D), lambda j: (row(j), 0))
    return pl.pallas_call(
        functools.partial(down_kernel, count),
        grid=(STEPS + ROWS // TILE,),
        in_specs=[
            pl.BlockSpec(memory_space=pltpu.SMEM),
            part,
            part,
            whole((ROWS, D)),
            whole((D, ROWS)),
            pl.BlockSpec((1, D, D), lambda j: (last(j), 0, 0)),
            tile,
            tile,
            tile,
            pl.BlockSpec((D, TILE), lambda j: (0, row(j))),
            whole((D, D)),
            tile,
            whole((16, D)),
        ]
        + [ANY] * (count + 1 + len(tokens)),
        out_specs=[
            tile,
            tile,
            tile,
            grad,
            grad,
            pl.BlockSpec((1, D), lambda j: (0, last(j))),
            whole((8, D)),
            ANY,
        ],
        out_shape=[
            jax.ShapeDtypeStruct((ROWS, D), f32),
            jax.ShapeDtypeStruct((ROWS, D), f32),
            jax.ShapeDtypeStruct((ROWS, D), bf16),
            jax.ShapeDtypeStruct((D // 2, FF + D), bf16),
            jax.ShapeDtypeStruct((D // 2, FF + D), bf16),
            jax.ShapeDtypeStruct((1, FF), f32),
            jax.ShapeDtypeStruct((8, D), f32),
            jax.ShapeDtypeStruct(passed.shape, passed.dtype),
        ],
        scratch_shapes=[
            pltpu.VMEM((ROWS, D), f32),
            pltpu.VMEM((ROWS, D), f32),
            pltpu.VMEM((D, D), f32),
            pltpu.VMEM((STEPS, D // size, size, D), bf16),
            pltpu.SemaphoreType.DMA((STEPS, count)),
        ],
        input_output_aliases={13 + count: 7},
        compiler_params=params(),
        cost_estimate=cost(35),
        name="mlp_down",
    )(me, m, gp, dz, ht, w1, x1, ct, a, ot, wp, dz, vec, *parts, passed, *tokens)


def back_kernel(passed, lens_ref, valid_ref, q_ref, k_ref, v_ref, do_ref, o_ref, lse_ref, ht_hbm, *refs):
    dq_out, dk_out, dv_out, keep_ref, away_ref, sums_ref = refs[-16 - passed :][:6]
    segc, segr, dk_acc, dv_acc, dq_ref, dk_ref, dv_ref, ht_ref, sems, ht_sem = refs[-10:]
    i = pl.program_id(0)
    steps = ROWS // QB

    def fetch():
        return pltpu.make_async_copy(ht_hbm, ht_ref, ht_sem)

    def store(n):
        return pltpu.make_async_copy((dq_ref, dk_ref, dv_ref)[n], (dq_out, dk_out, dv_out)[n], sems.at[n])

    @pl.when(i == 0)
    def _():
        fetch().start()
        fill_segments(lens_ref, valid_ref, segc, segr)
        dk_acc[...] = jnp.zeros_like(dk_acc)
        dv_acc[...] = jnp.zeros_like(dv_acc)

    @pl.when(i < steps)
    def _():
        here, window, bias = block_place(segc, segr, i)
        masks = lane_masks()
        for p in range(PAIRS):
            s = slice(p * BLK, (p + 1) * BLK)
            queries = stack_pair(q_ref[:, s], masks)
            grads = stack_pair(do_ref[:, s], masks)
            o = o_ref[:, s].astype(f32)
            center = jnp.sum(grads.astype(f32) * jnp.concatenate([o, o], axis=0), axis=1, keepdims=True)
            probs = jnp.exp(dot_nt(queries, k_ref[window, s]) + bias - lse_ref[0, :, p : p + 1])
            dscores = (probs * (dot_nt(grads, v_ref[window, s]) - center)).astype(bf16)
            dv_acc[window, s] += dot_tn(probs.astype(bf16), grads)
            dk_acc[window, s] += dot_tn(dscores, queries)
            dq_ref[here, s] = (pick_pair(dot_nn(dscores, k_ref[window, s])) * 0.125).astype(bf16)

    def weights(ref):
        away_ref[...] = dot_nn(ht_ref[D // 2 :], ref[...]).astype(bf16)
        keep_ref[...] = dot_nn(ht_ref[: D // 2], ref[...]).astype(bf16)

    @pl.when(i == steps)
    def _():
        dk_ref[...] = dk_acc[...].astype(bf16)
        dv_ref[...] = dv_acc[...].astype(bf16)
        for n in range(3):
            store(n).start()
        fetch().wait()
        weights(dq_ref)
        dbq = col_sum(dq_ref[...].astype(f32))
        dbv = col_sum(dv_ref[...].astype(f32))
        sums_ref[...] = jnp.concatenate([dbq, dbv, jnp.zeros((6, D), f32)], axis=0)

    @pl.when(i == steps + 1)
    def _():
        weights(dk_ref)

    @pl.when(i == steps + 2)
    def _():
        weights(dv_ref)
        for n in range(3):
            store(n).wait()


def back_call(lens, valid, q, k, v, do, o, lse, ht, passed=(), tokens=()):
    steps = ROWS // QB

    def last(i):
        return jnp.minimum(i, steps - 1)

    tok = pl.BlockSpec((QB, D), lambda i: (last(i), 0))
    full = whole((ROWS, D))
    grad = pl.BlockSpec((D // 2, D), lambda i: (0, jnp.maximum(i - steps, 0)))
    extra = list(passed) + list(tokens)
    out = pl.pallas_call(
        functools.partial(back_kernel, len(passed)),
        grid=(steps + 3,),
        in_specs=[
            pl.BlockSpec(memory_space=pltpu.SMEM),
            pl.BlockSpec(memory_space=pltpu.SMEM),
            tok,
            full,
            full,
            tok,
            tok,
            pl.BlockSpec((1, 2 * QB, BLK), lambda i: (last(i), 0, 0)),
            ANY,
        ]
        + [ANY] * len(extra),
        out_specs=[ANY] * 3 + [grad, grad, whole((8, D))] + [ANY] * len(passed),
        out_shape=[jax.ShapeDtypeStruct((ROWS, D), bf16)] * 3
        + [jax.ShapeDtypeStruct((D // 2, 3 * D), bf16)] * 2
        + [jax.ShapeDtypeStruct((8, D), f32)]
        + [jax.ShapeDtypeStruct(p.shape, p.dtype) for p in passed],
        scratch_shapes=[
            pltpu.VMEM((ROWS, BLK), jnp.int32),
            pltpu.VMEM((8, ROWS), jnp.int32),
            pltpu.VMEM((ROWS, D), f32),
            pltpu.VMEM((ROWS, D), f32),
            pltpu.VMEM((ROWS, D), bf16),
            pltpu.VMEM((ROWS, D), bf16),
            pltpu.VMEM((ROWS, D), bf16),
            pltpu.VMEM((D, ROWS), bf16),
            pltpu.SemaphoreType.DMA((3,)),
            pltpu.SemaphoreType.DMA,
        ],
        input_output_aliases={9 + n: 6 + n for n in range(len(passed))},
        compiler_params=params(),
        cost_estimate=cost(33),
        name="attend_back",
    )(lens, valid, q, k, v, do, o, lse, ht, *extra)
    return out[:6], out[6:]


def input_kernel(passed, dq_ref, dk_ref, dv_ref, w_ref, x_ref, dx1_ref, vec_ref, *refs):
    dx_ref, sums_ref = refs[len(refs) - 2 - passed :][:2]
    i = pl.program_id(0)
    dh = dot_nt(dq_ref[...], w_ref[:, :D]) + dot_nt(dk_ref[...], w_ref[:, D : 2 * D]) + dot_nt(dv_ref[...], w_ref[:, 2 * D :])
    normed, scale = norm_parts(x_ref[...])
    dx_ref[...] = dx1_ref[...] + norm_back(dh, normed, scale, vec_ref[0:1])
    sums = jnp.concatenate([col_sum(dh * normed), col_sum(dh), jnp.zeros((6, D), f32)], axis=0)

    @pl.when(i == 0)
    def _():
        sums_ref[...] = sums

    @pl.when(i > 0)
    def _():
        sums_ref[...] += sums


def input_call(dq, dk, dv, w, x, dx1, vec, passed=(), tokens=()):
    tok = pl.BlockSpec((TILE, D), lambda i: (i, 0))
    extra = list(passed) + list(tokens)
    out = pl.pallas_call(
        functools.partial(input_kernel, len(passed)),
        grid=(ROWS // TILE,),
        in_specs=[tok, tok, tok, whole((D, 3 * D)), tok, tok, whole((16, D))] + [ANY] * len(extra),
        out_specs=[tok, whole((8, D))] + [ANY] * len(passed),
        out_shape=[jax.ShapeDtypeStruct((ROWS, D), f32), jax.ShapeDtypeStruct((8, D), f32)]
        + [jax.ShapeDtypeStruct(p.shape, p.dtype) for p in passed],
        input_output_aliases={7 + n: 2 + n for n in range(len(passed))},
        compiler_params=params(),
        cost_estimate=cost(13),
        name="input_back",
    )(dq, dk, dv, w, x, dx1, vec, *extra)
    return out[:2], out[2:]


def swap_cores(x):
    return lax.ppermute(x, "c", [(0, 1), (1, 0)])


def from_peer(x, axes, k):
    return lax.ppermute(x, axes, [(i, i ^ k) for i in range(lax.axis_size(axes))])


def gate_kernel(*refs):
    del refs


def gate(arrays, tokens):
    out = pl.pallas_call(
        gate_kernel,
        in_specs=[ANY] * (len(arrays) + len(tokens)),
        out_specs=[ANY] * len(arrays),
        out_shape=[jax.ShapeDtypeStruct(a.shape, a.dtype) for a in arrays],
        input_output_aliases={n: n for n in range(len(arrays))},
        name="gate",
    )(*arrays, *tokens)
    return list(out)


def own_order(rows):
    place = jnp.arange(D, dtype=jnp.int32)
    k, rest = place % rows, place // rows
    na, nb, nf = lax.axis_size("a"), lax.axis_size("b"), lax.axis_size("f")
    a, rest = rest % na ^ lax.axis_index("a"), rest // na
    f, rest = rest % nf ^ lax.axis_index("f"), rest // nf
    b, c = rest % nb ^ lax.axis_index("b"), rest // nb ^ lax.axis_index("c")
    return (((a * nb + b) * nf + f) * 2 + c) * rows + k


def line(shard):
    return [shard] + [from_peer(shard, "a", k) for k in range(1, lax.axis_size("a"))]


def spread(shard, axis):
    return lax.all_to_all(jnp.broadcast_to(shard[None], (lax.axis_size(axis),) + shard.shape), axis, 0, 0)


def gather_plane(stack):
    return [stack] + [from_peer(stack, ("b", "f"), k) for k in range(1, lax.axis_size(("b", "f")))]


def by_owner(parts, order, natural_line=False):
    if natural_line:
        index = jnp.arange(lax.axis_size("a")) ^ lax.axis_index("a")
        parts = [jnp.take(p, index, axis=0) for p in parts]
    return jnp.take(jnp.concatenate(parts, axis=0), jnp.argsort(order), axis=0)


def add(terms):
    total = 0.0
    for array, low, high in terms:
        total = total + array[low:high].astype(f32)
    return total


def plain(arrays):
    return [(g, 0, g.shape[0]) for g in arrays]


def exchange(terms, axes):
    count = lax.axis_size(axes)
    size = (terms[0][2] - terms[0][1]) // count

    def block(k):
        return [(t, low + k * size, low + (k + 1) * size) for t, low, _ in terms]

    return block(0), [from_peer(add(block(k)).astype(bf16), axes, k) for k in range(1, count)]


def hold(terms, array):
    return [(array,) + terms[0][1:]] + terms[1:]


def shards(inputs, img_lens, valid_rows, w_qkv, w_proj, w_fc1, b_fc1, w_fc2, vectors, cotangent):
    devices = lax.axis_size(ALL)
    rows = D // devices
    slots = rows * BLK
    na, nb, nf = lax.axis_size("a"), lax.axis_size("b"), lax.axis_size("f")
    direct = na == STEPS and rows % 8 == 0
    me = jnp.stack([lax.axis_index("a"), lax.axis_index(("b", "f")), lax.axis_index("c")]).astype(jnp.int32)
    small = jnp.concatenate([vectors, b_fc1])
    small = jnp.pad(small, (0, slots - small.shape[0])).reshape(rows, BLK)
    head = jnp.concatenate([w_qkv.reshape(rows, 3 * D), small], axis=1).astype(bf16)
    wide = [w_fc1.reshape(rows, 4, D), w_proj.reshape(rows, 1, D)]
    wide = jnp.concatenate([jnp.swapaxes(t.astype(bf16), 0, 1) for t in wide], axis=0)
    tall = w_fc2.reshape(4 * rows, D).astype(bf16)

    order = own_order(rows)
    owners = order[::rows] // rows
    turn = (jnp.arange(D, dtype=jnp.int32)[:, None] == order[None, :]).astype(bf16)
    head = line(head)
    small = gather_plane(jnp.stack([t[:, 3 * D :] for t in head]))
    head = jnp.stack([t[:, : 3 * D] for t in head])
    head_parts = gather_plane(head)
    (wide,) = gate([wide], small[1:2])
    wide = spread(wide, "a")
    (tall,) = gate([tall], [wide])
    tall = spread(tall, "a")
    small = jnp.concatenate(small, axis=0).reshape(-1, BLK)
    small = jnp.concatenate([small, swap_cores(small)], axis=0)
    small = jnp.dot(turn, small, preferred_element_type=f32).reshape(devices, slots)
    nvec = vectors.shape[0]
    vec = jnp.pad(small[:, :nvec].reshape(10, D), ((0, 6), (0, 0)))
    b1 = small[:, nvec : nvec + b_fc1.shape[0]].reshape(1, FF)
    (wide,) = gate([wide], head_parts[1:])
    wide_parts = gather_plane(wide)
    head_parts = head_parts + [swap_cores(p) for p in head_parts]
    if not direct:
        head_parts = [by_owner(head_parts, owners).reshape(-1, D // 32, 3 * D)]
    (q, k, v, h1t, wqkv, o, lse), _ = attend_call(img_lens, valid_rows, me, head_parts, inputs, turn, vec)
    *wide_parts, tall = gate(wide_parts + [tall], [o])
    tall_parts = gather_plane(tall)
    wide_parts = wide_parts + [swap_cores(p) for p in wide_parts]
    if not direct:
        wide_parts = [jnp.swapaxes(by_owner(wide_parts, owners, True), 0, 1).reshape(5, 32, D // 32, D)]
    x1, a, h2t, ot, dz, wp, w1, m, gp, *dw2 = up_call(me, o, inputs, cotangent, turn, vec, b1, wide_parts)
    if direct:
        keep2, away2 = [g.reshape(FF // 2, D) for g in dw2]
    else:
        dw2 = jnp.take(dw2[0].reshape(devices, 4 * rows, D), owners, axis=0).reshape(FF, D)
        keep2, away2 = dw2[: FF // 2], dw2[FF // 2 :]
    tall_parts = tall_parts + [swap_cores(p) for p in tall_parts]
    if not direct:
        tall_parts = [by_owner(tall_parts, owners, True).reshape(STEPS, 8, D // 8, D)]

    bf = ("b", "f")
    core2 = swap_cores(gate([away2], tall_parts[1 : len(tall_parts) // 2])[0])
    up2, up2_got = exchange(plain([keep2, core2]), bf)
    result, dx1, do, keep, away, db1, sums2, keep2 = down_call(
        me, m, gp, dz, h2t, w1, tall_parts, x1, cotangent, a, ot, wp, vec, passed=keep2, tokens=[core2]
    )
    core = swap_cores(gate([away], up2_got)[0])
    up2, up2_last = exchange(hold(up2, keep2) + plain(up2_got), "a")
    mid, mid_got = exchange(plain([keep, core]), bf)

    (dq, dk, dv, keep1, away1, sums_a), (keep, keep2) = back_call(
        img_lens, valid_rows, q, k, v, do, o, lse, h1t, passed=[keep, keep2], tokens=[core]
    )
    core1 = swap_cores(gate([away1], mid_got + up2_last)[0])
    mid, mid_last = exchange(hold(mid, keep) + plain(mid_got), "a")
    second, second_got = exchange(plain([keep1, core1]), bf)

    (d_input, sums0), (keep, keep1, keep2) = input_call(
        dq, dk, dv, wqkv, inputs, dx1, vec, passed=[keep, keep1, keep2], tokens=[core1]
    )
    g_fc2 = add(hold(up2, keep2) + plain(up2_last))
    sums0, sums_a, sums2, db1 = gate([sums0, sums_a, sums2, db1], second_got + mid_last)
    second, second_last = exchange(hold(second, keep1) + plain(second_got), "a")
    gvec = jnp.concatenate([sums0[:2], sums_a[:2], sums2[:6]], axis=0).reshape(devices, nvec)
    gsmall = jnp.concatenate([gvec, db1.reshape(devices, b_fc1.shape[0])], axis=1)
    gsmall = jnp.pad(gsmall, ((0, 0), (0, -gsmall.shape[1] % BLK))).astype(bf16)
    gsmall = lax.all_to_all(gsmall.reshape(devices, 1, -1), ALL, 0, 0)
    gsmall = jnp.sum(gsmall.astype(f32), axis=0).reshape(-1)

    g_mid = add(hold(mid, keep) + plain(mid_last))
    g_fc1, g_proj = g_mid[:, :FF], g_mid[:, FF:]
    g_qkv = add(second + plain(second_last))
    return (
        result,
        d_input,
        g_qkv.reshape(-1),
        g_proj.reshape(-1),
        g_fc1.reshape(-1),
        gsmall[nvec : nvec + b_fc1.shape[0]],
        g_fc2.reshape(-1),
        gsmall[:nvec],
    )


def solution(mesh):
    dp, fsdp = mesh.shape["dp"], mesh.shape["fsdp"]
    fine = Mesh(mesh.devices.reshape(dp // 2, 2, fsdp // 2, 2), ALL)
    rows, flat = P(ALL, None), P(ALL)
    return jax.shard_map(
        shards,
        mesh=fine,
        in_specs=(rows, rows, flat, flat, flat, flat, flat, flat, flat, rows),
        out_specs=(rows, rows, flat, flat, flat, flat, flat, flat),
        check_vma=False,
    )
```

```python
import functools

import jax
import jax.numpy as jnp
from jax import lax
from jax.experimental import pallas as pl
from jax.experimental.pallas import tpu as pltpu
from jax.sharding import Mesh
from jax.sharding import PartitionSpec as P

HEADS = 12
HD = 64
ROWS = 1024
D = HEADS * HD
FF = 4 * D
PAIRS = HEADS // 2
BLK = 128
QB = 2 * BLK
WIN = QB + 2 * BLK
TILE = 256
EPS = 1e-06
ALL = ("a", "b", "f", "c")
bf16 = jnp.bfloat16
f32 = jnp.float32
VMEM_LIMIT = 60 * 1024 * 1024
ANY = pl.BlockSpec(memory_space=pl.ANY)


def cost(us):
    return pl.CostEstimate(flops=us * 1_100_000_000, bytes_accessed=us * 3_000_000, transcendentals=0)


def dot_nn(left, right):
    return lax.dot_general(left, right, (((1,), (0,)), ((), ())), preferred_element_type=f32)


def dot_nt(left, right):
    return lax.dot_general(left, right, (((1,), (1,)), ((), ())), preferred_element_type=f32)


def dot_tn(left, right):
    return lax.dot_general(left, right, (((0,), (0,)), ((), ())), preferred_element_type=f32)


def norm_parts(values):
    center = values - jnp.mean(values, axis=-1, keepdims=True)
    scale = lax.rsqrt(jnp.mean(center * center, axis=-1, keepdims=True) + EPS)
    return center * scale, scale


def norm_back(grad, normed, scale, gain):
    inner = grad * gain
    first = jnp.mean(inner, axis=-1, keepdims=True)
    second = jnp.mean(inner * normed, axis=-1, keepdims=True)
    return scale * (inner - first - normed * second)


def col_sum(values):
    return jnp.sum(values, axis=0, keepdims=True)


def gelu_parts(u):
    half = 0.5 + 0.5 * lax.erf(u * 0.7071067811865476)
    e = jnp.exp2((u * u) * -0.7213475204444817)
    return u * half, half + (0.3989422804014327 * u) * e


def params(**kw):
    return pltpu.CompilerParams(vmem_limit_bytes=VMEM_LIMIT, **kw)


def whole(shape):
    return pl.BlockSpec(shape, lambda *_: (0,) * len(shape))


def gather_copies(parts, line_me, me_ref, source, target, sems):
    if len(parts) == 1:
        return [pltpu.make_async_copy(source(parts[0], None), target(None), sems.at[0])]
    half, copies = len(parts) // 2, []
    for n, part in enumerate(parts):
        for k in range(part.shape[0]):
            device = ((k ^ line_me) * half + (n % half ^ me_ref[1])) * 2 + (n // half ^ me_ref[2])
            copies.append(pltpu.make_async_copy(source(part, k), target(device), sems.at[n * part.shape[0] + k]))
    return copies


def copy_count(parts):
    return 1 if len(parts) == 1 else len(parts) * parts[0].shape[0]


def fill_segments(lens_ref, valid_ref, segc, segr):
    row_c = lax.broadcasted_iota(jnp.int32, (ROWS, BLK), 0)
    row_r = lax.broadcasted_iota(jnp.int32, (8, ROWS), 1)
    sum_c = jnp.zeros((ROWS, BLK), jnp.int32)
    sum_r = jnp.zeros((8, ROWS), jnp.int32)
    end = jnp.int32(0)
    for j in range(lens_ref.shape[1]):
        end = end + lens_ref[0, j]
        sum_c = sum_c + (row_c >= end).astype(jnp.int32)
        sum_r = sum_r + (row_r >= end).astype(jnp.int32)
    valid = valid_ref[0]
    segc[...] = jnp.where(row_c < valid, sum_c, -1)
    segr[...] = jnp.where(row_r < valid, sum_r, -1)


def block_place(segc, segr, i):
    start = pl.multiple_of(jnp.clip(i * (QB // BLK) - 1, 0, (ROWS - WIN) // BLK) * BLK, BLK)
    here = pl.ds(pl.multiple_of(i * QB, BLK), QB)
    window = pl.ds(start, WIN)
    rows = jnp.concatenate([segc[here, :]] * (WIN // BLK), axis=1)
    bias = jnp.where(rows == segr[0:1, window], 0.0, -1000000000.0).astype(f32)
    return here, window, jnp.concatenate([bias, bias], axis=0)


def lane_masks():
    low = (lax.broadcasted_iota(jnp.int32, (1, BLK), 1) < HD).astype(f32)
    return low.astype(bf16), (1.0 - low).astype(bf16)


def stack_pair(block, masks):
    return jnp.concatenate([block * masks[0], block * masks[1]], axis=0)


def pick_pair(values):
    low = lax.broadcasted_iota(jnp.int32, (1, BLK), 1) < HD
    return jnp.where(low, values[:QB], values[QB:])


def attend_kernel(count, passed, lens_ref, valid_ref, me_ref, *refs):
    parts, (x_ref, turn_ref, vec_ref) = refs[:count], refs[count : count + 3]
    q_ref, k_ref, v_ref, ht_ref, w_out, o_ref, lse_ref = refs[-16 - passed :][:7]
    stage, w_ref, qs, ks, vs, segc, segr, sems, out_sem = refs[-9:]
    i = pl.program_id(0)
    tiles = ROWS // TILE

    def fetch():
        def source(part, k):
            return part if k is None else part.at[k]

        return gather_copies(parts, me_ref[0], me_ref, source, lambda n: stage if n is None else stage.at[n], sems)

    def store():
        return pltpu.make_async_copy(w_ref, w_out, out_sem)

    @pl.when(i == 0)
    def _():
        for copy in fetch():
            copy.start()
        fill_segments(lens_ref, valid_ref, segc, segr)
        for copy in fetch():
            copy.wait()
        w_ref[...] = stage[...].astype(f32).reshape(D, 3 * D).astype(bf16)
        store().start()

    @pl.when(i < tiles)
    def _():
        rows = pl.ds(pl.multiple_of(i * TILE, TILE), TILE)
        normed, _ = norm_parts(x_ref[...])
        low = (normed * vec_ref[0:1] + vec_ref[1:2]).astype(bf16)
        q = ((dot_nn(low, w_ref[:, :D]) + vec_ref[2:3]).astype(bf16).astype(f32) * 0.125).astype(bf16)
        k = dot_nn(low, w_ref[:, D : 2 * D]).astype(bf16)
        v = (dot_nn(low, w_ref[:, 2 * D :]) + vec_ref[3:4]).astype(bf16)
        for value, ref, scratch in ((q, q_ref, qs), (k, k_ref, ks), (v, v_ref, vs)):
            ref[...] = value
            scratch[rows] = value
        ht_ref[...] = dot_nt(turn_ref[...], low).astype(bf16)

    @pl.when(i >= tiles)
    def _():
        here, window, bias = block_place(segc, segr, i - tiles)
        masks = lane_masks()
        for p in range(PAIRS):
            s = slice(p * BLK, (p + 1) * BLK)
            scores = dot_nt(stack_pair(qs[here, s], masks), ks[window, s]) + bias
            peak = jnp.max(scores, axis=1, keepdims=True)
            expo = jnp.exp(scores - peak)
            total = jnp.sum(expo, axis=1, keepdims=True)
            o_ref[:, s] = pick_pair(dot_nn(expo.astype(bf16), vs[window, s]) * (1.0 / total)).astype(bf16)
            lse_ref[0, :, p : p + 1] = peak + jnp.log(total)

    @pl.when(i == tiles + ROWS // QB - 1)
    def _():
        store().wait()


def attend_call(lens, valid, me, parts, x, turn, vec, passed=(), tokens=()):
    tiles = ROWS // TILE

    def first(i):
        return jnp.minimum(i, tiles - 1)

    def second(i):
        return jnp.maximum(i - tiles, 0)

    tok = pl.BlockSpec((TILE, D), lambda i: (first(i), 0))
    smem = pl.BlockSpec(memory_space=pltpu.SMEM)
    count, rows = len(parts), parts[0].shape[1]
    extra = list(passed) + list(tokens)
    out = pl.pallas_call(
        functools.partial(attend_kernel, count, len(passed)),
        grid=(tiles + ROWS // QB,),
        in_specs=[smem] * 3 + [ANY] * count + [tok, whole((D, D)), whole((16, D))] + [ANY] * len(extra),
        out_specs=[
            tok,
            tok,
            tok,
            pl.BlockSpec((D, TILE), lambda i: (0, first(i))),
            ANY,
            pl.BlockSpec((QB, D), lambda i: (second(i), 0)),
            pl.BlockSpec((1, 2 * QB, BLK), lambda i: (second(i), 0, 0)),
        ]
        + [ANY] * len(passed),
        out_shape=[jax.ShapeDtypeStruct((ROWS, D), bf16)] * 3
        + [
            jax.ShapeDtypeStruct((D, ROWS), bf16),
            jax.ShapeDtypeStruct((D, 3 * D), bf16),
            jax.ShapeDtypeStruct((ROWS, D), bf16),
            jax.ShapeDtypeStruct((ROWS // QB, 2 * QB, BLK), f32),
        ]
        + [jax.ShapeDtypeStruct(p.shape, p.dtype) for p in passed],
        scratch_shapes=[
            pltpu.VMEM((D // rows, rows, 3 * D), bf16),
            pltpu.VMEM((D, 3 * D), bf16),
            pltpu.VMEM((ROWS, D), bf16),
            pltpu.VMEM((ROWS, D), bf16),
            pltpu.VMEM((ROWS, D), bf16),
            pltpu.VMEM((ROWS, BLK), jnp.int32),
            pltpu.VMEM((8, ROWS), jnp.int32),
            pltpu.SemaphoreType.DMA((copy_count(parts),)),
            pltpu.SemaphoreType.DMA,
        ],
        input_output_aliases={6 + count + n: 7 + n for n in range(len(passed))},
        compiler_params=params(),
        cost_estimate=cost(25),
        name="attend",
    )(lens, valid, me, *parts, x, turn, vec, *extra)
    return out[:7], out[7:]


STEPS = FF // D


def up_kernel(count, me_ref, o_ref, x_ref, ct_ref, turn_ref, vec_ref, b_ref, *refs):
    parts = refs[:count]
    h, dzs, stage, wp, dw_ref, p_sems, w_sems, out_sem = refs[-8:]
    grads = 2 if count > 1 else 1
    outs = refs[-17 - grads : -8]
    x1_ref, a_ref, ht_ref, ot_ref, dz_ref, wp_out, w_ref, m_ref, gp_ref, *grad_refs = outs
    i = pl.program_id(0)
    tiles = ROWS // TILE

    def fetch(first):
        block = pl.ds(4, 1) if first else pl.ds(0, 4)

        def source(part, k):
            return part.at[block] if k is None else part.at[k, block]

        def target(n):
            return stage.at[block] if n is None else stage.at[block, n]

        return gather_copies(parts, 0, me_ref, source, target, p_sems if first else w_sems)

    def store():
        return pltpu.make_async_copy(wp, wp_out, out_sem)

    @pl.when(i == 0)
    def _():
        for copy in fetch(True):
            copy.start()
        for copy in fetch(False):
            copy.start()
        for copy in fetch(True):
            copy.wait()
        wp[...] = stage[4].astype(f32).reshape(D, D).astype(bf16)
        store().start()

    @pl.when(i < tiles)
    def _():
        rows = pl.ds(pl.multiple_of(i * TILE, TILE), TILE)
        branch = dot_nn(o_ref[...], wp[...]) + vec_ref[4:5]
        inner = x_ref[...] + vec_ref[5:6] * branch
        x1_ref[...] = inner
        a_ref[...] = branch.astype(bf16)
        normed, _ = norm_parts(inner)
        low = (normed * vec_ref[6:7] + vec_ref[7:8]).astype(bf16)
        h[rows] = low
        dz = (vec_ref[9:10] * ct_ref[...]).astype(bf16)
        dz_ref[...] = dz
        dzs[rows] = dz
        ht_ref[...] = dot_nt(turn_ref[...], low).astype(bf16)
        ot_ref[...] = dot_nt(turn_ref[...], o_ref[...]).astype(bf16)

    @pl.when(i == tiles)
    def _():
        for copy in fetch(False):
            copy.wait()
        store().wait()

    @pl.when(i >= tiles)
    def _():
        chunk = (i - tiles) ^ (me_ref[0] if count > 1 else 0)
        w_ref[0] = stage[chunk].astype(f32).reshape(D, D).astype(bf16)
        for n in range(D // TILE):
            c = slice(n * TILE, (n + 1) * TILE)
            for t in range(tiles):
                r = slice(t * TILE, (t + 1) * TILE)
                m, gp = gelu_parts(dot_nn(h[r], w_ref[0, :, c]) + b_ref[:, c])
                m_ref[r, c] = m.astype(bf16)
                gp_ref[r, c] = gp.astype(bf16)
        for n in range(D // TILE):
            c = slice(n * TILE, (n + 1) * TILE)
            dw_ref[c] = dot_tn(m_ref[:, c], dzs[...])
        if grads == 1:
            grad_refs[0][...] = dw_ref[...].astype(bf16)
        else:
            blocks, _, size, _ = grad_refs[0].shape
            for k in range(blocks):
                for c, ref in enumerate(grad_refs):
                    row = ((k ^ me_ref[1]) * 2 + (c ^ me_ref[2])) * size
                    ref[k, 0] = dw_ref[pl.ds(pl.multiple_of(row, 8), size), :].astype(bf16)


def up_call(me, o, x, ct, turn, vec, b, parts, tokens=()):
    count = len(parts)
    tiles = ROWS // TILE
    _, n, r, _ = (1,) + parts[0].shape[1:] if count == 1 else (1, D // parts[0].shape[2], parts[0].shape[2], D)

    def first(i):
        return jnp.minimum(i, tiles - 1)

    def chunk(i, me):
        return jnp.maximum(i - tiles, 0) ^ (me[0] if count > 1 else 0)

    tok = pl.BlockSpec((TILE, D), lambda i, me: (first(i), 0))
    feat = pl.BlockSpec((D, TILE), lambda i, me: (0, first(i)))
    part = pl.BlockSpec((ROWS, D), lambda i, me: (0, chunk(i, me)))
    if count > 1:
        blocks = count // 2
        spec = pl.BlockSpec((blocks, 1, 4 * r, D), lambda i, me: (0, jnp.maximum(i - tiles, 0), 0, 0))
        grad_specs, grad_shapes = [spec] * 2, [jax.ShapeDtypeStruct((blocks, STEPS, 4 * r, D), bf16)] * 2
    else:
        grad_specs = [pl.BlockSpec((D, D), lambda i, me: (chunk(i, me), 0))]
        grad_shapes = [jax.ShapeDtypeStruct((FF, D), bf16)]
    return pl.pallas_call(
        functools.partial(up_kernel, count),
        grid_spec=pltpu.PrefetchScalarGridSpec(
            num_scalar_prefetch=1,
            grid=(tiles + STEPS,),
            in_specs=[tok, tok, tok, whole((D, D)), whole((16, D)), pl.BlockSpec((1, D), lambda i, me: (0, chunk(i, me)))]
            + [ANY] * (count + len(tokens)),
            out_specs=[
                tok,
                tok,
                feat,
                feat,
                tok,
                ANY,
                pl.BlockSpec((1, D, D), lambda i, me: (chunk(i, me), 0, 0)),
                part,
                part,
            ]
            + grad_specs,
            scratch_shapes=[
                pltpu.VMEM((ROWS, D), bf16),
                pltpu.VMEM((ROWS, D), bf16),
                pltpu.VMEM((5, n, r, D), bf16),
                pltpu.VMEM((D, D), bf16),
                pltpu.VMEM((D, D), f32),
                pltpu.SemaphoreType.DMA((copy_count(parts),)),
                pltpu.SemaphoreType.DMA((copy_count(parts),)),
                pltpu.SemaphoreType.DMA,
            ],
        ),
        out_shape=[
            jax.ShapeDtypeStruct((ROWS, D), f32),
            jax.ShapeDtypeStruct((ROWS, D), bf16),
            jax.ShapeDtypeStruct((D, ROWS), bf16),
            jax.ShapeDtypeStruct((D, ROWS), bf16),
            jax.ShapeDtypeStruct((ROWS, D), bf16),
            jax.ShapeDtypeStruct((D, D), bf16),
            jax.ShapeDtypeStruct((STEPS, D, D), bf16),
            jax.ShapeDtypeStruct((ROWS, FF), bf16),
            jax.ShapeDtypeStruct((ROWS, FF), bf16),
        ]
        + grad_shapes,
        compiler_params=params(),
        cost_estimate=cost(26),
        name="mlp_up",
    )(me, o, x, ct, turn, vec, b, *parts, *tokens)


def down_kernel(
    count, me_ref, m_ref, gp_ref, dz_ref, ht_ref, w1_ref, x1_ref, ct_ref, a_ref, ot_ref, wp_ref, dzt_ref, vec_ref, *refs
):
    parts = refs[:count]
    out_ref, dx_ref, do_ref, keep_ref, away_ref, db1_ref, sums_ref, _, z_acc, dh_acc, dwp_acc, w2_ref, sems = refs[-13:]
    j = pl.program_id(0)

    def fetch(step):
        if count == 1:
            return [pltpu.make_async_copy(parts[0].at[step], w2_ref.at[step], sems.at[step, 0])]
        half, copies = count // 2, []
        for n, part in enumerate(parts):
            place = (n % half ^ me_ref[1]) * 2 + (n // half ^ me_ref[2])
            copies.append(pltpu.make_async_copy(part.at[step], w2_ref.at[step, place], sems.at[step, n]))
        return copies

    @pl.when(j == 0)
    def _():
        for step in range(STEPS):
            for copy in fetch(step):
                copy.start()
        z_acc[...] = jnp.zeros_like(z_acc)
        dh_acc[...] = jnp.zeros_like(dh_acc)
        dwp_acc[...] = jnp.zeros_like(dwp_acc)
        sums_ref[...] = jnp.zeros_like(sums_ref)

    @pl.when(j < STEPS)
    def _():
        for copy in fetch(j):
            copy.wait()
        w1 = w1_ref[0]
        w2 = w2_ref[j].reshape(D, D)
        du = (dot_nt(dz_ref[...], w2) * gp_ref[...].astype(f32)).astype(bf16)
        db1_ref[...] = col_sum(du.astype(f32))
        keep_ref[...] = dot_nn(ht_ref[: D // 2], du).astype(bf16)
        away_ref[...] = dot_nn(ht_ref[D // 2 :], du).astype(bf16)
        z_acc[...] += dot_nn(m_ref[...], w2)
        dh_acc[...] += dot_nt(du, w1)

    @pl.when(j >= STEPS)
    def _():
        r = pl.ds(pl.multiple_of((j - STEPS) * TILE, TILE), TILE)
        inner, ct, branch = x1_ref[...], ct_ref[...], z_acc[r] + vec_ref[8:9]
        out_ref[...] = inner + vec_ref[9:10] * branch
        normed, scale = norm_parts(inner)
        dh = dh_acc[r]
        dx = ct + norm_back(dh, normed, scale, vec_ref[6:7])
        dx_ref[...] = dx
        da = (vec_ref[5:6] * dx).astype(bf16)
        do_ref[...] = dot_nt(da, wp_ref[...]).astype(bf16)
        dwp_acc[...] += dot_nn(ot_ref[...], da)
        adds = (da.astype(f32), dx * a_ref[...].astype(f32), dh * normed, dh, dzt_ref[...].astype(f32), ct * branch)
        sums_ref[...] += jnp.concatenate([col_sum(v) for v in adds] + [jnp.zeros((2, D), f32)], axis=0)

    @pl.when(j == STEPS + ROWS // TILE - 1)
    def _():
        keep_ref[...] = dwp_acc[: D // 2].astype(bf16)
        away_ref[...] = dwp_acc[D // 2 :].astype(bf16)


def down_call(me, m, gp, dz, ht, w1, parts, x1, ct, a, ot, wp, vec, passed, tokens):
    count = len(parts)
    size = parts[0].shape[-2]

    def last(j):
        return jnp.minimum(j, STEPS - 1)

    def row(j):
        return jnp.maximum(j - STEPS, 0)

    part = pl.BlockSpec((ROWS, D), lambda j: (0, last(j)))
    grad = pl.BlockSpec((D // 2, D), lambda j: (0, jnp.minimum(j, STEPS)))
    tile = pl.BlockSpec((TILE, D), lambda j: (row(j), 0))
    return pl.pallas_call(
        functools.partial(down_kernel, count),
        grid=(STEPS + ROWS // TILE,),
        in_specs=[
            pl.BlockSpec(memory_space=pltpu.SMEM),
            part,
            part,
            whole((ROWS, D)),
            whole((D, ROWS)),
            pl.BlockSpec((1, D, D), lambda j: (last(j), 0, 0)),
            tile,
            tile,
            tile,
            pl.BlockSpec((D, TILE), lambda j: (0, row(j))),
            whole((D, D)),
            tile,
            whole((16, D)),
        ]
        + [ANY] * (count + 1 + len(tokens)),
        out_specs=[
            tile,
            tile,
            tile,
            grad,
            grad,
            pl.BlockSpec((1, D), lambda j: (0, last(j))),
            whole((8, D)),
            ANY,
        ],
        out_shape=[
            jax.ShapeDtypeStruct((ROWS, D), f32),
            jax.ShapeDtypeStruct((ROWS, D), f32),
            jax.ShapeDtypeStruct((ROWS, D), bf16),
            jax.ShapeDtypeStruct((D // 2, FF + D), bf16),
            jax.ShapeDtypeStruct((D // 2, FF + D), bf16),
            jax.ShapeDtypeStruct((1, FF), f32),
            jax.ShapeDtypeStruct((8, D), f32),
            jax.ShapeDtypeStruct(passed.shape, passed.dtype),
        ],
        scratch_shapes=[
            pltpu.VMEM((ROWS, D), f32),
            pltpu.VMEM((ROWS, D), f32),
            pltpu.VMEM((D, D), f32),
            pltpu.VMEM((STEPS, D // size, size, D), bf16),
            pltpu.SemaphoreType.DMA((STEPS, count)),
        ],
        input_output_aliases={13 + count: 7},
        compiler_params=params(),
        cost_estimate=cost(35),
        name="mlp_down",
    )(me, m, gp, dz, ht, w1, x1, ct, a, ot, wp, dz, vec, *parts, passed, *tokens)


def back_kernel(passed, lens_ref, valid_ref, q_ref, k_ref, v_ref, do_ref, o_ref, lse_ref, ht_hbm, *refs):
    dq_out, dk_out, dv_out, keep_ref, away_ref, sums_ref = refs[-16 - passed :][:6]
    segc, segr, dk_acc, dv_acc, dq_ref, dk_ref, dv_ref, ht_ref, sems, ht_sem = refs[-10:]
    i = pl.program_id(0)
    steps = ROWS // QB

    def fetch():
        return pltpu.make_async_copy(ht_hbm, ht_ref, ht_sem)

    def store(n):
        return pltpu.make_async_copy((dq_ref, dk_ref, dv_ref)[n], (dq_out, dk_out, dv_out)[n], sems.at[n])

    @pl.when(i == 0)
    def _():
        fetch().start()
        fill_segments(lens_ref, valid_ref, segc, segr)
        dk_acc[...] = jnp.zeros_like(dk_acc)
        dv_acc[...] = jnp.zeros_like(dv_acc)

    @pl.when(i < steps)
    def _():
        here, window, bias = block_place(segc, segr, i)
        masks = lane_masks()
        for p in range(PAIRS):
            s = slice(p * BLK, (p + 1) * BLK)
            queries = stack_pair(q_ref[:, s], masks)
            grads = stack_pair(do_ref[:, s], masks)
            o = o_ref[:, s].astype(f32)
            center = jnp.sum(grads.astype(f32) * jnp.concatenate([o, o], axis=0), axis=1, keepdims=True)
            probs = jnp.exp(dot_nt(queries, k_ref[window, s]) + bias - lse_ref[0, :, p : p + 1])
            dscores = (probs * (dot_nt(grads, v_ref[window, s]) - center)).astype(bf16)
            dv_acc[window, s] += dot_tn(probs.astype(bf16), grads)
            dk_acc[window, s] += dot_tn(dscores, queries)
            dq_ref[here, s] = (pick_pair(dot_nn(dscores, k_ref[window, s])) * 0.125).astype(bf16)

    def weights(ref):
        away_ref[...] = dot_nn(ht_ref[D // 2 :], ref[...]).astype(bf16)
        keep_ref[...] = dot_nn(ht_ref[: D // 2], ref[...]).astype(bf16)

    @pl.when(i == steps)
    def _():
        dk_ref[...] = dk_acc[...].astype(bf16)
        dv_ref[...] = dv_acc[...].astype(bf16)
        for n in range(3):
            store(n).start()
        fetch().wait()
        weights(dq_ref)
        dbq = col_sum(dq_ref[...].astype(f32))
        dbv = col_sum(dv_ref[...].astype(f32))
        sums_ref[...] = jnp.concatenate([dbq, dbv, jnp.zeros((6, D), f32)], axis=0)

    @pl.when(i == steps + 1)
    def _():
        weights(dk_ref)

    @pl.when(i == steps + 2)
    def _():
        weights(dv_ref)
        for n in range(3):
            store(n).wait()


def back_call(lens, valid, q, k, v, do, o, lse, ht, passed=(), tokens=()):
    steps = ROWS // QB

    def last(i):
        return jnp.minimum(i, steps - 1)

    tok = pl.BlockSpec((QB, D), lambda i: (last(i), 0))
    full = whole((ROWS, D))
    grad = pl.BlockSpec((D // 2, D), lambda i: (0, jnp.maximum(i - steps, 0)))
    extra = list(passed) + list(tokens)
    out = pl.pallas_call(
        functools.partial(back_kernel, len(passed)),
        grid=(steps + 3,),
        in_specs=[
            pl.BlockSpec(memory_space=pltpu.SMEM),
            pl.BlockSpec(memory_space=pltpu.SMEM),
            tok,
            full,
            full,
            tok,
            tok,
            pl.BlockSpec((1, 2 * QB, BLK), lambda i: (last(i), 0, 0)),
            ANY,
        ]
        + [ANY] * len(extra),
        out_specs=[ANY] * 3 + [grad, grad, whole((8, D))] + [ANY] * len(passed),
        out_shape=[jax.ShapeDtypeStruct((ROWS, D), bf16)] * 3
        + [jax.ShapeDtypeStruct((D // 2, 3 * D), bf16)] * 2
        + [jax.ShapeDtypeStruct((8, D), f32)]
        + [jax.ShapeDtypeStruct(p.shape, p.dtype) for p in passed],
        scratch_shapes=[
            pltpu.VMEM((ROWS, BLK), jnp.int32),
            pltpu.VMEM((8, ROWS), jnp.int32),
            pltpu.VMEM((ROWS, D), f32),
            pltpu.VMEM((ROWS, D), f32),
            pltpu.VMEM((ROWS, D), bf16),
            pltpu.VMEM((ROWS, D), bf16),
            pltpu.VMEM((ROWS, D), bf16),
            pltpu.VMEM((D, ROWS), bf16),
            pltpu.SemaphoreType.DMA((3,)),
            pltpu.SemaphoreType.DMA,
        ],
        input_output_aliases={9 + n: 6 + n for n in range(len(passed))},
        compiler_params=params(),
        cost_estimate=cost(33),
        name="attend_back",
    )(lens, valid, q, k, v, do, o, lse, ht, *extra)
    return out[:6], out[6:]


def input_kernel(passed, dq_ref, dk_ref, dv_ref, w_ref, x_ref, dx1_ref, vec_ref, *refs):
    dx_ref, sums_ref = refs[len(refs) - 2 - passed :][:2]
    i = pl.program_id(0)
    dh = dot_nt(dq_ref[...], w_ref[:, :D]) + dot_nt(dk_ref[...], w_ref[:, D : 2 * D]) + dot_nt(dv_ref[...], w_ref[:, 2 * D :])
    normed, scale = norm_parts(x_ref[...])
    dx_ref[...] = dx1_ref[...] + norm_back(dh, normed, scale, vec_ref[0:1])
    sums = jnp.concatenate([col_sum(dh * normed), col_sum(dh), jnp.zeros((6, D), f32)], axis=0)

    @pl.when(i == 0)
    def _():
        sums_ref[...] = sums

    @pl.when(i > 0)
    def _():
        sums_ref[...] += sums


def input_call(dq, dk, dv, w, x, dx1, vec, passed=(), tokens=()):
    tok = pl.BlockSpec((TILE, D), lambda i: (i, 0))
    extra = list(passed) + list(tokens)
    out = pl.pallas_call(
        functools.partial(input_kernel, len(passed)),
        grid=(ROWS // TILE,),
        in_specs=[tok, tok, tok, whole((D, 3 * D)), tok, tok, whole((16, D))] + [ANY] * len(extra),
        out_specs=[tok, whole((8, D))] + [ANY] * len(passed),
        out_shape=[jax.ShapeDtypeStruct((ROWS, D), f32), jax.ShapeDtypeStruct((8, D), f32)]
        + [jax.ShapeDtypeStruct(p.shape, p.dtype) for p in passed],
        input_output_aliases={7 + n: 2 + n for n in range(len(passed))},
        compiler_params=params(),
        cost_estimate=cost(13),
        name="input_back",
    )(dq, dk, dv, w, x, dx1, vec, *extra)
    return out[:2], out[2:]


def swap_cores(x):
    return lax.ppermute(x, "c", [(0, 1), (1, 0)])


def from_peer(x, axes, k):
    return lax.ppermute(x, axes, [(i, i ^ k) for i in range(lax.axis_size(axes))])


def gate_kernel(*refs):
    del refs


def gate(arrays, tokens):
    out = pl.pallas_call(
        gate_kernel,
        in_specs=[ANY] * (len(arrays) + len(tokens)),
        out_specs=[ANY] * len(arrays),
        out_shape=[jax.ShapeDtypeStruct(a.shape, a.dtype) for a in arrays],
        input_output_aliases={n: n for n in range(len(arrays))},
        name="gate",
    )(*arrays, *tokens)
    return list(out)


def own_order(rows):
    place = jnp.arange(D, dtype=jnp.int32)
    k, rest = place % rows, place // rows
    na, nb, nf = lax.axis_size("a"), lax.axis_size("b"), lax.axis_size("f")
    a, rest = rest % na ^ lax.axis_index("a"), rest // na
    f, rest = rest % nf ^ lax.axis_index("f"), rest // nf
    b, c = rest % nb ^ lax.axis_index("b"), rest // nb ^ lax.axis_index("c")
    return (((a * nb + b) * nf + f) * 2 + c) * rows + k


def line(shard):
    return [shard] + [from_peer(shard, "a", k) for k in range(1, lax.axis_size("a"))]


def spread(shard, axis):
    return lax.all_to_all(jnp.broadcast_to(shard[None], (lax.axis_size(axis),) + shard.shape), axis, 0, 0)


def gather_plane(stack):
    return [stack] + [from_peer(stack, ("b", "f"), k) for k in range(1, lax.axis_size(("b", "f")))]


def by_owner(parts, order, natural_line=False):
    if natural_line:
        index = jnp.arange(lax.axis_size("a")) ^ lax.axis_index("a")
        parts = [jnp.take(p, index, axis=0) for p in parts]
    return jnp.take(jnp.concatenate(parts, axis=0), jnp.argsort(order), axis=0)


def add(terms):
    total = 0.0
    for array, low, high in terms:
        total = total + array[low:high].astype(f32)
    return total


def plain(arrays):
    return [(g, 0, g.shape[0]) for g in arrays]


def blocks(terms, axes):
    count = lax.axis_size(axes)
    size = (terms[0][2] - terms[0][1]) // count

    def block(k):
        return [(t, low + k * size, low + (k + 1) * size) for t, low, _ in terms]

    return block(0), [add(block(k)).astype(bf16) for k in range(1, count)]


def exchange(terms, axes):
    mine, sends = blocks(terms, axes)
    return mine, [from_peer(t, axes, k + 1) for k, t in enumerate(sends)]


def hold(terms, array):
    return [(array,) + terms[0][1:]] + terms[1:]


def shards(inputs, img_lens, valid_rows, w_qkv, w_proj, w_fc1, b_fc1, w_fc2, vectors, cotangent):
    devices = lax.axis_size(ALL)
    rows = D // devices
    slots = rows * BLK
    na, nb, nf = lax.axis_size("a"), lax.axis_size("b"), lax.axis_size("f")
    direct = na == STEPS and rows % 8 == 0
    me = jnp.stack([lax.axis_index("a"), lax.axis_index(("b", "f")), lax.axis_index("c")]).astype(jnp.int32)
    small = jnp.concatenate([vectors, b_fc1])
    small = jnp.pad(small, (0, slots - small.shape[0])).reshape(rows, BLK)
    head = jnp.concatenate([w_qkv.reshape(rows, 3 * D), small], axis=1).astype(bf16)
    wide = [w_fc1.reshape(rows, 4, D), w_proj.reshape(rows, 1, D)]
    wide = jnp.concatenate([jnp.swapaxes(t.astype(bf16), 0, 1) for t in wide], axis=0)
    tall = w_fc2.reshape(4 * rows, D).astype(bf16)

    order = own_order(rows)
    owners = order[::rows] // rows
    turn = (order[:, None] == jnp.arange(D, dtype=jnp.int32)[None, :]).astype(bf16)
    head = line(head)
    small = gather_plane(jnp.stack([t[:, 3 * D :] for t in head]))
    head = jnp.stack([t[:, : 3 * D] for t in head])
    head_parts = gather_plane(head)
    (wide,) = gate([wide], small[1:2])
    wide = spread(wide, "a")
    (tall,) = gate([tall], [wide])
    tall = spread(tall, "a")
    small = jnp.concatenate(small, axis=0).reshape(-1, BLK)
    small = jnp.concatenate([small, swap_cores(small)], axis=0)
    small = dot_tn(turn, small).reshape(devices, slots)
    nvec = vectors.shape[0]
    vec = jnp.pad(small[:, :nvec].reshape(10, D), ((0, 6), (0, 0)))
    b1 = small[:, nvec : nvec + b_fc1.shape[0]].reshape(1, FF)
    (wide,) = gate([wide], head_parts[1:])
    wide_parts = gather_plane(wide)
    head_parts = head_parts + [swap_cores(p) for p in head_parts]
    if not direct:
        head_parts = [by_owner(head_parts, owners).reshape(-1, D // 32, 3 * D)]
    (q, k, v, h1t, wqkv, o, lse), _ = attend_call(img_lens, valid_rows, me, head_parts, inputs, turn, vec)
    *wide_parts, tall = gate(wide_parts + [tall], [o])
    tall_parts = gather_plane(tall)
    wide_parts = wide_parts + [swap_cores(p) for p in wide_parts]
    if not direct:
        wide_parts = [jnp.swapaxes(by_owner(wide_parts, owners, True), 0, 1).reshape(5, 32, D // 32, D)]
    x1, a, h2t, ot, dz, wp, w1, m, gp, *dw2 = up_call(me, o, inputs, cotangent, turn, vec, b1, wide_parts)
    if direct:
        keep2, away2 = [g.reshape(FF // 2, D) for g in dw2]
    else:
        dw2 = jnp.take(dw2[0].reshape(devices, 4 * rows, D), owners, axis=0).reshape(FF, D)
        keep2, away2 = dw2[: FF // 2], dw2[FF // 2 :]
    tall_parts = tall_parts + [swap_cores(p) for p in tall_parts]
    if not direct:
        tall_parts = [by_owner(tall_parts, owners, True).reshape(STEPS, 8, D // 8, D)]

    bf = ("b", "f")
    core2 = swap_cores(gate([away2], tall_parts[1 : len(tall_parts) // 2])[0])
    up2, up2_got = exchange(plain([keep2, core2]), bf)
    result, dx1, do, keep, away, db1, sums2, keep2 = down_call(
        me, m, gp, dz, h2t, w1, tall_parts, x1, cotangent, a, ot, wp, vec, passed=keep2, tokens=[core2]
    )
    core = swap_cores(gate([away], up2_got)[0])
    up2, up2_last = exchange(hold(up2, keep2) + plain(up2_got), "a")
    mid, mid_got = exchange(plain([keep, core]), bf)

    (dq, dk, dv, keep1, away1, sums_a), (keep, keep2) = back_call(
        img_lens, valid_rows, q, k, v, do, o, lse, h1t, passed=[keep, keep2], tokens=[core]
    )
    core1 = swap_cores(gate([away1], mid_got + up2_last)[0])
    mid, mid_last = exchange(hold(mid, keep) + plain(mid_got), "a")
    second, second_got = exchange(plain([keep1, core1]), bf)

    (d_input, sums0), (keep, keep1, keep2) = input_call(
        dq, dk, dv, wqkv, inputs, dx1, vec, passed=[keep, keep1, keep2], tokens=[core1]
    )
    second, second_sends = blocks(hold(second, keep1) + plain(second_got), "a")
    sums0, sums_a, sums2, db1, keep, keep2 = gate([sums0, sums_a, sums2, db1, keep, keep2], second_sends + mid_last)
    second_last = [from_peer(t, "a", k + 1) for k, t in enumerate(second_sends)]
    g_fc2 = add(hold(up2, keep2) + plain(up2_last))
    gvec = jnp.concatenate([sums0[:2], sums_a[:2], sums2[:6]], axis=0).reshape(devices, nvec)
    gsmall = jnp.concatenate([gvec, db1.reshape(devices, b_fc1.shape[0])], axis=1)
    gsmall = jnp.pad(gsmall, ((0, 0), (0, -gsmall.shape[1] % BLK))).astype(bf16)
    gsmall = lax.all_to_all(gsmall.reshape(devices, 1, -1), ALL, 0, 0)
    gsmall = jnp.sum(gsmall.astype(f32), axis=0).reshape(-1)

    g_mid = add(hold(mid, keep) + plain(mid_last))
    g_fc1, g_proj = g_mid[:, :FF], g_mid[:, FF:]
    g_qkv = add(second + plain(second_last))
    return (
        result,
        d_input,
        g_qkv.reshape(-1),
        g_proj.reshape(-1),
        g_fc1.reshape(-1),
        gsmall[nvec : nvec + b_fc1.shape[0]],
        g_fc2.reshape(-1),
        gsmall[:nvec],
    )


def solution(mesh):
    dp, fsdp = mesh.shape["dp"], mesh.shape["fsdp"]
    fine = Mesh(mesh.devices.reshape(dp // 2, 2, fsdp // 2, 2), ALL)
    rows, flat = P(ALL, None), P(ALL)
    return jax.shard_map(
        shards,
        mesh=fine,
        in_specs=(rows, rows, flat, flat, flat, flat, flat, flat, flat, rows),
        out_specs=(rows, rows, flat, flat, flat, flat, flat, flat),
        check_vma=False,
    )
```

```python
import functools

import jax
import jax.numpy as jnp
from jax import lax
from jax.experimental import pallas as pl
from jax.experimental.pallas import tpu as pltpu
from jax.sharding import Mesh
from jax.sharding import PartitionSpec as P

HEADS = 12
HD = 64
ROWS = 1024
D = HEADS * HD
FF = 4 * D
PAIRS = HEADS // 2
BLK = 128
QB = 2 * BLK
WIN = QB + 2 * BLK
TILE = 256
EPS = 1e-06
ALL = ("a", "b", "f", "c")
bf16 = jnp.bfloat16
f32 = jnp.float32
VMEM_LIMIT = 60 * 1024 * 1024
ANY = pl.BlockSpec(memory_space=pl.ANY)


def cost(us):
    return pl.CostEstimate(flops=us * 1_100_000_000, bytes_accessed=us * 3_000_000, transcendentals=0)


def dot_nn(left, right):
    return lax.dot_general(left, right, (((1,), (0,)), ((), ())), preferred_element_type=f32)


def dot_nt(left, right):
    return lax.dot_general(left, right, (((1,), (1,)), ((), ())), preferred_element_type=f32)


def dot_tn(left, right):
    return lax.dot_general(left, right, (((0,), (0,)), ((), ())), preferred_element_type=f32)


def norm_parts(values):
    center = values - jnp.mean(values, axis=-1, keepdims=True)
    scale = lax.rsqrt(jnp.mean(center * center, axis=-1, keepdims=True) + EPS)
    return center * scale, scale


def norm_back(grad, normed, scale, gain):
    inner = grad * gain
    first = jnp.mean(inner, axis=-1, keepdims=True)
    second = jnp.mean(inner * normed, axis=-1, keepdims=True)
    return scale * (inner - first - normed * second)


def col_sum(values):
    return jnp.sum(values, axis=0, keepdims=True)


def gelu_parts(u):
    half = 0.5 + 0.5 * lax.erf(u * 0.7071067811865476)
    e = jnp.exp2((u * u) * -0.7213475204444817)
    return u * half, half + (0.3989422804014327 * u) * e


def params(**kw):
    return pltpu.CompilerParams(vmem_limit_bytes=VMEM_LIMIT, **kw)


def whole(shape):
    return pl.BlockSpec(shape, lambda *_: (0,) * len(shape))


def gather_copies(parts, line_me, me_ref, source, target, sems):
    if len(parts) == 1:
        return [pltpu.make_async_copy(source(parts[0], None), target(None), sems.at[0])]
    half, copies = len(parts) // 2, []
    for n, part in enumerate(parts):
        for k in range(part.shape[0]):
            device = ((k ^ line_me) * half + (n % half ^ me_ref[1])) * 2 + (n // half ^ me_ref[2])
            copies.append(pltpu.make_async_copy(source(part, k), target(device), sems.at[n * part.shape[0] + k]))
    return copies


def copy_count(parts):
    return 1 if len(parts) == 1 else len(parts) * parts[0].shape[0]


def fill_segments(lens_ref, valid_ref, segc, segr):
    row_c = lax.broadcasted_iota(jnp.int32, (ROWS, BLK), 0)
    row_r = lax.broadcasted_iota(jnp.int32, (8, ROWS), 1)
    sum_c = jnp.zeros((ROWS, BLK), jnp.int32)
    sum_r = jnp.zeros((8, ROWS), jnp.int32)
    end = jnp.int32(0)
    for j in range(lens_ref.shape[1]):
        end = end + lens_ref[0, j]
        sum_c = sum_c + (row_c >= end).astype(jnp.int32)
        sum_r = sum_r + (row_r >= end).astype(jnp.int32)
    valid = valid_ref[0]
    segc[...] = jnp.where(row_c < valid, sum_c, -1)
    segr[...] = jnp.where(row_r < valid, sum_r, -1)


def block_place(segc, segr, i):
    start = pl.multiple_of(jnp.clip(i * (QB // BLK) - 1, 0, (ROWS - WIN) // BLK) * BLK, BLK)
    here = pl.ds(pl.multiple_of(i * QB, BLK), QB)
    window = pl.ds(start, WIN)
    rows = jnp.concatenate([segc[here, :]] * (WIN // BLK), axis=1)
    bias = jnp.where(rows == segr[0:1, window], 0.0, -1000000000.0).astype(f32)
    return here, window, jnp.concatenate([bias, bias], axis=0)


def lane_masks():
    low = (lax.broadcasted_iota(jnp.int32, (1, BLK), 1) < HD).astype(f32)
    return low.astype(bf16), (1.0 - low).astype(bf16)


def stack_pair(block, masks):
    return jnp.concatenate([block * masks[0], block * masks[1]], axis=0)


def pick_pair(values):
    low = lax.broadcasted_iota(jnp.int32, (1, BLK), 1) < HD
    return jnp.where(low, values[:QB], values[QB:])


def attend_kernel(count, passed, lens_ref, valid_ref, me_ref, *refs):
    parts, (x_ref, turn_ref, vec_ref) = refs[:count], refs[count : count + 3]
    q_ref, k_ref, v_ref, ht_ref, w_out, o_ref, lse_ref = refs[-16 - passed :][:7]
    stage, w_ref, qs, ks, vs, segc, segr, sems, out_sem = refs[-9:]
    i = pl.program_id(0)
    tiles = ROWS // TILE

    def fetch():
        def source(part, k):
            return part if k is None else part.at[k]

        return gather_copies(parts, me_ref[0], me_ref, source, lambda n: stage if n is None else stage.at[n], sems)

    def store():
        return pltpu.make_async_copy(w_ref, w_out, out_sem)

    @pl.when(i == 0)
    def _():
        for copy in fetch():
            copy.start()
        fill_segments(lens_ref, valid_ref, segc, segr)
        for copy in fetch():
            copy.wait()
        w_ref[...] = stage[...].astype(f32).reshape(D, 3 * D).astype(bf16)
        store().start()

    @pl.when(i < tiles)
    def _():
        rows = pl.ds(pl.multiple_of(i * TILE, TILE), TILE)
        normed, _ = norm_parts(x_ref[...])
        low = (normed * vec_ref[0:1] + vec_ref[1:2]).astype(bf16)
        q = ((dot_nn(low, w_ref[:, :D]) + vec_ref[2:3]).astype(bf16).astype(f32) * 0.125).astype(bf16)
        k = dot_nn(low, w_ref[:, D : 2 * D]).astype(bf16)
        v = (dot_nn(low, w_ref[:, 2 * D :]) + vec_ref[3:4]).astype(bf16)
        for value, ref, scratch in ((q, q_ref, qs), (k, k_ref, ks), (v, v_ref, vs)):
            ref[...] = value
            scratch[rows] = value
        ht_ref[...] = dot_nt(turn_ref[...], low).astype(bf16)

    @pl.when(i >= tiles)
    def _():
        here, window, bias = block_place(segc, segr, i - tiles)
        masks = lane_masks()
        for p in range(PAIRS):
            s = slice(p * BLK, (p + 1) * BLK)
            scores = dot_nt(stack_pair(qs[here, s], masks), ks[window, s]) + bias
            peak = jnp.max(scores, axis=1, keepdims=True)
            expo = jnp.exp(scores - peak)
            total = jnp.sum(expo, axis=1, keepdims=True)
            o_ref[:, s] = pick_pair(dot_nn(expo.astype(bf16), vs[window, s]) * (1.0 / total)).astype(bf16)
            lse_ref[0, :, p : p + 1] = peak + jnp.log(total)

    @pl.when(i == tiles + ROWS // QB - 1)
    def _():
        store().wait()


def attend_call(lens, valid, me, parts, x, turn, vec, passed=(), tokens=()):
    tiles = ROWS // TILE

    def first(i):
        return jnp.minimum(i, tiles - 1)

    def second(i):
        return jnp.maximum(i - tiles, 0)

    tok = pl.BlockSpec((TILE, D), lambda i: (first(i), 0))
    smem = pl.BlockSpec(memory_space=pltpu.SMEM)
    count, rows = len(parts), parts[0].shape[1]
    extra = list(passed) + list(tokens)
    out = pl.pallas_call(
        functools.partial(attend_kernel, count, len(passed)),
        grid=(tiles + ROWS // QB,),
        in_specs=[smem] * 3 + [ANY] * count + [tok, whole((D, D)), whole((16, D))] + [ANY] * len(extra),
        out_specs=[
            tok,
            tok,
            tok,
            pl.BlockSpec((D, TILE), lambda i: (0, first(i))),
            ANY,
            pl.BlockSpec((QB, D), lambda i: (second(i), 0)),
            pl.BlockSpec((1, 2 * QB, BLK), lambda i: (second(i), 0, 0)),
        ]
        + [ANY] * len(passed),
        out_shape=[jax.ShapeDtypeStruct((ROWS, D), bf16)] * 3
        + [
            jax.ShapeDtypeStruct((D, ROWS), bf16),
            jax.ShapeDtypeStruct((D, 3 * D), bf16),
            jax.ShapeDtypeStruct((ROWS, D), bf16),
            jax.ShapeDtypeStruct((ROWS // QB, 2 * QB, BLK), f32),
        ]
        + [jax.ShapeDtypeStruct(p.shape, p.dtype) for p in passed],
        scratch_shapes=[
            pltpu.VMEM((D // rows, rows, 3 * D), bf16),
            pltpu.VMEM((D, 3 * D), bf16),
            pltpu.VMEM((ROWS, D), bf16),
            pltpu.VMEM((ROWS, D), bf16),
            pltpu.VMEM((ROWS, D), bf16),
            pltpu.VMEM((ROWS, BLK), jnp.int32),
            pltpu.VMEM((8, ROWS), jnp.int32),
            pltpu.SemaphoreType.DMA((copy_count(parts),)),
            pltpu.SemaphoreType.DMA,
        ],
        input_output_aliases={6 + count + n: 7 + n for n in range(len(passed))},
        compiler_params=params(),
        cost_estimate=cost(25),
        name="attend",
    )(lens, valid, me, *parts, x, turn, vec, *extra)
    return out[:7], out[7:]


STEPS = FF // D


def up_kernel(count, me_ref, o_ref, x_ref, ct_ref, turn_ref, vec_ref, b_ref, *refs):
    parts = refs[:count]
    h, dzs, stage, wp, dw_ref, p_sems, w_sems, out_sem = refs[-8:]
    grads = 2 if count > 1 else 1
    outs = refs[-17 - grads : -8]
    x1_ref, a_ref, ht_ref, ot_ref, dz_ref, wp_out, w_ref, m_ref, gp_ref, *grad_refs = outs
    i = pl.program_id(0)
    tiles = ROWS // TILE

    def fetch(first):
        block = pl.ds(4, 1) if first else pl.ds(0, 4)

        def source(part, k):
            return part.at[block] if k is None else part.at[k, block]

        def target(n):
            return stage.at[block] if n is None else stage.at[block, n]

        return gather_copies(parts, 0, me_ref, source, target, p_sems if first else w_sems)

    def store():
        return pltpu.make_async_copy(wp, wp_out, out_sem)

    @pl.when(i == 0)
    def _():
        for copy in fetch(True):
            copy.start()
        for copy in fetch(False):
            copy.start()
        for copy in fetch(True):
            copy.wait()
        wp[...] = stage[4].astype(f32).reshape(D, D).astype(bf16)
        store().start()

    @pl.when(i < tiles)
    def _():
        rows = pl.ds(pl.multiple_of(i * TILE, TILE), TILE)
        branch = dot_nn(o_ref[...], wp[...]) + vec_ref[4:5]
        inner = x_ref[...] + vec_ref[5:6] * branch
        x1_ref[...] = inner
        a_ref[...] = branch.astype(bf16)
        normed, _ = norm_parts(inner)
        low = (normed * vec_ref[6:7] + vec_ref[7:8]).astype(bf16)
        h[rows] = low
        dz = (vec_ref[9:10] * ct_ref[...]).astype(bf16)
        dz_ref[...] = dz
        dzs[rows] = dz
        ht_ref[...] = dot_nt(turn_ref[...], low).astype(bf16)
        ot_ref[...] = dot_nt(turn_ref[...], o_ref[...]).astype(bf16)

    @pl.when(i == tiles)
    def _():
        for copy in fetch(False):
            copy.wait()
        store().wait()

    @pl.when(i >= tiles)
    def _():
        chunk = (i - tiles) ^ (me_ref[0] if count > 1 else 0)
        w_ref[0] = stage[chunk].astype(f32).reshape(D, D).astype(bf16)
        for n in range(D // TILE):
            c = slice(n * TILE, (n + 1) * TILE)
            for t in range(tiles):
                r = slice(t * TILE, (t + 1) * TILE)
                m, gp = gelu_parts(dot_nn(h[r], w_ref[0, :, c]) + b_ref[:, c])
                m_ref[r, c] = m.astype(bf16)
                gp_ref[r, c] = gp.astype(bf16)
        for n in range(D // TILE):
            c = slice(n * TILE, (n + 1) * TILE)
            dw_ref[c] = dot_tn(m_ref[:, c], dzs[...])
        if grads == 1:
            grad_refs[0][...] = dw_ref[...].astype(bf16)
        else:
            blocks, _, size, _ = grad_refs[0].shape
            for k in range(blocks):
                for c, ref in enumerate(grad_refs):
                    row = ((k ^ me_ref[1]) * 2 + (c ^ me_ref[2])) * size
                    ref[k, 0] = dw_ref[pl.ds(pl.multiple_of(row, 8), size), :].astype(bf16)


def up_call(me, o, x, ct, turn, vec, b, parts, tokens=()):
    count = len(parts)
    tiles = ROWS // TILE
    _, n, r, _ = (1,) + parts[0].shape[1:] if count == 1 else (1, D // parts[0].shape[2], parts[0].shape[2], D)

    def first(i):
        return jnp.minimum(i, tiles - 1)

    def chunk(i, me):
        return jnp.maximum(i - tiles, 0) ^ (me[0] if count > 1 else 0)

    tok = pl.BlockSpec((TILE, D), lambda i, me: (first(i), 0))
    feat = pl.BlockSpec((D, TILE), lambda i, me: (0, first(i)))
    part = pl.BlockSpec((ROWS, D), lambda i, me: (0, chunk(i, me)))
    if count > 1:
        blocks = count // 2
        spec = pl.BlockSpec((blocks, 1, 4 * r, D), lambda i, me: (0, jnp.maximum(i - tiles, 0), 0, 0))
        grad_specs, grad_shapes = [spec] * 2, [jax.ShapeDtypeStruct((blocks, STEPS, 4 * r, D), bf16)] * 2
    else:
        grad_specs = [pl.BlockSpec((D, D), lambda i, me: (chunk(i, me), 0))]
        grad_shapes = [jax.ShapeDtypeStruct((FF, D), bf16)]
    return pl.pallas_call(
        functools.partial(up_kernel, count),
        grid_spec=pltpu.PrefetchScalarGridSpec(
            num_scalar_prefetch=1,
            grid=(tiles + STEPS,),
            in_specs=[tok, tok, tok, whole((D, D)), whole((16, D)), pl.BlockSpec((1, D), lambda i, me: (0, chunk(i, me)))]
            + [ANY] * (count + len(tokens)),
            out_specs=[
                tok,
                tok,
                feat,
                feat,
                tok,
                ANY,
                pl.BlockSpec((1, D, D), lambda i, me: (chunk(i, me), 0, 0)),
                part,
                part,
            ]
            + grad_specs,
            scratch_shapes=[
                pltpu.VMEM((ROWS, D), bf16),
                pltpu.VMEM((ROWS, D), bf16),
                pltpu.VMEM((5, n, r, D), bf16),
                pltpu.VMEM((D, D), bf16),
                pltpu.VMEM((D, D), f32),
                pltpu.SemaphoreType.DMA((copy_count(parts),)),
                pltpu.SemaphoreType.DMA((copy_count(parts),)),
                pltpu.SemaphoreType.DMA,
            ],
        ),
        out_shape=[
            jax.ShapeDtypeStruct((ROWS, D), f32),
            jax.ShapeDtypeStruct((ROWS, D), bf16),
            jax.ShapeDtypeStruct((D, ROWS), bf16),
            jax.ShapeDtypeStruct((D, ROWS), bf16),
            jax.ShapeDtypeStruct((ROWS, D), bf16),
            jax.ShapeDtypeStruct((D, D), bf16),
            jax.ShapeDtypeStruct((STEPS, D, D), bf16),
            jax.ShapeDtypeStruct((ROWS, FF), bf16),
            jax.ShapeDtypeStruct((ROWS, FF), bf16),
        ]
        + grad_shapes,
        compiler_params=params(),
        cost_estimate=cost(26),
        name="mlp_up",
    )(me, o, x, ct, turn, vec, b, *parts, *tokens)


def down_kernel(
    count, me_ref, m_ref, gp_ref, dz_ref, ht_ref, w1_ref, x1_ref, ct_ref, a_ref, ot_ref, wp_ref, dzt_ref, vec_ref, *refs
):
    parts = refs[:count]
    out_ref, dx_ref, do_ref, keep_ref, away_ref, db1_ref, sums_ref, _, z_acc, dh_acc, dwp_acc, w2_ref, sems = refs[-13:]
    j = pl.program_id(0)

    def fetch(step):
        if count == 1:
            return [pltpu.make_async_copy(parts[0].at[step], w2_ref.at[step], sems.at[step, 0])]
        half, copies = count // 2, []
        for n, part in enumerate(parts):
            place = (n % half ^ me_ref[1]) * 2 + (n // half ^ me_ref[2])
            copies.append(pltpu.make_async_copy(part.at[step], w2_ref.at[step, place], sems.at[step, n]))
        return copies

    @pl.when(j == 0)
    def _():
        for step in range(STEPS):
            for copy in fetch(step):
                copy.start()
        z_acc[...] = jnp.zeros_like(z_acc)
        dh_acc[...] = jnp.zeros_like(dh_acc)
        dwp_acc[...] = jnp.zeros_like(dwp_acc)
        sums_ref[...] = jnp.zeros_like(sums_ref)

    @pl.when(j < STEPS)
    def _():
        for copy in fetch(j):
            copy.wait()
        w1 = w1_ref[0]
        w2 = w2_ref[j].reshape(D, D)
        du = (dot_nt(dz_ref[...], w2) * gp_ref[...].astype(f32)).astype(bf16)
        db1_ref[...] = col_sum(du.astype(f32))
        keep_ref[...] = dot_nn(ht_ref[: D // 2], du).astype(bf16)
        away_ref[...] = dot_nn(ht_ref[D // 2 :], du).astype(bf16)
        z_acc[...] += dot_nn(m_ref[...], w2)
        dh_acc[...] += dot_nt(du, w1)

    @pl.when(j >= STEPS)
    def _():
        r = pl.ds(pl.multiple_of((j - STEPS) * TILE, TILE), TILE)
        inner, ct, branch = x1_ref[...], ct_ref[...], z_acc[r] + vec_ref[8:9]
        out_ref[...] = inner + vec_ref[9:10] * branch
        normed, scale = norm_parts(inner)
        dh = dh_acc[r]
        dx = ct + norm_back(dh, normed, scale, vec_ref[6:7])
        dx_ref[...] = dx
        da = (vec_ref[5:6] * dx).astype(bf16)
        do_ref[...] = dot_nt(da, wp_ref[...]).astype(bf16)
        dwp_acc[...] += dot_nn(ot_ref[...], da)
        adds = (da.astype(f32), dx * a_ref[...].astype(f32), dh * normed, dh, dzt_ref[...].astype(f32), ct * branch)
        sums_ref[...] += jnp.concatenate([col_sum(v) for v in adds] + [jnp.zeros((2, D), f32)], axis=0)

    @pl.when(j == STEPS + ROWS // TILE - 1)
    def _():
        keep_ref[...] = dwp_acc[: D // 2].astype(bf16)
        away_ref[...] = dwp_acc[D // 2 :].astype(bf16)


def down_call(me, m, gp, dz, ht, w1, parts, x1, ct, a, ot, wp, vec, passed, tokens):
    count = len(parts)
    size = parts[0].shape[-2]

    def last(j):
        return jnp.minimum(j, STEPS - 1)

    def row(j):
        return jnp.maximum(j - STEPS, 0)

    part = pl.BlockSpec((ROWS, D), lambda j: (0, last(j)))
    grad = pl.BlockSpec((D // 2, D), lambda j: (0, jnp.minimum(j, STEPS)))
    tile = pl.BlockSpec((TILE, D), lambda j: (row(j), 0))
    return pl.pallas_call(
        functools.partial(down_kernel, count),
        grid=(STEPS + ROWS // TILE,),
        in_specs=[
            pl.BlockSpec(memory_space=pltpu.SMEM),
            part,
            part,
            whole((ROWS, D)),
            whole((D, ROWS)),
            pl.BlockSpec((1, D, D), lambda j: (last(j), 0, 0)),
            tile,
            tile,
            tile,
            pl.BlockSpec((D, TILE), lambda j: (0, row(j))),
            whole((D, D)),
            tile,
            whole((16, D)),
        ]
        + [ANY] * (count + 1 + len(tokens)),
        out_specs=[
            tile,
            tile,
            tile,
            grad,
            grad,
            pl.BlockSpec((1, D), lambda j: (0, last(j))),
            whole((8, D)),
            ANY,
        ],
        out_shape=[
            jax.ShapeDtypeStruct((ROWS, D), f32),
            jax.ShapeDtypeStruct((ROWS, D), f32),
            jax.ShapeDtypeStruct((ROWS, D), bf16),
            jax.ShapeDtypeStruct((D // 2, FF + D), bf16),
            jax.ShapeDtypeStruct((D // 2, FF + D), bf16),
            jax.ShapeDtypeStruct((1, FF), f32),
            jax.ShapeDtypeStruct((8, D), f32),
            jax.ShapeDtypeStruct(passed.shape, passed.dtype),
        ],
        scratch_shapes=[
            pltpu.VMEM((ROWS, D), f32),
            pltpu.VMEM((ROWS, D), f32),
            pltpu.VMEM((D, D), f32),
            pltpu.VMEM((STEPS, D // size, size, D), bf16),
            pltpu.SemaphoreType.DMA((STEPS, count)),
        ],
        input_output_aliases={13 + count: 7},
        compiler_params=params(),
        cost_estimate=cost(35),
        name="mlp_down",
    )(me, m, gp, dz, ht, w1, x1, ct, a, ot, wp, dz, vec, *parts, passed, *tokens)


def back_kernel(passed, lens_ref, valid_ref, q_ref, k_ref, v_ref, do_ref, o_ref, lse_ref, ht_hbm, *refs):
    dq_out, dk_out, dv_out, keep_ref, away_ref, sums_ref = refs[-16 - passed :][:6]
    segc, segr, dk_acc, dv_acc, dq_ref, dk_ref, dv_ref, ht_ref, sems, ht_sem = refs[-10:]
    i = pl.program_id(0)
    steps = ROWS // QB

    def fetch():
        return pltpu.make_async_copy(ht_hbm, ht_ref, ht_sem)

    def store(n):
        return pltpu.make_async_copy((dq_ref, dk_ref, dv_ref)[n], (dq_out, dk_out, dv_out)[n], sems.at[n])

    @pl.when(i == 0)
    def _():
        fetch().start()
        fill_segments(lens_ref, valid_ref, segc, segr)
        dk_acc[...] = jnp.zeros_like(dk_acc)
        dv_acc[...] = jnp.zeros_like(dv_acc)

    @pl.when(i < steps)
    def _():
        here, window, bias = block_place(segc, segr, i)
        masks = lane_masks()
        for p in range(PAIRS):
            s = slice(p * BLK, (p + 1) * BLK)
            queries = stack_pair(q_ref[:, s], masks)
            grads = stack_pair(do_ref[:, s], masks)
            o = o_ref[:, s].astype(f32)
            center = jnp.sum(grads.astype(f32) * jnp.concatenate([o, o], axis=0), axis=1, keepdims=True)
            probs = jnp.exp(dot_nt(queries, k_ref[window, s]) + bias - lse_ref[0, :, p : p + 1])
            dscores = (probs * (dot_nt(grads, v_ref[window, s]) - center)).astype(bf16)
            dv_acc[window, s] += dot_tn(probs.astype(bf16), grads)
            dk_acc[window, s] += dot_tn(dscores, queries)
            dq_ref[here, s] = (pick_pair(dot_nn(dscores, k_ref[window, s])) * 0.125).astype(bf16)

    def weights(ref):
        away_ref[...] = dot_nn(ht_ref[D // 2 :], ref[...]).astype(bf16)
        keep_ref[...] = dot_nn(ht_ref[: D // 2], ref[...]).astype(bf16)

    @pl.when(i == steps)
    def _():
        dk_ref[...] = dk_acc[...].astype(bf16)
        dv_ref[...] = dv_acc[...].astype(bf16)
        for n in range(3):
            store(n).start()
        fetch().wait()
        weights(dq_ref)
        dbq = col_sum(dq_ref[...].astype(f32))
        dbv = col_sum(dv_ref[...].astype(f32))
        sums_ref[...] = jnp.concatenate([dbq, dbv, jnp.zeros((6, D), f32)], axis=0)

    @pl.when(i == steps + 1)
    def _():
        weights(dk_ref)

    @pl.when(i == steps + 2)
    def _():
        weights(dv_ref)
        for n in range(3):
            store(n).wait()


def back_call(lens, valid, q, k, v, do, o, lse, ht, passed=(), tokens=()):
    steps = ROWS // QB

    def last(i):
        return jnp.minimum(i, steps - 1)

    tok = pl.BlockSpec((QB, D), lambda i: (last(i), 0))
    full = whole((ROWS, D))
    grad = pl.BlockSpec((D // 2, D), lambda i: (0, jnp.maximum(i - steps, 0)))
    extra = list(passed) + list(tokens)
    out = pl.pallas_call(
        functools.partial(back_kernel, len(passed)),
        grid=(steps + 3,),
        in_specs=[
            pl.BlockSpec(memory_space=pltpu.SMEM),
            pl.BlockSpec(memory_space=pltpu.SMEM),
            tok,
            full,
            full,
            tok,
            tok,
            pl.BlockSpec((1, 2 * QB, BLK), lambda i: (last(i), 0, 0)),
            ANY,
        ]
        + [ANY] * len(extra),
        out_specs=[ANY] * 3 + [grad, grad, whole((8, D))] + [ANY] * len(passed),
        out_shape=[jax.ShapeDtypeStruct((ROWS, D), bf16)] * 3
        + [jax.ShapeDtypeStruct((D // 2, 3 * D), bf16)] * 2
        + [jax.ShapeDtypeStruct((8, D), f32)]
        + [jax.ShapeDtypeStruct(p.shape, p.dtype) for p in passed],
        scratch_shapes=[
            pltpu.VMEM((ROWS, BLK), jnp.int32),
            pltpu.VMEM((8, ROWS), jnp.int32),
            pltpu.VMEM((ROWS, D), f32),
            pltpu.VMEM((ROWS, D), f32),
            pltpu.VMEM((ROWS, D), bf16),
            pltpu.VMEM((ROWS, D), bf16),
            pltpu.VMEM((ROWS, D), bf16),
            pltpu.VMEM((D, ROWS), bf16),
            pltpu.SemaphoreType.DMA((3,)),
            pltpu.SemaphoreType.DMA,
        ],
        input_output_aliases={9 + n: 6 + n for n in range(len(passed))},
        compiler_params=params(),
        cost_estimate=cost(33),
        name="attend_back",
    )(lens, valid, q, k, v, do, o, lse, ht, *extra)
    return out[:6], out[6:]


def input_kernel(passed, dq_ref, dk_ref, dv_ref, w_ref, x_ref, dx1_ref, vec_ref, *refs):
    dx_ref, sums_ref = refs[len(refs) - 2 - passed :][:2]
    i = pl.program_id(0)
    dh = dot_nt(dq_ref[...], w_ref[:, :D]) + dot_nt(dk_ref[...], w_ref[:, D : 2 * D]) + dot_nt(dv_ref[...], w_ref[:, 2 * D :])
    normed, scale = norm_parts(x_ref[...])
    dx_ref[...] = dx1_ref[...] + norm_back(dh, normed, scale, vec_ref[0:1])
    sums = jnp.concatenate([col_sum(dh * normed), col_sum(dh), jnp.zeros((6, D), f32)], axis=0)

    @pl.when(i == 0)
    def _():
        sums_ref[...] = sums

    @pl.when(i > 0)
    def _():
        sums_ref[...] += sums


def input_call(dq, dk, dv, w, x, dx1, vec, passed=(), tokens=()):
    tok = pl.BlockSpec((TILE, D), lambda i: (i, 0))
    extra = list(passed) + list(tokens)
    out = pl.pallas_call(
        functools.partial(input_kernel, len(passed)),
        grid=(ROWS // TILE,),
        in_specs=[tok, tok, tok, whole((D, 3 * D)), tok, tok, whole((16, D))] + [ANY] * len(extra),
        out_specs=[tok, whole((8, D))] + [ANY] * len(passed),
        out_shape=[jax.ShapeDtypeStruct((ROWS, D), f32), jax.ShapeDtypeStruct((8, D), f32)]
        + [jax.ShapeDtypeStruct(p.shape, p.dtype) for p in passed],
        input_output_aliases={7 + n: 2 + n for n in range(len(passed))},
        compiler_params=params(),
        cost_estimate=cost(13),
        name="input_back",
    )(dq, dk, dv, w, x, dx1, vec, *extra)
    return out[:2], out[2:]


def swap_cores(x):
    return lax.ppermute(x, "c", [(0, 1), (1, 0)])


def from_peer(x, axes, k):
    return lax.ppermute(x, axes, [(i, i ^ k) for i in range(lax.axis_size(axes))])


def gate_kernel(*refs):
    del refs


def gate(arrays, tokens):
    out = pl.pallas_call(
        gate_kernel,
        in_specs=[ANY] * (len(arrays) + len(tokens)),
        out_specs=[ANY] * len(arrays),
        out_shape=[jax.ShapeDtypeStruct(a.shape, a.dtype) for a in arrays],
        input_output_aliases={n: n for n in range(len(arrays))},
        name="gate",
    )(*arrays, *tokens)
    return list(out)


def own_order(rows):
    place = jnp.arange(D, dtype=jnp.int32)
    k, rest = place % rows, place // rows
    na, nb, nf = lax.axis_size("a"), lax.axis_size("b"), lax.axis_size("f")
    a, rest = rest % na ^ lax.axis_index("a"), rest // na
    f, rest = rest % nf ^ lax.axis_index("f"), rest // nf
    b, c = rest % nb ^ lax.axis_index("b"), rest // nb ^ lax.axis_index("c")
    return (((a * nb + b) * nf + f) * 2 + c) * rows + k


def line(shard):
    return [shard] + [from_peer(shard, "a", k) for k in range(1, lax.axis_size("a"))]


def spread(shard, axis):
    return lax.all_to_all(jnp.broadcast_to(shard[None], (lax.axis_size(axis),) + shard.shape), axis, 0, 0)


def gather_plane(stack):
    return [stack] + [from_peer(stack, ("b", "f"), k) for k in range(1, lax.axis_size(("b", "f")))]


def by_owner(parts, order, natural_line=False):
    if natural_line:
        index = jnp.arange(lax.axis_size("a")) ^ lax.axis_index("a")
        parts = [jnp.take(p, index, axis=0) for p in parts]
    return jnp.take(jnp.concatenate(parts, axis=0), jnp.argsort(order), axis=0)


def add(terms):
    total = 0.0
    for array, low, high in terms:
        total = total + array[low:high].astype(f32)
    return total


def plain(arrays):
    return [(g, 0, g.shape[0]) for g in arrays]


def blocks(terms, axes):
    count = lax.axis_size(axes)
    size = (terms[0][2] - terms[0][1]) // count

    def block(k):
        return [(t, low + k * size, low + (k + 1) * size) for t, low, _ in terms]

    return block(0), [add(block(k)).astype(bf16) for k in range(1, count)]


def exchange(terms, axes):
    mine, sends = blocks(terms, axes)
    return mine, [from_peer(t, axes, k + 1) for k, t in enumerate(sends)]


def hold(terms, array):
    return [(array,) + terms[0][1:]] + terms[1:]


def shards(inputs, img_lens, valid_rows, w_qkv, w_proj, w_fc1, b_fc1, w_fc2, vectors, cotangent):
    devices = lax.axis_size(ALL)
    rows = D // devices
    slots = rows * BLK
    na, nb, nf = lax.axis_size("a"), lax.axis_size("b"), lax.axis_size("f")
    direct = na == STEPS and rows % 8 == 0
    me = jnp.stack([lax.axis_index("a"), lax.axis_index(("b", "f")), lax.axis_index("c")]).astype(jnp.int32)
    small = jnp.concatenate([vectors, b_fc1])
    small = jnp.pad(small, (0, slots - small.shape[0])).reshape(rows, BLK)
    head = jnp.concatenate([w_qkv.reshape(rows, 3 * D), small], axis=1).astype(bf16)
    wide = [w_fc1.reshape(rows, 4, D), w_proj.reshape(rows, 1, D)]
    wide = jnp.concatenate([jnp.swapaxes(t.astype(bf16), 0, 1) for t in wide], axis=0)
    tall = w_fc2.reshape(4 * rows, D).astype(bf16)

    order = own_order(rows)
    owners = order[::rows] // rows
    turn = (order[:, None] == jnp.arange(D, dtype=jnp.int32)[None, :]).astype(bf16)
    head = line(head)
    small = gather_plane(jnp.stack([t[:, 3 * D :] for t in head]))
    head = jnp.stack([t[:, : 3 * D] for t in head])
    head_parts = gather_plane(head)
    (wide,) = gate([wide], small[1:2])
    wide = spread(wide, "a")
    small = jnp.concatenate(small, axis=0).reshape(-1, BLK)
    small = jnp.concatenate([small, swap_cores(small)], axis=0)
    small = dot_tn(turn, small).reshape(devices, slots)
    nvec = vectors.shape[0]
    vec = jnp.pad(small[:, :nvec].reshape(10, D), ((0, 6), (0, 0)))
    b1 = small[:, nvec : nvec + b_fc1.shape[0]].reshape(1, FF)
    (wide,) = gate([wide], head_parts[1:])
    wide_parts = gather_plane(wide)
    swapped = [swap_cores(p) for p in head_parts]
    head_parts = head_parts + swapped
    (tall,) = gate([tall], swapped + [wide, vec])
    tall = spread(tall, "a")
    if not direct:
        head_parts = [by_owner(head_parts, owners).reshape(-1, D // 32, 3 * D)]
    (q, k, v, h1t, wqkv, o, lse), _ = attend_call(img_lens, valid_rows, me, head_parts, inputs, turn, vec)
    *wide_parts, tall = gate(wide_parts + [tall], [o])
    tall_parts = gather_plane(tall)
    wide_parts = wide_parts + [swap_cores(p) for p in wide_parts]
    if not direct:
        wide_parts = [jnp.swapaxes(by_owner(wide_parts, owners, True), 0, 1).reshape(5, 32, D // 32, D)]
    x1, a, h2t, ot, dz, wp, w1, m, gp, *dw2 = up_call(me, o, inputs, cotangent, turn, vec, b1, wide_parts)
    if direct:
        keep2, away2 = [g.reshape(FF // 2, D) for g in dw2]
    else:
        dw2 = jnp.take(dw2[0].reshape(devices, 4 * rows, D), owners, axis=0).reshape(FF, D)
        keep2, away2 = dw2[: FF // 2], dw2[FF // 2 :]
    tall_parts = tall_parts + [swap_cores(p) for p in tall_parts]
    if not direct:
        tall_parts = [by_owner(tall_parts, owners, True).reshape(STEPS, 8, D // 8, D)]

    bf = ("b", "f")
    core2 = swap_cores(gate([away2], tall_parts[1 : len(tall_parts) // 2])[0])
    up2, up2_got = exchange(plain([keep2, core2]), bf)
    result, dx1, do, keep, away, db1, sums2, keep2 = down_call(
        me, m, gp, dz, h2t, w1, tall_parts, x1, cotangent, a, ot, wp, vec, passed=keep2, tokens=[core2]
    )
    core = swap_cores(gate([away], up2_got)[0])
    up2, up2_last = exchange(hold(up2, keep2) + plain(up2_got), "a")
    mid, mid_got = exchange(plain([keep, core]), bf)

    (dq, dk, dv, keep1, away1, sums_a), (keep, keep2) = back_call(
        img_lens, valid_rows, q, k, v, do, o, lse, h1t, passed=[keep, keep2], tokens=[core]
    )
    core1 = swap_cores(gate([away1], mid_got + up2_last)[0])
    mid, mid_last = exchange(hold(mid, keep) + plain(mid_got), "a")
    second, second_got = exchange(plain([keep1, core1]), bf)

    (d_input, sums0), (keep, keep1, keep2) = input_call(
        dq, dk, dv, wqkv, inputs, dx1, vec, passed=[keep, keep1, keep2], tokens=[core1]
    )
    second, second_sends = blocks(hold(second, keep1) + plain(second_got), "a")
    sums0, sums_a, sums2, db1, keep, keep2 = gate([sums0, sums_a, sums2, db1, keep, keep2], second_sends + mid_last)
    second_last = [from_peer(t, "a", k + 1) for k, t in enumerate(second_sends)]
    g_fc2 = add(hold(up2, keep2) + plain(up2_last))
    gvec = jnp.concatenate([sums0[:2], sums_a[:2], sums2[:6]], axis=0).reshape(devices, nvec)
    gsmall = jnp.concatenate([gvec, db1.reshape(devices, b_fc1.shape[0])], axis=1)
    gsmall = jnp.pad(gsmall, ((0, 0), (0, -gsmall.shape[1] % BLK))).astype(bf16)
    gsmall = lax.all_to_all(gsmall.reshape(devices, 1, -1), ALL, 0, 0)
    gsmall = jnp.sum(gsmall.astype(f32), axis=0).reshape(-1)

    g_mid = add(hold(mid, keep) + plain(mid_last))
    g_fc1, g_proj = g_mid[:, :FF], g_mid[:, FF:]
    g_qkv = add(second + plain(second_last))
    return (
        result,
        d_input,
        g_qkv.reshape(-1),
        g_proj.reshape(-1),
        g_fc1.reshape(-1),
        gsmall[nvec : nvec + b_fc1.shape[0]],
        g_fc2.reshape(-1),
        gsmall[:nvec],
    )


def solution(mesh):
    dp, fsdp = mesh.shape["dp"], mesh.shape["fsdp"]
    fine = Mesh(mesh.devices.reshape(dp // 2, 2, fsdp // 2, 2), ALL)
    rows, flat = P(ALL, None), P(ALL)
    return jax.shard_map(
        shards,
        mesh=fine,
        in_specs=(rows, rows, flat, flat, flat, flat, flat, flat, flat, rows),
        out_specs=(rows, rows, flat, flat, flat, flat, flat, flat),
        check_vma=False,
    )
```

```python
import functools

import jax
import jax.numpy as jnp
from jax import lax
from jax.experimental import pallas as pl
from jax.experimental.pallas import tpu as pltpu
from jax.sharding import Mesh
from jax.sharding import PartitionSpec as P

HEADS = 12
HD = 64
ROWS = 1024
D = HEADS * HD
FF = 4 * D
PAIRS = HEADS // 2
BLK = 128
QB = 2 * BLK
WIN = QB + 2 * BLK
TILE = 256
EPS = 1e-06
ALL = ("a", "b", "f", "c")
bf16 = jnp.bfloat16
f32 = jnp.float32
VMEM_LIMIT = 60 * 1024 * 1024
ANY = pl.BlockSpec(memory_space=pl.ANY)


def cost(us):
    return pl.CostEstimate(flops=us * 1_100_000_000, bytes_accessed=us * 3_000_000, transcendentals=0)


def dot_nn(left, right):
    return lax.dot_general(left, right, (((1,), (0,)), ((), ())), preferred_element_type=f32)


def dot_nt(left, right):
    return lax.dot_general(left, right, (((1,), (1,)), ((), ())), preferred_element_type=f32)


def dot_tn(left, right):
    return lax.dot_general(left, right, (((0,), (0,)), ((), ())), preferred_element_type=f32)


def norm_parts(values):
    center = values - jnp.mean(values, axis=-1, keepdims=True)
    scale = lax.rsqrt(jnp.mean(center * center, axis=-1, keepdims=True) + EPS)
    return center * scale, scale


def norm_back(grad, normed, scale, gain):
    inner = grad * gain
    first = jnp.mean(inner, axis=-1, keepdims=True)
    second = jnp.mean(inner * normed, axis=-1, keepdims=True)
    return scale * (inner - first - normed * second)


def col_sum(values):
    return jnp.sum(values, axis=0, keepdims=True)


def gelu_parts(u):
    half = 0.5 + 0.5 * lax.erf(u * 0.7071067811865476)
    e = jnp.exp2((u * u) * -0.7213475204444817)
    return u * half, half + (0.3989422804014327 * u) * e


def params(**kw):
    return pltpu.CompilerParams(vmem_limit_bytes=VMEM_LIMIT, **kw)


def whole(shape):
    return pl.BlockSpec(shape, lambda *_: (0,) * len(shape))


def gather_copies(parts, line_me, me_ref, source, target, sems):
    if len(parts) == 1:
        return [pltpu.make_async_copy(source(parts[0], None), target(None), sems.at[0])]
    half, copies = len(parts) // 2, []
    for n, part in enumerate(parts):
        for k in range(part.shape[0]):
            device = ((k ^ line_me) * half + (n % half ^ me_ref[1])) * 2 + (n // half ^ me_ref[2])
            copies.append(pltpu.make_async_copy(source(part, k), target(device), sems.at[n * part.shape[0] + k]))
    return copies


def copy_count(parts):
    return 1 if len(parts) == 1 else len(parts) * parts[0].shape[0]


def fill_segments(lens_ref, valid_ref, segc, segr):
    row_c = lax.broadcasted_iota(jnp.int32, (ROWS, BLK), 0)
    row_r = lax.broadcasted_iota(jnp.int32, (8, ROWS), 1)
    sum_c = jnp.zeros((ROWS, BLK), jnp.int32)
    sum_r = jnp.zeros((8, ROWS), jnp.int32)
    end = jnp.int32(0)
    for j in range(lens_ref.shape[1]):
        end = end + lens_ref[0, j]
        sum_c = sum_c + (row_c >= end).astype(jnp.int32)
        sum_r = sum_r + (row_r >= end).astype(jnp.int32)
    valid = valid_ref[0]
    segc[...] = jnp.where(row_c < valid, sum_c, -1)
    segr[...] = jnp.where(row_r < valid, sum_r, -1)


def block_place(segc, segr, i):
    start = pl.multiple_of(jnp.clip(i * (QB // BLK) - 1, 0, (ROWS - WIN) // BLK) * BLK, BLK)
    here = pl.ds(pl.multiple_of(i * QB, BLK), QB)
    window = pl.ds(start, WIN)
    rows = jnp.concatenate([segc[here, :]] * (WIN // BLK), axis=1)
    bias = jnp.where(rows == segr[0:1, window], 0.0, -1000000000.0).astype(f32)
    return here, window, jnp.concatenate([bias, bias], axis=0)


def lane_masks():
    low = (lax.broadcasted_iota(jnp.int32, (1, BLK), 1) < HD).astype(f32)
    return low.astype(bf16), (1.0 - low).astype(bf16)


def stack_pair(block, masks):
    return jnp.concatenate([block * masks[0], block * masks[1]], axis=0)


def pick_pair(values):
    low = lax.broadcasted_iota(jnp.int32, (1, BLK), 1) < HD
    return jnp.where(low, values[:QB], values[QB:])


def attend_kernel(count, passed, lens_ref, valid_ref, me_ref, *refs):
    parts, (x_ref, turn_ref, vec_ref) = refs[:count], refs[count : count + 3]
    q_ref, k_ref, v_ref, ht_ref, w_out, o_ref, lse_ref = refs[-16 - passed :][:7]
    stage, w_ref, qs, ks, vs, segc, segr, sems, out_sem = refs[-9:]
    i = pl.program_id(0)
    tiles = ROWS // TILE

    def fetch():
        def source(part, k):
            return part if k is None else part.at[k]

        return gather_copies(parts, me_ref[0], me_ref, source, lambda n: stage if n is None else stage.at[n], sems)

    def store():
        return pltpu.make_async_copy(w_ref, w_out, out_sem)

    @pl.when(i == 0)
    def _():
        for copy in fetch():
            copy.start()
        fill_segments(lens_ref, valid_ref, segc, segr)
        for copy in fetch():
            copy.wait()
        w_ref[...] = stage[...].astype(f32).reshape(D, 3 * D).astype(bf16)
        store().start()

    @pl.when(i < tiles)
    def _():
        rows = pl.ds(pl.multiple_of(i * TILE, TILE), TILE)
        normed, _ = norm_parts(x_ref[...])
        low = (normed * vec_ref[0:1] + vec_ref[1:2]).astype(bf16)
        q = ((dot_nn(low, w_ref[:, :D]) + vec_ref[2:3]).astype(bf16).astype(f32) * 0.125).astype(bf16)
        k = dot_nn(low, w_ref[:, D : 2 * D]).astype(bf16)
        v = (dot_nn(low, w_ref[:, 2 * D :]) + vec_ref[3:4]).astype(bf16)
        for value, ref, scratch in ((q, q_ref, qs), (k, k_ref, ks), (v, v_ref, vs)):
            ref[...] = value
            scratch[rows] = value
        ht_ref[...] = dot_nt(turn_ref[...], low).astype(bf16)

    @pl.when(i >= tiles)
    def _():
        here, window, bias = block_place(segc, segr, i - tiles)
        masks = lane_masks()
        for p in range(PAIRS):
            s = slice(p * BLK, (p + 1) * BLK)
            scores = dot_nt(stack_pair(qs[here, s], masks), ks[window, s]) + bias
            peak = jnp.max(scores, axis=1, keepdims=True)
            expo = jnp.exp(scores - peak)
            total = jnp.sum(expo, axis=1, keepdims=True)
            o_ref[:, s] = pick_pair(dot_nn(expo.astype(bf16), vs[window, s]) * (1.0 / total)).astype(bf16)
            lse_ref[0, :, p : p + 1] = peak + jnp.log(total)

    @pl.when(i == tiles + ROWS // QB - 1)
    def _():
        store().wait()


def attend_call(lens, valid, me, parts, x, turn, vec, passed=(), tokens=()):
    tiles = ROWS // TILE

    def first(i):
        return jnp.minimum(i, tiles - 1)

    def second(i):
        return jnp.maximum(i - tiles, 0)

    tok = pl.BlockSpec((TILE, D), lambda i: (first(i), 0))
    smem = pl.BlockSpec(memory_space=pltpu.SMEM)
    count, rows = len(parts), parts[0].shape[1]
    extra = list(passed) + list(tokens)
    out = pl.pallas_call(
        functools.partial(attend_kernel, count, len(passed)),
        grid=(tiles + ROWS // QB,),
        in_specs=[smem] * 3 + [ANY] * count + [tok, whole((D, D)), whole((16, D))] + [ANY] * len(extra),
        out_specs=[
            tok,
            tok,
            tok,
            pl.BlockSpec((D, TILE), lambda i: (0, first(i))),
            ANY,
            pl.BlockSpec((QB, D), lambda i: (second(i), 0)),
            pl.BlockSpec((1, 2 * QB, BLK), lambda i: (second(i), 0, 0)),
        ]
        + [ANY] * len(passed),
        out_shape=[jax.ShapeDtypeStruct((ROWS, D), bf16)] * 3
        + [
            jax.ShapeDtypeStruct((D, ROWS), bf16),
            jax.ShapeDtypeStruct((D, 3 * D), bf16),
            jax.ShapeDtypeStruct((ROWS, D), bf16),
            jax.ShapeDtypeStruct((ROWS // QB, 2 * QB, BLK), f32),
        ]
        + [jax.ShapeDtypeStruct(p.shape, p.dtype) for p in passed],
        scratch_shapes=[
            pltpu.VMEM((D // rows, rows, 3 * D), bf16),
            pltpu.VMEM((D, 3 * D), bf16),
            pltpu.VMEM((ROWS, D), bf16),
            pltpu.VMEM((ROWS, D), bf16),
            pltpu.VMEM((ROWS, D), bf16),
            pltpu.VMEM((ROWS, BLK), jnp.int32),
            pltpu.VMEM((8, ROWS), jnp.int32),
            pltpu.SemaphoreType.DMA((copy_count(parts),)),
            pltpu.SemaphoreType.DMA,
        ],
        input_output_aliases={6 + count + n: 7 + n for n in range(len(passed))},
        compiler_params=params(),
        cost_estimate=cost(25),
        name="attend",
    )(lens, valid, me, *parts, x, turn, vec, *extra)
    return out[:7], out[7:]


STEPS = FF // D


def up_kernel(count, me_ref, o_ref, x_ref, ct_ref, turn_ref, vec_ref, b_ref, *refs):
    parts = refs[:count]
    h, dzs, stage, wp, dw_ref, p_sems, w_sems, out_sem = refs[-8:]
    grads = 2 if count > 1 else 1
    outs = refs[-17 - grads : -8]
    x1_ref, a_ref, ht_ref, ot_ref, dz_ref, wp_out, w_ref, m_ref, gp_ref, *grad_refs = outs
    i = pl.program_id(0)
    tiles = ROWS // TILE

    def fetch(first):
        block = pl.ds(4, 1) if first else pl.ds(0, 4)

        def source(part, k):
            return part.at[block] if k is None else part.at[k, block]

        def target(n):
            return stage.at[block] if n is None else stage.at[block, n]

        return gather_copies(parts, 0, me_ref, source, target, p_sems if first else w_sems)

    def store():
        return pltpu.make_async_copy(wp, wp_out, out_sem)

    @pl.when(i == 0)
    def _():
        for copy in fetch(True):
            copy.start()
        for copy in fetch(False):
            copy.start()
        for copy in fetch(True):
            copy.wait()
        wp[...] = stage[4].astype(f32).reshape(D, D).astype(bf16)
        store().start()

    @pl.when(i < tiles)
    def _():
        rows = pl.ds(pl.multiple_of(i * TILE, TILE), TILE)
        branch = dot_nn(o_ref[...], wp[...]) + vec_ref[4:5]
        inner = x_ref[...] + vec_ref[5:6] * branch
        x1_ref[...] = inner
        a_ref[...] = branch.astype(bf16)
        normed, _ = norm_parts(inner)
        low = (normed * vec_ref[6:7] + vec_ref[7:8]).astype(bf16)
        h[rows] = low
        dz = (vec_ref[9:10] * ct_ref[...]).astype(bf16)
        dz_ref[...] = dz
        dzs[rows] = dz
        ht_ref[...] = dot_nt(turn_ref[...], low).astype(bf16)
        ot_ref[...] = dot_nt(turn_ref[...], o_ref[...]).astype(bf16)

    @pl.when(i == tiles)
    def _():
        for copy in fetch(False):
            copy.wait()
        store().wait()

    @pl.when(i >= tiles)
    def _():
        chunk = (i - tiles) ^ (me_ref[0] if count > 1 else 0)
        w_ref[0] = stage[chunk].astype(f32).reshape(D, D).astype(bf16)
        for n in range(D // TILE):
            c = slice(n * TILE, (n + 1) * TILE)
            for t in range(tiles):
                r = slice(t * TILE, (t + 1) * TILE)
                m, gp = gelu_parts(dot_nn(h[r], w_ref[0, :, c]) + b_ref[:, c])
                m_ref[r, c] = m.astype(bf16)
                gp_ref[r, c] = gp.astype(bf16)
        for n in range(D // TILE):
            c = slice(n * TILE, (n + 1) * TILE)
            dw_ref[c] = dot_tn(m_ref[:, c], dzs[...])
        if grads == 1:
            grad_refs[0][...] = dw_ref[...].astype(bf16)
        else:
            blocks, _, size, _ = grad_refs[0].shape
            for k in range(blocks):
                for c, ref in enumerate(grad_refs):
                    row = ((k ^ me_ref[1]) * 2 + (c ^ me_ref[2])) * size
                    ref[k, 0] = dw_ref[pl.ds(pl.multiple_of(row, 8), size), :].astype(bf16)


def up_call(me, o, x, ct, turn, vec, b, parts, tokens=()):
    count = len(parts)
    tiles = ROWS // TILE
    _, n, r, _ = (1,) + parts[0].shape[1:] if count == 1 else (1, D // parts[0].shape[2], parts[0].shape[2], D)

    def first(i):
        return jnp.minimum(i, tiles - 1)

    def chunk(i, me):
        return jnp.maximum(i - tiles, 0) ^ (me[0] if count > 1 else 0)

    tok = pl.BlockSpec((TILE, D), lambda i, me: (first(i), 0))
    feat = pl.BlockSpec((D, TILE), lambda i, me: (0, first(i)))
    part = pl.BlockSpec((ROWS, D), lambda i, me: (0, chunk(i, me)))
    if count > 1:
        blocks = count // 2
        spec = pl.BlockSpec((blocks, 1, 4 * r, D), lambda i, me: (0, jnp.maximum(i - tiles, 0), 0, 0))
        grad_specs, grad_shapes = [spec] * 2, [jax.ShapeDtypeStruct((blocks, STEPS, 4 * r, D), bf16)] * 2
    else:
        grad_specs = [pl.BlockSpec((D, D), lambda i, me: (chunk(i, me), 0))]
        grad_shapes = [jax.ShapeDtypeStruct((FF, D), bf16)]
    return pl.pallas_call(
        functools.partial(up_kernel, count),
        grid_spec=pltpu.PrefetchScalarGridSpec(
            num_scalar_prefetch=1,
            grid=(tiles + STEPS,),
            in_specs=[tok, tok, tok, whole((D, D)), whole((16, D)), pl.BlockSpec((1, D), lambda i, me: (0, chunk(i, me)))]
            + [ANY] * (count + len(tokens)),
            out_specs=[
                tok,
                tok,
                feat,
                feat,
                tok,
                ANY,
                pl.BlockSpec((1, D, D), lambda i, me: (chunk(i, me), 0, 0)),
                part,
                part,
            ]
            + grad_specs,
            scratch_shapes=[
                pltpu.VMEM((ROWS, D), bf16),
                pltpu.VMEM((ROWS, D), bf16),
                pltpu.VMEM((5, n, r, D), bf16),
                pltpu.VMEM((D, D), bf16),
                pltpu.VMEM((D, D), f32),
                pltpu.SemaphoreType.DMA((copy_count(parts),)),
                pltpu.SemaphoreType.DMA((copy_count(parts),)),
                pltpu.SemaphoreType.DMA,
            ],
        ),
        out_shape=[
            jax.ShapeDtypeStruct((ROWS, D), f32),
            jax.ShapeDtypeStruct((ROWS, D), bf16),
            jax.ShapeDtypeStruct((D, ROWS), bf16),
            jax.ShapeDtypeStruct((D, ROWS), bf16),
            jax.ShapeDtypeStruct((ROWS, D), bf16),
            jax.ShapeDtypeStruct((D, D), bf16),
            jax.ShapeDtypeStruct((STEPS, D, D), bf16),
            jax.ShapeDtypeStruct((ROWS, FF), bf16),
            jax.ShapeDtypeStruct((ROWS, FF), bf16),
        ]
        + grad_shapes,
        compiler_params=params(),
        cost_estimate=cost(26),
        name="mlp_up",
    )(me, o, x, ct, turn, vec, b, *parts, *tokens)


def down_kernel(
    count, me_ref, m_ref, gp_ref, dz_ref, ht_ref, w1_ref, x1_ref, ct_ref, a_ref, ot_ref, wp_ref, dzt_ref, vec_ref, *refs
):
    parts = refs[:count]
    out_ref, dx_ref, do_ref, keep_ref, away_ref, db1_ref, sums_ref, _, z_acc, dh_acc, dwp_acc, w2_ref, sems = refs[-13:]
    j = pl.program_id(0)

    def fetch(step):
        if count == 1:
            return [pltpu.make_async_copy(parts[0].at[step], w2_ref.at[step], sems.at[step, 0])]
        half, copies = count // 2, []
        for n, part in enumerate(parts):
            place = (n % half ^ me_ref[1]) * 2 + (n // half ^ me_ref[2])
            copies.append(pltpu.make_async_copy(part.at[step], w2_ref.at[step, place], sems.at[step, n]))
        return copies

    @pl.when(j == 0)
    def _():
        for step in range(STEPS):
            for copy in fetch(step):
                copy.start()
        z_acc[...] = jnp.zeros_like(z_acc)
        dh_acc[...] = jnp.zeros_like(dh_acc)
        dwp_acc[...] = jnp.zeros_like(dwp_acc)
        sums_ref[...] = jnp.zeros_like(sums_ref)

    @pl.when(j < STEPS)
    def _():
        for copy in fetch(j):
            copy.wait()
        w1 = w1_ref[0]
        w2 = w2_ref[j].reshape(D, D)
        du = (dot_nt(dz_ref[...], w2) * gp_ref[...].astype(f32)).astype(bf16)
        db1_ref[...] = col_sum(du.astype(f32))
        keep_ref[...] = dot_nn(ht_ref[: D // 2], du).astype(bf16)
        away_ref[...] = dot_nn(ht_ref[D // 2 :], du).astype(bf16)
        z_acc[...] += dot_nn(m_ref[...], w2)
        dh_acc[...] += dot_nt(du, w1)

    @pl.when(j >= STEPS)
    def _():
        r = pl.ds(pl.multiple_of((j - STEPS) * TILE, TILE), TILE)
        inner, ct, branch = x1_ref[...], ct_ref[...], z_acc[r] + vec_ref[8:9]
        out_ref[...] = inner + vec_ref[9:10] * branch
        normed, scale = norm_parts(inner)
        dh = dh_acc[r]
        dx = ct + norm_back(dh, normed, scale, vec_ref[6:7])
        dx_ref[...] = dx
        da = (vec_ref[5:6] * dx).astype(bf16)
        do_ref[...] = dot_nt(da, wp_ref[...]).astype(bf16)
        dwp_acc[...] += dot_nn(ot_ref[...], da)
        adds = (da.astype(f32), dx * a_ref[...].astype(f32), dh * normed, dh, dzt_ref[...].astype(f32), ct * branch)
        sums_ref[...] += jnp.concatenate([col_sum(v) for v in adds] + [jnp.zeros((2, D), f32)], axis=0)

    @pl.when(j == STEPS + ROWS // TILE - 1)
    def _():
        keep_ref[...] = dwp_acc[: D // 2].astype(bf16)
        away_ref[...] = dwp_acc[D // 2 :].astype(bf16)


def down_call(me, m, gp, dz, ht, w1, parts, x1, ct, a, ot, wp, vec, passed, tokens):
    count = len(parts)
    size = parts[0].shape[-2]

    def last(j):
        return jnp.minimum(j, STEPS - 1)

    def row(j):
        return jnp.maximum(j - STEPS, 0)

    part = pl.BlockSpec((ROWS, D), lambda j: (0, last(j)))
    grad = pl.BlockSpec((D // 2, D), lambda j: (0, jnp.minimum(j, STEPS)))
    tile = pl.BlockSpec((TILE, D), lambda j: (row(j), 0))
    return pl.pallas_call(
        functools.partial(down_kernel, count),
        grid=(STEPS + ROWS // TILE,),
        in_specs=[
            pl.BlockSpec(memory_space=pltpu.SMEM),
            part,
            part,
            whole((ROWS, D)),
            whole((D, ROWS)),
            pl.BlockSpec((1, D, D), lambda j: (last(j), 0, 0)),
            tile,
            tile,
            tile,
            pl.BlockSpec((D, TILE), lambda j: (0, row(j))),
            whole((D, D)),
            tile,
            whole((16, D)),
        ]
        + [ANY] * (count + 1 + len(tokens)),
        out_specs=[
            tile,
            tile,
            tile,
            grad,
            grad,
            pl.BlockSpec((1, D), lambda j: (0, last(j))),
            whole((8, D)),
            ANY,
        ],
        out_shape=[
            jax.ShapeDtypeStruct((ROWS, D), f32),
            jax.ShapeDtypeStruct((ROWS, D), f32),
            jax.ShapeDtypeStruct((ROWS, D), bf16),
            jax.ShapeDtypeStruct((D // 2, FF + D), bf16),
            jax.ShapeDtypeStruct((D // 2, FF + D), bf16),
            jax.ShapeDtypeStruct((1, FF), f32),
            jax.ShapeDtypeStruct((8, D), f32),
            jax.ShapeDtypeStruct(passed.shape, passed.dtype),
        ],
        scratch_shapes=[
            pltpu.VMEM((ROWS, D), f32),
            pltpu.VMEM((ROWS, D), f32),
            pltpu.VMEM((D, D), f32),
            pltpu.VMEM((STEPS, D // size, size, D), bf16),
            pltpu.SemaphoreType.DMA((STEPS, count)),
        ],
        input_output_aliases={13 + count: 7},
        compiler_params=params(),
        cost_estimate=cost(35),
        name="mlp_down",
    )(me, m, gp, dz, ht, w1, x1, ct, a, ot, wp, dz, vec, *parts, passed, *tokens)


def back_kernel(passed, lens_ref, valid_ref, q_ref, k_ref, v_ref, do_ref, o_ref, lse_ref, ht_hbm, *refs):
    dq_out, dk_out, dv_out, keep_ref, away_ref, sums_ref = refs[-16 - passed :][:6]
    segc, segr, dk_acc, dv_acc, dq_ref, dk_ref, dv_ref, ht_ref, sems, ht_sem = refs[-10:]
    i = pl.program_id(0)
    steps = ROWS // QB

    def fetch():
        return pltpu.make_async_copy(ht_hbm, ht_ref, ht_sem)

    def store(n):
        return pltpu.make_async_copy((dq_ref, dk_ref, dv_ref)[n], (dq_out, dk_out, dv_out)[n], sems.at[n])

    @pl.when(i == 0)
    def _():
        fetch().start()
        fill_segments(lens_ref, valid_ref, segc, segr)
        dk_acc[...] = jnp.zeros_like(dk_acc)
        dv_acc[...] = jnp.zeros_like(dv_acc)

    @pl.when(i < steps)
    def _():
        here, window, bias = block_place(segc, segr, i)
        masks = lane_masks()
        for p in range(PAIRS):
            s = slice(p * BLK, (p + 1) * BLK)
            queries = stack_pair(q_ref[:, s], masks)
            grads = stack_pair(do_ref[:, s], masks)
            o = o_ref[:, s].astype(f32)
            center = jnp.sum(grads.astype(f32) * jnp.concatenate([o, o], axis=0), axis=1, keepdims=True)
            probs = jnp.exp(dot_nt(queries, k_ref[window, s]) + bias - lse_ref[0, :, p : p + 1])
            dscores = (probs * (dot_nt(grads, v_ref[window, s]) - center)).astype(bf16)
            dv_acc[window, s] += dot_tn(probs.astype(bf16), grads)
            dk_acc[window, s] += dot_tn(dscores, queries)
            dq_ref[here, s] = (pick_pair(dot_nn(dscores, k_ref[window, s])) * 0.125).astype(bf16)

    def weights(ref):
        away_ref[...] = dot_nn(ht_ref[D // 2 :], ref[...]).astype(bf16)
        keep_ref[...] = dot_nn(ht_ref[: D // 2], ref[...]).astype(bf16)

    @pl.when(i == steps)
    def _():
        dk_ref[...] = dk_acc[...].astype(bf16)
        dv_ref[...] = dv_acc[...].astype(bf16)
        for n in range(3):
            store(n).start()
        fetch().wait()
        weights(dq_ref)
        dbq = col_sum(dq_ref[...].astype(f32))
        dbv = col_sum(dv_ref[...].astype(f32))
        sums_ref[...] = jnp.concatenate([dbq, dbv, jnp.zeros((6, D), f32)], axis=0)

    @pl.when(i == steps + 1)
    def _():
        weights(dk_ref)

    @pl.when(i == steps + 2)
    def _():
        weights(dv_ref)
        for n in range(3):
            store(n).wait()


def back_call(lens, valid, q, k, v, do, o, lse, ht, passed=(), tokens=()):
    steps = ROWS // QB

    def last(i):
        return jnp.minimum(i, steps - 1)

    tok = pl.BlockSpec((QB, D), lambda i: (last(i), 0))
    full = whole((ROWS, D))
    grad = pl.BlockSpec((D // 2, D), lambda i: (0, jnp.maximum(i - steps, 0)))
    extra = list(passed) + list(tokens)
    out = pl.pallas_call(
        functools.partial(back_kernel, len(passed)),
        grid=(steps + 3,),
        in_specs=[
            pl.BlockSpec(memory_space=pltpu.SMEM),
            pl.BlockSpec(memory_space=pltpu.SMEM),
            tok,
            full,
            full,
            tok,
            tok,
            pl.BlockSpec((1, 2 * QB, BLK), lambda i: (last(i), 0, 0)),
            ANY,
        ]
        + [ANY] * len(extra),
        out_specs=[ANY] * 3 + [grad, grad, whole((8, D))] + [ANY] * len(passed),
        out_shape=[jax.ShapeDtypeStruct((ROWS, D), bf16)] * 3
        + [jax.ShapeDtypeStruct((D // 2, 3 * D), bf16)] * 2
        + [jax.ShapeDtypeStruct((8, D), f32)]
        + [jax.ShapeDtypeStruct(p.shape, p.dtype) for p in passed],
        scratch_shapes=[
            pltpu.VMEM((ROWS, BLK), jnp.int32),
            pltpu.VMEM((8, ROWS), jnp.int32),
            pltpu.VMEM((ROWS, D), f32),
            pltpu.VMEM((ROWS, D), f32),
            pltpu.VMEM((ROWS, D), bf16),
            pltpu.VMEM((ROWS, D), bf16),
            pltpu.VMEM((ROWS, D), bf16),
            pltpu.VMEM((D, ROWS), bf16),
            pltpu.SemaphoreType.DMA((3,)),
            pltpu.SemaphoreType.DMA,
        ],
        input_output_aliases={9 + n: 6 + n for n in range(len(passed))},
        compiler_params=params(),
        cost_estimate=cost(33),
        name="attend_back",
    )(lens, valid, q, k, v, do, o, lse, ht, *extra)
    return out[:6], out[6:]


def input_kernel(passed, dq_ref, dk_ref, dv_ref, w_ref, x_ref, dx1_ref, vec_ref, *refs):
    dx_ref, sums_ref = refs[len(refs) - 2 - passed :][:2]
    i = pl.program_id(0)
    dh = dot_nt(dq_ref[...], w_ref[:, :D]) + dot_nt(dk_ref[...], w_ref[:, D : 2 * D]) + dot_nt(dv_ref[...], w_ref[:, 2 * D :])
    normed, scale = norm_parts(x_ref[...])
    dx_ref[...] = dx1_ref[...] + norm_back(dh, normed, scale, vec_ref[0:1])
    sums = jnp.concatenate([col_sum(dh * normed), col_sum(dh), jnp.zeros((6, D), f32)], axis=0)

    @pl.when(i == 0)
    def _():
        sums_ref[...] = sums

    @pl.when(i > 0)
    def _():
        sums_ref[...] += sums


def input_call(dq, dk, dv, w, x, dx1, vec, passed=(), tokens=()):
    tok = pl.BlockSpec((TILE, D), lambda i: (i, 0))
    extra = list(passed) + list(tokens)
    out = pl.pallas_call(
        functools.partial(input_kernel, len(passed)),
        grid=(ROWS // TILE,),
        in_specs=[tok, tok, tok, whole((D, 3 * D)), tok, tok, whole((16, D))] + [ANY] * len(extra),
        out_specs=[tok, whole((8, D))] + [ANY] * len(passed),
        out_shape=[jax.ShapeDtypeStruct((ROWS, D), f32), jax.ShapeDtypeStruct((8, D), f32)]
        + [jax.ShapeDtypeStruct(p.shape, p.dtype) for p in passed],
        input_output_aliases={7 + n: 2 + n for n in range(len(passed))},
        compiler_params=params(),
        cost_estimate=cost(13),
        name="input_back",
    )(dq, dk, dv, w, x, dx1, vec, *extra)
    return out[:2], out[2:]


def swap_cores(x):
    return lax.ppermute(x, "c", [(0, 1), (1, 0)])


def from_peer(x, axes, k):
    return lax.ppermute(x, axes, [(i, i ^ k) for i in range(lax.axis_size(axes))])


def gate_kernel(*refs):
    del refs


def gate(arrays, tokens):
    out = pl.pallas_call(
        gate_kernel,
        in_specs=[ANY] * (len(arrays) + len(tokens)),
        out_specs=[ANY] * len(arrays),
        out_shape=[jax.ShapeDtypeStruct(a.shape, a.dtype) for a in arrays],
        input_output_aliases={n: n for n in range(len(arrays))},
        name="gate",
    )(*arrays, *tokens)
    return list(out)


def own_order(rows):
    place = jnp.arange(D, dtype=jnp.int32)
    k, rest = place % rows, place // rows
    na, nb, nf = lax.axis_size("a"), lax.axis_size("b"), lax.axis_size("f")
    a, rest = rest % na ^ lax.axis_index("a"), rest // na
    f, rest = rest % nf ^ lax.axis_index("f"), rest // nf
    b, c = rest % nb ^ lax.axis_index("b"), rest // nb ^ lax.axis_index("c")
    return (((a * nb + b) * nf + f) * 2 + c) * rows + k


def line(shard):
    return [shard] + [from_peer(shard, "a", k) for k in range(1, lax.axis_size("a"))]


def spread(shard, axis):
    return lax.all_to_all(jnp.broadcast_to(shard[None], (lax.axis_size(axis),) + shard.shape), axis, 0, 0)


def gather_plane(stack):
    return [stack] + [from_peer(stack, ("b", "f"), k) for k in range(1, lax.axis_size(("b", "f")))]


def by_owner(parts, order, natural_line=False):
    if natural_line:
        index = jnp.arange(lax.axis_size("a")) ^ lax.axis_index("a")
        parts = [jnp.take(p, index, axis=0) for p in parts]
    return jnp.take(jnp.concatenate(parts, axis=0), jnp.argsort(order), axis=0)


def add(terms):
    total = 0.0
    for array, low, high in terms:
        total = total + array[low:high].astype(f32)
    return total


def plain(arrays):
    return [(g, 0, g.shape[0]) for g in arrays]


def blocks(terms, axes):
    count = lax.axis_size(axes)
    size = (terms[0][2] - terms[0][1]) // count

    def block(k):
        return [(t, low + k * size, low + (k + 1) * size) for t, low, _ in terms]

    return block(0), [add(block(k)).astype(bf16) for k in range(1, count)]


def exchange(terms, axes):
    mine, sends = blocks(terms, axes)
    return mine, [from_peer(t, axes, k + 1) for k, t in enumerate(sends)]


def hold(terms, array):
    return [(array,) + terms[0][1:]] + terms[1:]


def shards(inputs, img_lens, valid_rows, w_qkv, w_proj, w_fc1, b_fc1, w_fc2, vectors, cotangent):
    devices = lax.axis_size(ALL)
    rows = D // devices
    slots = rows * BLK
    na, nb, nf = lax.axis_size("a"), lax.axis_size("b"), lax.axis_size("f")
    direct = na == STEPS and rows % 8 == 0
    me = jnp.stack([lax.axis_index("a"), lax.axis_index(("b", "f")), lax.axis_index("c")]).astype(jnp.int32)
    small = jnp.concatenate([vectors, b_fc1])
    small = jnp.pad(small, (0, slots - small.shape[0])).reshape(rows, BLK)
    head = jnp.concatenate([w_qkv.reshape(rows, 3 * D), small], axis=1).astype(bf16)
    wide = [w_fc1.reshape(rows, 4, D), w_proj.reshape(rows, 1, D)]
    wide = jnp.concatenate([jnp.swapaxes(t.astype(bf16), 0, 1) for t in wide], axis=0)
    tall = w_fc2.reshape(4 * rows, D).astype(bf16)

    order = own_order(rows)
    owners = order[::rows] // rows
    turn = (order[:, None] == jnp.arange(D, dtype=jnp.int32)[None, :]).astype(bf16)
    head = line(head)
    small = gather_plane(jnp.stack([t[:, 3 * D :] for t in head]))
    head = jnp.stack([t[:, : 3 * D] for t in head])
    head_parts = gather_plane(head)
    (wide,) = gate([wide], small[1:2])
    wide = spread(wide, "a")
    small = jnp.concatenate(small, axis=0).reshape(-1, BLK)
    small = jnp.concatenate([small, swap_cores(small)], axis=0)
    small = dot_tn(turn, small).reshape(devices, slots)
    nvec = vectors.shape[0]
    vec = jnp.pad(small[:, :nvec].reshape(10, D), ((0, 6), (0, 0)))
    b1 = small[:, nvec : nvec + b_fc1.shape[0]].reshape(1, FF)
    head_parts = head_parts[:1] + gate(head_parts[1:], [vec, b1])
    (wide,) = gate([wide], head_parts[1:])
    wide_parts = gather_plane(wide)
    swapped = [swap_cores(p) for p in head_parts]
    head_parts = head_parts + swapped
    (tall,) = gate([tall], swapped + [wide, vec])
    tall = spread(tall, "a")
    if not direct:
        head_parts = [by_owner(head_parts, owners).reshape(-1, D // 32, 3 * D)]
    (q, k, v, h1t, wqkv, o, lse), _ = attend_call(img_lens, valid_rows, me, head_parts, inputs, turn, vec)
    *wide_parts, tall = gate(wide_parts + [tall], [o])
    tall_parts = gather_plane(tall)
    wide_parts = wide_parts + [swap_cores(p) for p in wide_parts]
    if not direct:
        wide_parts = [jnp.swapaxes(by_owner(wide_parts, owners, True), 0, 1).reshape(5, 32, D // 32, D)]
    x1, a, h2t, ot, dz, wp, w1, m, gp, *dw2 = up_call(me, o, inputs, cotangent, turn, vec, b1, wide_parts)
    if direct:
        keep2, away2 = [g.reshape(FF // 2, D) for g in dw2]
    else:
        dw2 = jnp.take(dw2[0].reshape(devices, 4 * rows, D), owners, axis=0).reshape(FF, D)
        keep2, away2 = dw2[: FF // 2], dw2[FF // 2 :]
    tall_parts = tall_parts + [swap_cores(p) for p in tall_parts]
    if not direct:
        tall_parts = [by_owner(tall_parts, owners, True).reshape(STEPS, 8, D // 8, D)]

    bf = ("b", "f")
    core2 = swap_cores(gate([away2], tall_parts[1 : len(tall_parts) // 2])[0])
    up2, up2_got = exchange(plain([keep2, core2]), bf)
    result, dx1, do, keep, away, db1, sums2, keep2 = down_call(
        me, m, gp, dz, h2t, w1, tall_parts, x1, cotangent, a, ot, wp, vec, passed=keep2, tokens=[core2]
    )
    core = swap_cores(gate([away], up2_got)[0])
    up2, up2_last = exchange(hold(up2, keep2) + plain(up2_got), "a")
    mid, mid_got = exchange(plain([keep, core]), bf)

    (dq, dk, dv, keep1, away1, sums_a), (keep, keep2) = back_call(
        img_lens, valid_rows, q, k, v, do, o, lse, h1t, passed=[keep, keep2], tokens=[core]
    )
    core1 = swap_cores(gate([away1], mid_got + up2_last)[0])
    mid, mid_last = exchange(hold(mid, keep) + plain(mid_got), "a")
    second, second_got = exchange(plain([keep1, core1]), bf)

    (d_input, sums0), (keep, keep1, keep2) = input_call(
        dq, dk, dv, wqkv, inputs, dx1, vec, passed=[keep, keep1, keep2], tokens=[core1]
    )
    second, second_sends = blocks(hold(second, keep1) + plain(second_got), "a")
    sums0, sums_a, sums2, db1, keep, keep2 = gate([sums0, sums_a, sums2, db1, keep, keep2], second_sends + mid_last)
    second_last = [from_peer(t, "a", k + 1) for k, t in enumerate(second_sends)]
    g_fc2 = add(hold(up2, keep2) + plain(up2_last))
    gvec = jnp.concatenate([sums0[:2], sums_a[:2], sums2[:6]], axis=0).reshape(devices, nvec)
    gsmall = jnp.concatenate([gvec, db1.reshape(devices, b_fc1.shape[0])], axis=1)
    gsmall = jnp.pad(gsmall, ((0, 0), (0, -gsmall.shape[1] % BLK))).astype(bf16)
    gsmall = lax.all_to_all(gsmall.reshape(devices, 1, -1), ALL, 0, 0)
    gsmall = jnp.sum(gsmall.astype(f32), axis=0).reshape(-1)

    g_mid = add(hold(mid, keep) + plain(mid_last))
    g_fc1, g_proj = g_mid[:, :FF], g_mid[:, FF:]
    g_qkv = add(second + plain(second_last))
    return (
        result,
        d_input,
        g_qkv.reshape(-1),
        g_proj.reshape(-1),
        g_fc1.reshape(-1),
        gsmall[nvec : nvec + b_fc1.shape[0]],
        g_fc2.reshape(-1),
        gsmall[:nvec],
    )


def solution(mesh):
    dp, fsdp = mesh.shape["dp"], mesh.shape["fsdp"]
    fine = Mesh(mesh.devices.reshape(dp // 2, 2, fsdp // 2, 2), ALL)
    rows, flat = P(ALL, None), P(ALL)
    return jax.shard_map(
        shards,
        mesh=fine,
        in_specs=(rows, rows, flat, flat, flat, flat, flat, flat, flat, rows),
        out_specs=(rows, rows, flat, flat, flat, flat, flat, flat),
        check_vma=False,
    )
```
